32 devices in a mesh: dp: 4 (over z), cout: 4 (over y, x), cin: 2 (over core).
Axes of the slice: x: 2, y: 2, z: 4, core: 2. Of those that a mesh axis runs over, the one named last changes fastest.
Arguments:
- images: bfloat16 [16, 512, 512], P(None, ('dp', 'cin')), may hold values from -6 to 6
- masks: int32 [16, 512], P(None, ('dp', 'cin')), may hold values from 0 to 1, as said below
- labels: int32 [512], P(('dp', 'cin')), may hold values from 0 to 9
- w_first: float32 [9, 512, 512], P(None, None, 'cout'), may hold values from -0.09375 to 0.09375
- w_second: float32 [9, 512, 512], P(None, 'cout'), may hold values from -0.09375 to 0.09375
- norm_params: float32 [4, 512], P(None, 'cout'), may hold values from 0.1 to 1.9
- head_w: float32 [512, 10], P('cout'), may hold values from -1 to 1
- head_b: float32 [10], replicated, may hold values from -1.75 to 1.75
- bases: bfloat16 [2, 2, 512, 512], replicated, may hold values from -1 to 1
- scales_first: float32 [9, 512, 512], P(None, None, 'cout'), may hold values from 0.0090112 to 0.073728
- scales_second: float32 [9, 512, 512], P(None, 'cout'), may hold values from 0.0090112 to 0.073728
- w_first_mean: float32 [9, 512, 512], P(None, None, 'cout'), may hold values from -0.00030517578 to 0.00030517578
- w_first_square: float32 [9, 512, 512], P(None, None, 'cout'), may hold values from 2.1192763e-10 to 8.477105e-10
- w_second_mean: float32 [9, 512, 512], P(None, 'cout'), may hold values from -0.00030517578 to 0.00030517578
- w_second_square: float32 [9, 512, 512], P(None, 'cout'), may hold values from 2.1192763e-10 to 8.477105e-10
- norm_mean: float32 [4, 512], P(None, 'cout'), may hold values from -9.3789174e-05 to 9.3789174e-05
- norm_square: float32 [4, 512], P(None, 'cout'), may hold values from 1.28e-14 to 1.573376e-10
- head_w_mean: float32 [512, 10], P('cout'), may hold values from -0.00012207031 to 0.00012207031
- head_w_square: float32 [512, 10], P('cout'), may hold values from 4.194304e-11 to 1.6777216e-10
- head_b_mean: float32 [10], replicated, may hold values from -0.00024414062 to 0.00024414062
- head_b_square: float32 [10], replicated, may hold values from 1.6777216e-10 to 6.815744e-10
Outputs:
- loss_total: float32 [], replicated
- grad_norm: float32 [], replicated
- w_first_new: float32 [9, 512, 512], P(None, None, 'cout')
- w_first_mean_new: float32 [9, 512, 512], P(None, None, 'cout')
- w_first_square_new: float32 [9, 512, 512], P(None, None, 'cout')
- w_second_new: float32 [9, 512, 512], P(None, 'cout')
- w_second_mean_new: float32 [9, 512, 512], P(None, 'cout')
- w_second_square_new: float32 [9, 512, 512], P(None, 'cout')
- norm_first_mean_new: float32 [2, 512], P(None, 'cout')
- norm_first_square_new: float32 [2, 512], P(None, 'cout')
- norm_second_mean_new: float32 [2, 512], P(None, 'cout')
- norm_second_square_new: float32 [2, 512], P(None, 'cout')
- head_w_mean_new: float32 [512, 10], P('cout')
- head_w_square_new: float32 [512, 10], P('cout')
- head_b_mean_new: float32 [10], replicated
- head_b_square_new: float32 [10], replicated
- scales_first_new: float32 [9, 512, 512], P(None, None, 'cout')
- scales_second_new: float32 [9, 512, 512], P(None, 'cout')
The draws below stay inside these ranges and needn't reach their ends.
Inputs may be any that keep to these rules, and one draw needn't show every extreme that they name: `masks`: each image keeps one rectangle of 2 to 4 by 2 to 4 pixels.
All inputs are finite; a program needn't handle non-finite values.
Results may differ from the reference program's by a relative error of at most 0.025.
Values may be sent and summed in bfloat16 or wider, within the bound.
No kernel may reach another device: no remote copies, remote signals or barrier semaphores. Data moves between devices by JAX's collectives and lax.ppermute only.
A program may use at most 128 MiB of HBM per device.

```python
import math
import jax
import jax.numpy as jnp
from jax import lax

C = 512
CLASSES = 10
SIDE = 4
PIX = 16
TAPS = 9
STEP = 10
BATCH = 512
N_COUT = 4


def draw_masks(key, part):
    key = jax.random.fold_in(key, 7)
    key_rows, key_cols, key_top, key_left = jax.random.split(key, 4)
    image_index = jnp.arange(BATCH, dtype=jnp.int32)
    crop_level = 2 + 3 * image_index // BATCH
    height = jnp.clip(crop_level + jax.random.randint(key_rows, (BATCH,), -1, 1), 2, SIDE)
    breadth = jnp.clip(crop_level + jax.random.randint(key_cols, (BATCH,), -1, 1), 2, SIDE)
    top_row = jax.random.randint(key_top, (BATCH,), 0, SIDE + 1 - height)
    left_col = jax.random.randint(key_left, (BATCH,), 0, SIDE + 1 - breadth)
    pixel_index = jnp.arange(PIX, dtype=jnp.int32)
    row_of = (pixel_index // SIDE)[:, None]
    col_of = (pixel_index % SIDE)[:, None]
    inside = (row_of >= top_row[None, :]) & (row_of < (top_row + height)[None, :])
    inside = inside & (col_of >= left_col[None, :]) & (col_of < (left_col + breadth)[None, :])
    return inside.astype(jnp.int32)


def scaled_rows(key, low_end, high_end):
    entries = jax.random.truncated_normal(key, -3.0, 3.0, (2, 2, C, C), jnp.float32)
    position = jnp.arange(C, dtype=jnp.float32) / (C - 1)
    row_scale = low_end * (high_end / low_end) ** position
    return entries * row_scale[None, None, :, None] / C ** 0.5


def draw_bases(key, part):
    key = jax.random.fold_in(key, 11)
    return scaled_rows(key, 0.6, 1.8).astype(jnp.bfloat16)


def layer_levels(first_level, second_level):
    return jnp.array([first_level, first_level, second_level, second_level], jnp.float32)[:, None]


def draw_norm_mean(key, part):
    key = jax.random.fold_in(key, 13)
    entries = jax.random.truncated_normal(key, -3.0, 3.0, (4, C), jnp.float32)
    return entries * layer_levels(2.4e-08 * BATCH ** 0.5, 6e-08 * BATCH)


def draw_norm_square(key, part):
    key = jax.random.fold_in(key, 17)
    spread = jnp.exp(jax.random.uniform(key, (4, C), jnp.float32, -0.6931, 0.6931))
    return spread * layer_levels(5e-17 * BATCH, 3e-16 * BATCH * BATCH)


def touch_ends(values, stream_key, least, top_value):
    longest = values.shape.index(max(values.shape))
    spots = []
    for shift in (0, 1):
        where = [jax.random.randint(jax.random.fold_in(stream_key, axis), (), 0, length) for axis, length in enumerate(values.shape)]
        where[longest] = (where[longest] + shift) % values.shape[longest]
        spots.append(tuple(where))
    return values.at[spots[0]].set(least).at[spots[1]].set(top_value)


def shard_levels(stream_key, shape, pieces, least, top_value):
    factor_of = 1.0
    for axis_at, parts in pieces:
        steps = jax.random.uniform(jax.random.fold_in(jax.random.fold_in(stream_key, 6), axis_at), (parts,), jnp.float32, least / len(pieces), top_value / len(pieces))
        factor_of = factor_of * jnp.repeat(jnp.exp(steps), shape[axis_at] // parts).reshape((-1,) + (1,) * (len(shape) - 1 - axis_at))
    return factor_of


def bell_draw(rng, dims, scale, bound, cuts=(), kind=jnp.bfloat16):
    factor_of = shard_levels(rng, dims, cuts, -0.22, 0.18) if cuts else 1.0
    values = jax.random.normal(rng, dims, jnp.float32) * scale * factor_of
    return jnp.minimum(jnp.maximum(values, -bound), bound).astype(kind)


def setup_inputs(seed: int = 0) -> dict:
    streams_of = jax.random.split(jax.random.key(seed), 22)
    images = bell_draw(streams_of[0], (PIX, BATCH, C), 1.0, 6.0, ((1, 8),))
    masks = draw_masks(jax.random.fold_in(streams_of[21], 71), 0)
    labels = touch_ends(jax.random.randint(streams_of[2], (BATCH,), 0, CLASSES), jax.random.fold_in(streams_of[2], 1), 0, CLASSES - 1).astype(jnp.int32)
    w_first = bell_draw(streams_of[3], (TAPS, C, C), (TAPS * C) ** -0.5, 0.09375, ((2, 4),), jnp.float32)
    w_second = bell_draw(streams_of[4], (TAPS, C, C), (TAPS * C) ** -0.5, 0.09375, ((1, 4),), jnp.float32)
    norm_params = jnp.clip(1.0 + 0.18 * jax.random.normal(streams_of[5], (4, C), jnp.float32), 0.1, 1.9)
    head_w = bell_draw(streams_of[6], (C, CLASSES), (C // 16) ** -0.5, 1.0, ((0, 4),), jnp.float32)
    head_b = bell_draw(streams_of[7], (CLASSES,), 0.3, 1.75, (), jnp.float32)
    bases = draw_bases(jax.random.fold_in(streams_of[21], 71), 0)
    scales_first = jnp.clip(jnp.exp(math.log(0.073728) - 2.1019145 * jax.random.uniform(streams_of[9], (TAPS, C, C), jnp.float32) ** shard_levels(streams_of[9], (TAPS, C, C), ((2, 4),), -0.2, 0.2)), 0.0090112, 0.073728)
    scales_second = jnp.clip(jnp.exp(math.log(0.073728) - 2.1019145 * jax.random.uniform(streams_of[10], (TAPS, C, C), jnp.float32) ** shard_levels(streams_of[10], (TAPS, C, C), ((1, 4),), -0.2, 0.2)), 0.0090112, 0.073728)
    w_first_mean = bell_draw(streams_of[11], (TAPS, C, C), (0.11 / (18 * C * C) ** 0.5), 0.00030517578, ((2, 4),), jnp.float32)
    w_first_square = jnp.clip(jnp.exp(math.log(8.477105128967821e-10) - 1.3862944 * jax.random.uniform(streams_of[12], (TAPS, C, C), jnp.float32) ** shard_levels(streams_of[12], (TAPS, C, C), ((2, 4),), -0.2, 0.2)), 2.1192762822419553e-10, 8.477105128967821e-10)
    w_second_mean = bell_draw(streams_of[13], (TAPS, C, C), (0.11 / (18 * C * C) ** 0.5), 0.00030517578, ((1, 4),), jnp.float32)
    w_second_square = jnp.clip(jnp.exp(math.log(8.477105128967821e-10) - 1.3862944 * jax.random.uniform(streams_of[14], (TAPS, C, C), jnp.float32) ** shard_levels(streams_of[14], (TAPS, C, C), ((1, 4),), -0.2, 0.2)), 2.1192762822419553e-10, 8.477105128967821e-10)
    norm_mean = draw_norm_mean(jax.random.fold_in(streams_of[21], 71), 0)
    norm_square = draw_norm_square(jax.random.fold_in(streams_of[21], 71), 0)
    head_w_mean = bell_draw(streams_of[17], (C, CLASSES), (4.4e-8 * BATCH), 0.00012207031, ((0, 4),), jnp.float32)
    head_w_square = jnp.clip(jnp.exp(math.log(1.6777215727792338e-10) - 1.3862944 * jax.random.uniform(streams_of[18], (C, CLASSES), jnp.float32) ** shard_levels(streams_of[18], (C, CLASSES), ((0, 4),), -0.2, 0.2)), 4.1943039319480846e-11, 1.6777215727792338e-10)
    head_b_mean = bell_draw(streams_of[19], (CLASSES,), (8.8e-8 * BATCH), 0.00024414062, (), jnp.float32)
    head_b_square = jnp.clip(jnp.exp(jax.random.uniform(streams_of[20], (CLASSES,), jnp.float32, math.log(1.6777215727792338e-10), math.log(6.81574408023522e-10))), 1.6777215727792338e-10, 6.81574408023522e-10)
    return dict(images=images, masks=masks, labels=labels, w_first=w_first, w_second=w_second, norm_params=norm_params, head_w=head_w, head_b=head_b, bases=bases, scales_first=scales_first, scales_second=scales_second, w_first_mean=w_first_mean, w_first_square=w_first_square, w_second_mean=w_second_mean, w_second_square=w_second_square, norm_mean=norm_mean, norm_square=norm_square, head_w_mean=head_w_mean, head_w_square=head_w_square, head_b_mean=head_b_mean, head_b_square=head_b_square)


PRECISE = lax.Precision.HIGHEST
EPS_NORM = 1e-05
SCALE_DECAY = 0.95
DAMPING = 0.001
CLIP_NORM = 1.0
LEARN_RATE = 0.01
BETA_ONE = 0.9
BETA_TWO = 0.999
ADAM_EPS = 1e-08
WEIGHT_DECAY = 0.01
SMOOTH = 0.1
OFFSETS = [(row_step, col_step) for row_step in (-1, 0, 1) for col_step in (-1, 0, 1)]

@jax.custom_vjp
def low(v):
    return lax.optimization_barrier(v.astype(jnp.bfloat16)).astype(jnp.float32)

@jax.custom_vjp
def low_back(v):
    return v

def low_keep(v):
    return (low(v), None)

def low_pass(kept, grad):
    return (grad,)

def back_keep(v):
    return (v, None)

def back_low(kept, grad):
    return (low(grad),)
low.defvjp(low_keep, low_pass)
low_back.defvjp(back_keep, back_low)

def shifted(values, row_step, col_step):
    cell_grid = values.reshape((SIDE, SIDE) + values.shape[1:])
    padding = [(1, 1), (1, 1)] + [(0, 0)] * (values.ndim - 1)
    padded = jnp.pad(cell_grid, padding)
    window = padded[1 + row_step:1 + row_step + SIDE, 1 + col_step:1 + col_step + SIDE]
    return window.reshape(values.shape)

def convolve(values, weight):
    summed = None
    for tap_index, (row_step, col_step) in enumerate(OFFSETS):
        product = jnp.einsum('pbi,io->pbo', shifted(values, row_step, col_step), weight[tap_index], precision=PRECISE)
        summed = product if summed is None else summed + product
    return summed

def normalize(values, mask_cube, kept_count, gain, offset):
    mean_value = lax.optimization_barrier(jnp.sum(values * mask_cube, axis=(0, 1))) / kept_count
    variance = lax.optimization_barrier(jnp.sum(values * values * mask_cube, axis=(0, 1))) / kept_count - mean_value * mean_value
    scaled = (values - mean_value) * lax.rsqrt(variance + EPS_NORM)
    return gain * scaled + offset

def forward(w_first, w_second, norm_params, head_w, head_b, probe_first, probe_second, inputs, mask_cube, kept_count, labels):
    first_out = low_back(convolve(inputs, low(w_first)) + probe_first)
    hidden = low(jax.nn.gelu(normalize(first_out, mask_cube, kept_count, norm_params[0], norm_params[1])) * mask_cube)
    second_low = low(w_second)
    block_width = C // N_COUT
    second_sum = None
    for block_index in range(N_COUT):
        lower_edge = block_index * block_width
        partial_out = low(convolve(hidden[:, :, lower_edge:lower_edge + block_width], second_low[:, lower_edge:lower_edge + block_width, :]))
        second_sum = partial_out if second_sum is None else second_sum + partial_out
    second_out = low_back(second_sum + probe_second)
    activated = jax.nn.gelu(normalize(second_out, mask_cube, kept_count, norm_params[2], norm_params[3])) * mask_cube
    pooled = lax.optimization_barrier(jnp.sum(activated, axis=0)) / PIX
    logits = jnp.dot(low(pooled), low(head_w), precision=PRECISE) + head_b
    log_probs = jax.nn.log_softmax(logits, axis=-1)
    smoothed = (1.0 - SMOOTH) * jax.nn.one_hot(labels, CLASSES, dtype=logits.dtype) + SMOOTH / CLASSES
    return (-jnp.sum(smoothed * log_probs), hidden)

def project(values, basis):
    return low(jnp.einsum('pbi,ij->pbj', values, basis, precision=PRECISE))

def coefficients(left_side, right_side):
    return jnp.stack([jnp.einsum('pbj,pbk->jk', shifted(left_side, row_step, col_step), right_side, precision=PRECISE) for row_step, col_step in OFFSETS])

def precondition(coeffs, scales, basis_in, basis_out):
    new_scales = SCALE_DECAY * scales + (1.0 - SCALE_DECAY) * coeffs * coeffs
    ratio = coeffs / (new_scales + DAMPING)
    middle = jnp.einsum('ij,tjk->tik', basis_in, ratio, precision=PRECISE)
    return (new_scales, jnp.einsum('tik,lk->til', middle, basis_out, precision=PRECISE))

def moments(gradient, mean_old, square_old):
    mean_new = BETA_ONE * mean_old + (1.0 - BETA_ONE) * gradient
    square_new = BETA_TWO * square_old + (1.0 - BETA_TWO) * gradient * gradient
    return (mean_new, square_new)

def adamw(weight, gradient, mean_old, square_old):
    mean_new, square_new = moments(gradient, mean_old, square_old)
    mean_hat = mean_new / (1.0 - BETA_ONE ** STEP)
    square_hat = square_new / (1.0 - BETA_TWO ** STEP)
    updated = weight - LEARN_RATE * (mean_hat / (jnp.sqrt(square_hat) + ADAM_EPS) + WEIGHT_DECAY * weight)
    return (updated, mean_new, square_new)

def reference(images, masks, labels, w_first, w_second, norm_params, head_w, head_b, bases, scales_first, scales_second, w_first_mean, w_first_square, w_second_mean, w_second_square, norm_mean, norm_square, head_w_mean, head_w_square, head_b_mean, head_b_square):
    mask_plane = masks.astype(jnp.float32)
    mask_cube = mask_plane[:, :, None]
    kept_count = jnp.sum(mask_plane)
    inputs = images.astype(jnp.float32) * mask_cube
    basis_full = bases.astype(jnp.float32)
    probe_zero = jnp.zeros((PIX, BATCH, C), jnp.float32)

    def objective(first_w, second_w, norm_w, head_weight, head_bias, probe_one, probe_two):
        return forward(first_w, second_w, norm_w, head_weight, head_bias, probe_one, probe_two, inputs, mask_cube, kept_count, labels)
    loss_total, vjp_fn, hidden = jax.vjp(objective, w_first, w_second, norm_params, head_w, head_b, probe_zero, probe_zero, has_aux=True)
    cotangents = vjp_fn(jnp.ones_like(loss_total))
    norm_grad, head_w_grad, head_b_grad, grad_first, grad_second = (cotangents[2], cotangents[3], cotangents[4], cotangents[5], cotangents[6])
    coeff_first = coefficients(project(inputs, basis_full[0, 0]), project(grad_first, basis_full[0, 1]))
    coeff_second = coefficients(project(hidden, basis_full[1, 0]), project(grad_second, basis_full[1, 1]))
    scales_first_new, precond_first = precondition(coeff_first, scales_first, basis_full[0, 0], basis_full[0, 1])
    scales_second_new, precond_second = precondition(coeff_second, scales_second, basis_full[1, 0], basis_full[1, 1])
    squares = jnp.sum(precond_first * precond_first) + jnp.sum(precond_second * precond_second)
    squares = squares + jnp.sum(norm_grad * norm_grad) + jnp.sum(head_w_grad * head_w_grad) + jnp.sum(head_b_grad * head_b_grad)
    grad_norm = jnp.sqrt(squares)
    factor = CLIP_NORM / jnp.maximum(grad_norm, CLIP_NORM)
    first_new, first_mean_new, first_square_new = adamw(w_first, factor * precond_first, w_first_mean, w_first_square)
    second_new, second_mean_new, second_square_new = adamw(w_second, factor * precond_second, w_second_mean, w_second_square)
    norm_mean_new, norm_square_new = moments(factor * norm_grad, norm_mean, norm_square)
    head_mean_new, head_square_new = moments(factor * head_w_grad, head_w_mean, head_w_square)
    bias_mean_new, bias_square_new = moments(factor * head_b_grad, head_b_mean, head_b_square)
    return (loss_total, grad_norm, first_new, first_mean_new, first_square_new, second_new, second_mean_new, second_square_new, norm_mean_new[:2], norm_square_new[:2], norm_mean_new[2:], norm_square_new[2:], head_mean_new, head_square_new, bias_mean_new, bias_square_new, scales_first_new, scales_second_new)
```

```python
import jax
import jax.numpy as jnp
from jax import lax
from jax.sharding import PartitionSpec as P

CLASSES = 10
SIDE = 4
PIX = 16
TAPS = 9
STEP = 10

EPS_NORM = 1e-05
SCALE_DECAY = 0.95
DAMPING = 0.001
CLIP_NORM = 1.0
LEARN_RATE = 0.01
BETA_ONE = 0.9
BETA_TWO = 0.999
ADAM_EPS = 1e-08
WEIGHT_DECAY = 0.01
SMOOTH = 0.1
OFFSETS = [(row_step, col_step) for row_step in (-1, 0, 1) for col_step in (-1, 0, 1)]
EVERY = ("dp", "cout", "cin")
BF = jnp.bfloat16
F32 = jnp.float32


def shifted(values, row_step, col_step):
    cell_grid = values.reshape((SIDE, SIDE) + values.shape[1:])
    padding = [(1, 1), (1, 1)] + [(0, 0)] * (values.ndim - 1)
    padded = jnp.pad(cell_grid, padding)
    window = padded[1 + row_step : 1 + row_step + SIDE, 1 + col_step : 1 + col_step + SIDE]
    return window.reshape(values.shape)


def convolve(values, weight):
    summed = None
    for tap_index, (row_step, col_step) in enumerate(OFFSETS):
        product = jnp.einsum(
            "pbi,io->pbo",
            shifted(values, row_step, col_step),
            weight[tap_index],
            preferred_element_type=F32,
        )
        summed = product if summed is None else summed + product
    return summed


def convolve_back(cotangent, weight):
    summed = None
    for tap_index, (row_step, col_step) in enumerate(OFFSETS):
        product = jnp.einsum(
            "pbo,io->pbi",
            shifted(cotangent, -row_step, -col_step),
            weight[tap_index],
            preferred_element_type=F32,
        )
        summed = product if summed is None else summed + product
    return summed


def swap(values, axis, step):
    count = lax.axis_size(axis)
    return lax.ppermute(values, axis, [(here, here ^ step) for here in range(count)])


def gathered(values, axis):
    return [values] + [swap(values, axis, step) for step in range(1, lax.axis_size(axis))]


def exchanged(block_of, axis):
    me = lax.axis_index(axis)
    return [block_of(me)] + [
        swap(block_of(me ^ step), axis, step) for step in range(1, lax.axis_size(axis))
    ]


def tree_sum(slots):
    while len(slots) > 1:
        slots = [slots[at] + slots[at + 1] for at in range(0, len(slots), 2)]
    return slots[0]


def in_order(slots, axis):
    me = lax.axis_index(axis)
    stacked = jnp.stack(slots)
    return [
        lax.dynamic_index_in_dim(stacked, me ^ place, 0, keepdims=False)
        for place in range(len(slots))
    ]


def spread_sum(block):
    sizes = tuple(lax.axis_size(name) for name in EVERY)
    total = sizes[0] * sizes[1] * sizes[2]
    sent = jnp.broadcast_to(block[None], (total,) + block.shape)
    got = lax.all_to_all(sent, EVERY, 0, 0, tiled=True)
    return got.reshape(sizes + block.shape)


def moments(gradient, mean_old, square_old):
    mean_new = BETA_ONE * mean_old + (1.0 - BETA_ONE) * gradient
    square_new = BETA_TWO * square_old + (1.0 - BETA_TWO) * gradient * gradient
    return (mean_new, square_new)


def adamw(weight, gradient, mean_old, square_old):
    mean_new, square_new = moments(gradient, mean_old, square_old)
    mean_hat = mean_new / (1.0 - BETA_ONE**STEP)
    square_hat = square_new / (1.0 - BETA_TWO**STEP)
    updated = weight - LEARN_RATE * (
        mean_hat / (jnp.sqrt(square_hat) + ADAM_EPS) + WEIGHT_DECAY * weight
    )
    return (updated, mean_new, square_new)


def gelu_back(pre_values, upstream):
    return jax.vjp(jax.nn.gelu, pre_values)[1](upstream)[0]


def norm_back(dz_values, scaled, inverse_std, gain, gain_grad, shift_grad, mask_cube, kept_count):
    return inverse_std * (
        gain * dz_values - mask_cube * gain * (shift_grad + scaled * gain_grad) / kept_count
    )


def project(values, basis):
    return jnp.einsum("pbi,ij->pbj", values, basis, preferred_element_type=F32).astype(BF)


def tap_products(left_side, right_side, spec):
    return jnp.concatenate(
        [
            jnp.einsum(
                spec,
                shifted(left_side, row_step, col_step),
                right_side,
                preferred_element_type=F32,
            ).astype(BF)
            for row_step, col_step in OFFSETS
        ],
        axis=0,
    )


def batch_scatter(partial):
    count_dp, count_cin = lax.axis_size("dp"), lax.axis_size("cin")
    rows, width = partial.shape
    split = partial.reshape(count_dp, count_cin, rows // (count_dp * count_cin), width)
    slots = exchanged(lambda k: lax.dynamic_index_in_dim(split, k, 1, keepdims=False), "cin")
    near = sum(slot.astype(F32) for slot in slots).astype(BF)
    slots = exchanged(lambda k: lax.dynamic_index_in_dim(near, k, 0, keepdims=False), "dp")
    return sum(slot.astype(F32) for slot in slots)


def batch_gather(block):
    far = jnp.stack(in_order(gathered(block, "dp"), "dp"))
    both = in_order(gathered(far, "cin"), "cin")
    return jnp.stack(both, axis=1).reshape(-1, block.shape[-1])


def batch_rows(values):
    count_cin = lax.axis_size("cin")
    count = lax.axis_size("dp") * count_cin
    place = lax.axis_index("dp") * count_cin + lax.axis_index("cin")
    rows = values.shape[0] // count
    return lax.dynamic_slice_in_dim(values, place * rows, rows, 0)


def local(
    images,
    masks,
    labels,
    w_first,
    w_second,
    norm_params,
    head_w,
    head_b,
    bases,
    scales_first,
    scales_second,
    w_first_mean,
    w_first_square,
    w_second_mean,
    w_second_square,
    norm_mean,
    norm_square,
    head_w_mean,
    head_w_square,
    head_b_mean,
    head_b_square,
):
    me = lax.axis_index("cout")
    groups = lax.axis_size("cout")
    count_cin = lax.axis_size("cin")
    channels = w_first.shape[1]
    width = w_first.shape[2]
    part = images.shape[1] // groups
    mine = lambda values, axis: lax.dynamic_slice_in_dim(values, me * part, part, axis)
    block = lambda values, k, axis: lax.dynamic_slice_in_dim(values, k * width, width, axis)
    in_slots = lambda values, axis: jnp.concatenate(
        [block(values, me ^ step, axis) for step in range(groups)], axis
    )

    second_low = w_second.astype(BF)
    depth = width // count_cin
    piece = lax.dynamic_slice_in_dim(second_low, lax.axis_index("cin") * depth, depth, 1)
    w_blocks = []
    for slot in gathered(piece, "cout"):
        w_blocks.append(jnp.concatenate(in_order(gathered(slot, "cin"), "cin"), axis=1))
    w_full = jnp.concatenate(in_order(w_blocks, "cout"), axis=1)

    small = jnp.concatenate([norm_params, head_w.T, jnp.zeros((2, width), F32)], axis=0)
    small = jnp.concatenate(in_order(gathered(small, "cout"), "cout"), axis=1)
    gain_first, offset_first, gain_second, offset_second = (small[row] for row in range(4))
    head_full = small[4 : 4 + CLASSES].T

    mask_plane = masks.astype(F32)
    inputs = images * masks.astype(BF)[:, :, None]
    first_block = convolve(inputs, w_first.astype(BF))
    masked = first_block * mask_plane[:, :, None]
    stats = jnp.stack(
        [
            jnp.sum(masked, axis=(0, 1)),
            jnp.sum(masked * first_block, axis=(0, 1)),
            jnp.full((width,), jnp.sum(mask_plane)),
        ]
        + [jnp.zeros((width,), F32)] * 5
    )
    first_low = first_block.astype(BF)
    first_out = jnp.concatenate(
        in_order(
            exchanged(
                lambda k: lax.dynamic_slice_in_dim(first_low, k * part, part, 1), "cout"
            ),
            "cout",
        ),
        axis=2,
    ).astype(F32)
    stats = jnp.sum(spread_sum(stats), axis=(0, 2))
    stats = jnp.moveaxis(stats, 0, 1).reshape(8, -1)
    kept_count = stats[2, 0]
    mask_cube = mine(mask_plane, 1)[:, :, None]

    def standardised(values, first_sum, square_sum):
        mean_value = first_sum / kept_count
        inverse_std = lax.rsqrt(square_sum / kept_count - mean_value * mean_value + EPS_NORM)
        return ((values - mean_value) * inverse_std, inverse_std)

    def all_sums(*rows):
        packed = jnp.stack(rows).reshape(-1, 128)
        summed = jnp.sum(spread_sum(packed), axis=(0, 1, 2))
        return summed.reshape(len(rows), -1)

    scaled_first, rstd_first = standardised(first_out, stats[0], stats[1])
    pre_first = gain_first * scaled_first + offset_first
    hidden = (jax.nn.gelu(pre_first) * mask_cube).astype(BF)
    second_out = convolve(hidden, w_full)
    masked = second_out * mask_cube
    sums = all_sums(jnp.sum(masked, axis=(0, 1)), jnp.sum(masked * second_out, axis=(0, 1)))
    scaled_second, rstd_second = standardised(second_out, sums[0], sums[1])
    pre_second = gain_second * scaled_second + offset_second
    pooled_low = (jnp.sum(jax.nn.gelu(pre_second) * mask_cube, axis=0) / PIX).astype(BF)
    head_low = head_full.astype(BF)
    logits = jnp.dot(pooled_low, head_low, preferred_element_type=F32) + head_b
    log_probs = jax.nn.log_softmax(logits, axis=-1)
    smoothed = (1.0 - SMOOTH) * jax.nn.one_hot(
        mine(labels, 0), CLASSES, dtype=F32
    ) + SMOOTH / CLASSES
    loss_local = -jnp.sum(smoothed * log_probs)
    logit_grad = jnp.exp(log_probs) - smoothed
    precise = lax.Precision.HIGHEST
    head_part = jnp.dot(logit_grad.T, pooled_low.astype(F32), precision=precise)
    bias_part = jnp.sum(logit_grad, axis=0)
    pooled_grad = jnp.dot(logit_grad, head_low.astype(F32).T, precision=precise)
    dz_second = gelu_back(pre_second, mask_cube * pooled_grad[None, :, :] / PIX)
    gain_two, shift_two = all_sums(
        jnp.sum(dz_second * scaled_second, axis=(0, 1)), jnp.sum(dz_second, axis=(0, 1))
    )
    grad_second = norm_back(
        dz_second, scaled_second, rstd_second, gain_second, gain_two, shift_two, mask_cube, kept_count
    ).astype(BF)
    hidden_grad = convolve_back(grad_second, w_full)
    dz_first = gelu_back(pre_first, hidden_grad * mask_cube)
    gain_one, shift_one = all_sums(
        jnp.sum(dz_first * scaled_first, axis=(0, 1)), jnp.sum(dz_first, axis=(0, 1))
    )
    grad_first = norm_back(
        dz_first, scaled_first, rstd_first, gain_first, gain_one, shift_one, mask_cube, kept_count
    ).astype(BF)

    tail_row = jnp.concatenate([bias_part, loss_local[None], jnp.zeros((width - CLASSES - 1,), F32)])
    tail_row = jnp.broadcast_to(tail_row[None, None], (groups, 1, width))
    head_blocks = jnp.moveaxis(head_part.reshape(CLASSES, groups, width), 1, 0)
    head_blocks = jnp.concatenate(
        [head_blocks, tail_row, jnp.zeros((groups, 5, width), F32)], axis=1
    )
    sizes = tuple(lax.axis_size(name) for name in EVERY)
    sent = jnp.broadcast_to(head_blocks[None, :, None], sizes + head_blocks.shape[1:])
    got = lax.all_to_all(sent.reshape((-1,) + head_blocks.shape[1:]), EVERY, 0, 0, tiled=True)
    head_sums = jnp.sum(got, axis=0)
    head_w_grad = head_sums[:CLASSES].T
    head_b_grad = head_sums[CLASSES, :CLASSES]
    loss_total = head_sums[CLASSES, CLASSES]

    def by_images(values):
        return jnp.concatenate(exchanged(lambda k: block(values, k, 2), "cout"), axis=1)

    def slot_images(values):
        return jnp.concatenate(
            [
                lax.dynamic_slice_in_dim(values, (me ^ step) * part, part, 1)
                for step in range(groups)
            ],
            axis=1,
        )

    basis_in_first, basis_out_first = bases[0, 0], bases[0, 1]
    basis_in_second, basis_out_second = bases[1, 0], bases[1, 1]

    def layer(left, right, spec, scales, basis_rows):
        own = batch_scatter(tap_products(left, right, spec))
        scales_own = batch_rows(scales)
        scales_own = SCALE_DECAY * scales_own + (1.0 - SCALE_DECAY) * own * own
        ratio = (own / (scales_own + DAMPING)).astype(BF)
        ratio = jnp.concatenate(gathered(ratio, "cout"), axis=1)
        middle = jnp.dot(ratio, basis_rows.T, preferred_element_type=F32).astype(BF)
        return batch_gather(own.astype(BF)).astype(F32), batch_gather(middle)

    left_second = by_images(project(hidden, basis_in_second))
    right_second = jnp.concatenate(gathered(project(grad_second, basis_out_second), "cout"), axis=1)
    coeff_second, middle_second = layer(
        left_second,
        right_second,
        "pbj,pbk->kj",
        jnp.swapaxes(scales_second, 1, 2).reshape(-1, width),
        in_slots(block(basis_in_second, me, 0), 1),
    )
    coeff_second = jnp.swapaxes(coeff_second.reshape(TAPS, channels, width), 1, 2)
    precond_second = jnp.einsum(
        "tki,lk->til",
        middle_second.reshape(TAPS, channels, width),
        basis_out_second,
        preferred_element_type=F32,
    )

    left_first = slot_images(project(inputs, basis_in_first))
    right_first = by_images(project(grad_first, basis_out_first))
    coeff_first, middle_first = layer(
        left_first,
        right_first,
        "pbj,pbk->jk",
        scales_first.reshape(-1, width),
        in_slots(block(basis_out_first, me, 0), 1),
    )
    coeff_first = coeff_first.reshape(TAPS, channels, width)
    precond_first = jnp.einsum(
        "ij,tjl->til",
        basis_in_first,
        middle_first.reshape(TAPS, channels, width),
        preferred_element_type=F32,
    )

    scales_first_new = SCALE_DECAY * scales_first + (1.0 - SCALE_DECAY) * coeff_first * coeff_first
    scales_second_new = (
        SCALE_DECAY * scales_second + (1.0 - SCALE_DECAY) * coeff_second * coeff_second
    )
    norm_grad = block(jnp.stack([gain_one, shift_one, gain_two, shift_two]), me, 1)
    bias_square = jnp.where(me == 0, jnp.sum(head_b_grad * head_b_grad), 0.0)
    local_square = jnp.sum(precond_first * precond_first) + jnp.sum(precond_second * precond_second)
    local_square = (
        local_square
        + jnp.sum(norm_grad * norm_grad)
        + jnp.sum(head_w_grad * head_w_grad)
        + bias_square
    )
    square_sum = tree_sum(gathered(jnp.full((8, 128), local_square), "cout"))[0, 0]
    grad_norm = jnp.sqrt(square_sum)
    factor = CLIP_NORM / jnp.maximum(grad_norm, CLIP_NORM)
    first_new, first_mean_new, first_square_new = adamw(
        w_first, factor * precond_first, w_first_mean, w_first_square
    )
    second_new, second_mean_new, second_square_new = adamw(
        w_second, factor * precond_second, w_second_mean, w_second_square
    )
    norm_mean_new, norm_square_new = moments(factor * norm_grad, norm_mean, norm_square)
    head_mean_new, head_square_new = moments(factor * head_w_grad, head_w_mean, head_w_square)
    bias_mean_new, bias_square_new = moments(factor * head_b_grad, head_b_mean, head_b_square)
    return (
        loss_total,
        grad_norm,
        first_new,
        first_mean_new,
        first_square_new,
        second_new,
        second_mean_new,
        second_square_new,
        norm_mean_new[:2],
        norm_square_new[:2],
        norm_mean_new[2:],
        norm_square_new[2:],
        head_mean_new,
        head_square_new,
        bias_mean_new,
        bias_square_new,
        scales_first_new,
        scales_second_new,
    )
def solution(mesh):
    return jax.shard_map(
        local,
        mesh=mesh,
        in_specs=(
            P(None, ("dp", "cin"), None),
            P(None, ("dp", "cin")),
            P(("dp", "cin")),
            P(None, None, "cout"),
            P(None, "cout", None),
            P(None, "cout"),
            P("cout", None),
            P(),
            P(),
            P(None, None, "cout"),
            P(None, "cout", None),
            P(None, None, "cout"),
            P(None, None, "cout"),
            P(None, "cout", None),
            P(None, "cout", None),
            P(None, "cout"),
            P(None, "cout"),
            P("cout", None),
            P("cout", None),
            P(),
            P(),
        ),
        out_specs=(
            P(),
            P(),
            P(None, None, "cout"),
            P(None, None, "cout"),
            P(None, None, "cout"),
            P(None, "cout", None),
            P(None, "cout", None),
            P(None, "cout", None),
            P(None, "cout"),
            P(None, "cout"),
            P(None, "cout"),
            P(None, "cout"),
            P("cout", None),
            P("cout", None),
            P(),
            P(),
            P(None, None, "cout"),
            P(None, "cout", None),
        ),
        check_vma=False,
    )
```

```python
import functools
import math

import jax
import jax.numpy as jnp
from jax import lax
from jax.experimental import pallas as pl
from jax.experimental.pallas import tpu as pltpu
from jax.sharding import PartitionSpec as P

CLASSES = 10
SIDE = 4
PIX = 16
TAPS = 9
STEP = 10
LANES = 128

EPS_NORM = 1e-05
SCALE_DECAY = 0.95
DAMPING = 0.001
CLIP_NORM = 1.0
LEARN_RATE = 0.01
BETA_ONE = 0.9
BETA_TWO = 0.999
ADAM_EPS = 1e-08
WEIGHT_DECAY = 0.01
SMOOTH = 0.1
OFFSETS = [(row_step, col_step) for row_step in (-1, 0, 1) for col_step in (-1, 0, 1)]
EVERY = ("dp", "cout", "cin")
BF = jnp.bfloat16
F32 = jnp.float32
PRECISE = lax.Precision.HIGHEST
NN = (((1,), (0,)), ((), ()))
NT = (((1,), (1,)), ((), ()))
TN = (((0,), (0,)), ((), ()))
VMEM_BYTES = 40 * 1024 * 1024


def matmul(left, right, dims=NN, precision=None):
    return lax.dot_general(
        left, right, dims, precision=precision, preferred_element_type=F32
    )


def runs(row_step, col_step, count):
    low, high = max(0, -col_step), min(SIDE, SIDE - col_step)
    found = []
    for row in range(max(0, -row_step), min(SIDE, SIDE - row_step)):
        to_row = (row * SIDE + low) * count
        from_row = ((row + row_step) * SIDE + low + col_step) * count
        length = (high - low) * count
        if found and found[-1][0] + found[-1][2] == to_row and found[-1][1] + found[-1][2] == from_row:
            found[-1] = (found[-1][0], found[-1][1], found[-1][2] + length)
        else:
            found.append((to_row, from_row, length))
    return found


def call(kernel, outs, args, scratch=(), flops=0, scalars=1):
    specs = [pl.BlockSpec(memory_space=pltpu.SMEM)] * scalars
    specs += [pl.BlockSpec(memory_space=pltpu.VMEM)] * (len(args) - scalars)
    moved = sum(math.prod(a.shape) * a.dtype.itemsize for a in list(args) + list(outs))
    return pl.pallas_call(
        kernel,
        out_shape=list(outs),
        in_specs=specs,
        out_specs=[pl.BlockSpec(memory_space=pltpu.VMEM)] * len(outs),
        scratch_shapes=list(scratch),
        compiler_params=pltpu.CompilerParams(vmem_limit_bytes=VMEM_BYTES),
        cost_estimate=pl.CostEstimate(flops=flops, bytes_accessed=moved, transcendentals=0),
    )(*args)


def shape(dims, dtype):
    return jax.ShapeDtypeStruct(dims, dtype)


def gelu_parts(values):
    rate = math.sqrt(2.0 / math.pi)
    bend = jnp.tanh(rate * (values + 0.044715 * values * values * values))
    share = 0.5 * (1.0 + bend)
    slope = share + 0.5 * values * (1.0 - bend * bend) * rate * (1.0 + 0.134145 * values * values)
    return values * share, slope


def fill_mask(masks_ref, mask_ref):
    count = masks_ref.shape[1]
    same = lax.broadcasted_iota(jnp.int32, (count, count), 0) == lax.broadcasted_iota(
        jnp.int32, (count, count), 1
    )
    for pixel in range(PIX):
        row = masks_ref[pixel : pixel + 1, :].astype(F32)
        column = jnp.sum(jnp.where(same, row, 0.0), axis=1, keepdims=True)
        mask_ref[pixel * count : (pixel + 1) * count, :] = jnp.broadcast_to(column, (count, LANES))


def fill_inputs(images_ref, mask_ref, inputs_ref):
    low = mask_ref[...].astype(BF)
    for lane in range(0, images_ref.shape[1], LANES):
        inputs_ref[:, lane : lane + LANES] = images_ref[:, lane : lane + LANES] * low


def first_kernel(
    groups, place_ref, images_ref, masks_ref, weight_ref, params_ref,
    out_ref, stats_ref, own_mask_ref, mask_ref, inputs_ref, low_ref, sum_ref,
):
    count = masks_ref.shape[1]
    part = count // groups
    me = place_ref[0]
    fill_mask(masks_ref, mask_ref)
    fill_inputs(images_ref, mask_ref, inputs_ref)
    for tap in range(TAPS):
        low_ref[:, tap * LANES : (tap + 1) * LANES] = weight_ref[tap].astype(BF)
    sum_ref[...] = jnp.zeros_like(sum_ref)
    for tap in range(0, TAPS, 2):
        taps = min(2, TAPS - tap)
        product = matmul(inputs_ref[...], low_ref[:, tap * LANES : (tap + taps) * LANES])
        for nth in range(taps):
            for to_row, from_row, length in runs(*OFFSETS[tap + nth], count):
                sum_ref[to_row : to_row + length, :] += product[
                    from_row : from_row + length, nth * LANES : (nth + 1) * LANES
                ]
    mask = mask_ref[...]
    total = sum_ref[...]
    masked = total * mask
    tile = jnp.concatenate(
        [
            jnp.sum(masked, axis=0, keepdims=True),
            jnp.sum(masked * total, axis=0, keepdims=True),
            jnp.sum(mask, axis=0, keepdims=True),
            params_ref[0:2, :],
            jnp.zeros((3, LANES), F32),
        ],
        axis=0,
    )
    stats_ref[...] = jnp.broadcast_to(tile[None], stats_ref.shape)
    for pixel in range(PIX):
        for group in range(groups):
            base = pixel * count + group * part
            out_ref[group, pixel * part : (pixel + 1) * part, :] = sum_ref[base : base + part, :].astype(BF)
        own = pl.multiple_of(pixel * count + me * part, part)
        own_mask_ref[pixel * part : (pixel + 1) * part, :] = mask_ref[pl.ds(own, part), :]


def first_norm_kernel(sizes, place_ref, slot_refs, got_ref, mask_ref, hidden_ref, first_ref, norm_ref):
    count_dp, groups, count_cin = sizes
    me = place_ref[0]
    tiles = []
    for group in range(groups):
        total = None
        for far in range(count_dp):
            for near in range(count_cin):
                tile = got_ref[(far * groups + group) * count_cin + near]
                total = tile if total is None else total + tile
        tiles.append((total, got_ref[group * count_cin]))
    kept = tiles[0][0][2:3, :]
    for group, (total, single) in enumerate(tiles):
        lanes = slice(group * LANES, (group + 1) * LANES)
        mean = total[0:1, :] / kept
        norm_ref[0:1, lanes] = mean
        norm_ref[1:2, lanes] = lax.rsqrt(total[1:2, :] / kept - mean * mean + EPS_NORM)
        norm_ref[2:4, lanes] = single[3:5, :]
        norm_ref[4:5, lanes] = kept
        norm_ref[5:8, lanes] = jnp.zeros((3, LANES), F32)
    for step, slot_ref in enumerate(slot_refs):
        lanes = pl.ds(pl.multiple_of((me ^ step) * LANES, LANES), LANES)
        low = slot_ref[...]
        scaled = (low.astype(F32) - norm_ref[0:1, lanes]) * norm_ref[1:2, lanes]
        value, _ = gelu_parts(norm_ref[2:3, lanes] * scaled + norm_ref[3:4, lanes])
        hidden_ref[:, lanes] = (value * mask_ref[...]).astype(BF)
        first_ref[:, lanes] = low


def second_kernel(
    place_ref, own_ref, other_ref, own_mask_ref, other_mask_ref, params_ref, slot_refs,
    mine_ref, theirs_ref, stats_ref, inputs_ref, weight_ref, sum_ref,
):
    me = place_ref[0]
    rows = own_ref.shape[0]
    part = rows // PIX
    depth, half = slot_refs[0].shape[1:]
    inputs_ref[0:rows, :] = own_ref[...]
    inputs_ref[rows : 2 * rows, :] = other_ref[...]
    for step, slot_ref in enumerate(slot_refs):
        span = pl.ds(pl.multiple_of((me ^ step) * depth, depth), depth)
        for tap in range(TAPS):
            weight_ref[span, tap * half : (tap + 1) * half] = slot_ref[tap]
    sum_ref[...] = jnp.zeros_like(sum_ref)
    for tap in range(TAPS):
        product = matmul(inputs_ref[...], weight_ref[:, tap * half : (tap + 1) * half])
        for to_row, from_row, length in runs(*OFFSETS[tap], part):
            for base in (0, rows):
                sum_ref[base + to_row : base + to_row + length, :] += product[
                    base + from_row : base + from_row + length, :
                ]
    mine_ref[...] = sum_ref[0:rows, :]
    theirs_ref[...] = sum_ref[rows : 2 * rows, :]
    lines = [[], []]
    for lane in range(0, half, LANES):
        first = square = None
        for base, mask_ref in ((0, own_mask_ref), (rows, other_mask_ref)):
            total = sum_ref[base : base + rows, lane : lane + LANES]
            masked = total * mask_ref[...]
            first_part = jnp.sum(masked, axis=0, keepdims=True)
            square_part = jnp.sum(masked * total, axis=0, keepdims=True)
            first = first_part if first is None else first + first_part
            square = square_part if square is None else square + square_part
        lines[0].append(first)
        lines[1].append(square)
    spare = 8 - 2 * (half // LANES) - 2
    tile = jnp.concatenate(
        lines[0] + lines[1] + [params_ref[2:4, :], jnp.zeros((spare, LANES), F32)], axis=0
    )
    stats_ref[...] = jnp.broadcast_to(tile[None], stats_ref.shape)


def head_kernel(
    sizes, place_ref, mine_ref, got_ref_rows, got_ref, norm_first_ref, mask_ref, head_ref, bias_ref, labels_ref,
    wide_ref, norm_ref, dz_ref, sums_ref, head_out_ref, slope_ref, pooled_ref, weight_ref,
):
    count_dp, groups, count_cin = sizes
    side = place_ref[1]
    rows, half = mine_ref.shape
    part = rows // PIX
    blocks = half // LANES
    wide_ref[:, pl.ds(pl.multiple_of(side * half, half), half)] = mine_ref[...]
    wide_ref[:, pl.ds(pl.multiple_of((1 - side) * half, half), half)] = got_ref_rows[...]
    totals = [None, None]
    for source in range(count_dp * groups * count_cin):
        which = source % count_cin % 2
        tile = got_ref[source]
        totals[which] = tile if totals[which] is None else totals[which] + tile
    kept = norm_first_ref[4:5, 0:LANES]
    mask = mask_ref[...]
    for group in range(groups):
        lanes = slice(group * LANES, (group + 1) * LANES)
        total, line = totals[group // blocks], group % blocks
        mean = total[line : line + 1, :] / kept
        rstd = lax.rsqrt(total[blocks + line : blocks + line + 1, :] / kept - mean * mean + EPS_NORM)
        single = got_ref[group * count_cin]
        gain = single[2 * blocks : 2 * blocks + 1, :]
        shift = single[2 * blocks + 1 : 2 * blocks + 2, :]
        norm_ref[0:1, lanes] = mean
        norm_ref[1:2, lanes] = rstd
        norm_ref[2:3, lanes] = gain
        norm_ref[3:4, lanes] = shift
        norm_ref[4:8, lanes] = jnp.broadcast_to(kept, (4, LANES))
        value, slope = gelu_parts(gain * ((wide_ref[:, lanes] - mean) * rstd) + shift)
        slope_ref[:, lanes] = slope * mask * (1.0 / PIX)
        pooled_ref[:, lanes] = jnp.sum((value * mask).reshape(PIX, part, LANES), axis=0) * (1.0 / PIX)
        weight_ref[0:16, lanes] = head_ref[group]
    weight_ref[16:LANES, :] = jnp.zeros((LANES - 16, weight_ref.shape[1]), F32)
    pooled = pooled_ref[...].astype(BF)
    head = weight_ref[...].astype(BF)
    class_index = lax.broadcasted_iota(jnp.int32, (part, LANES), 1)
    logits = matmul(pooled, head, NT) + bias_ref[...]
    logits = jnp.where(class_index < CLASSES, logits, -1e30)
    logits = logits - jnp.max(logits, axis=1, keepdims=True)
    log_probs = logits - jnp.log(jnp.sum(jnp.exp(logits), axis=1, keepdims=True))
    wanted = jnp.where(class_index == labels_ref[...], 1.0 - SMOOTH, 0.0) + SMOOTH / CLASSES
    wanted = jnp.where(class_index < CLASSES, wanted, 0.0)
    loss = -jnp.sum(jnp.sum(wanted * log_probs, axis=1, keepdims=True), axis=0, keepdims=True)
    logit_grad = jnp.exp(log_probs) - wanted
    head_grad = matmul(logit_grad, pooled.astype(F32), TN, PRECISE)
    pooled_grad = matmul(logit_grad, head.astype(F32), NN, PRECISE)
    extra = jnp.sum(logit_grad, axis=0, keepdims=True)
    extra = jnp.where(class_index[0:1, :] == CLASSES, loss, extra)
    line = lax.broadcasted_iota(jnp.int32, (16, LANES), 0)
    gains, shifts = [], []
    for group in range(groups):
        lanes = slice(group * LANES, (group + 1) * LANES)
        head_out_ref[group] = jnp.where(line == CLASSES, extra, head_grad[0:16, lanes])
        spread = jnp.broadcast_to(pooled_grad[:, lanes][None], (PIX, part, LANES)).reshape(rows, LANES)
        dz = slope_ref[:, lanes] * spread
        dz_ref[:, lanes] = dz
        scaled = (wide_ref[:, lanes] - norm_ref[0:1, lanes]) * norm_ref[1:2, lanes]
        gains.append(jnp.sum(dz * scaled, axis=0, keepdims=True))
        shifts.append(jnp.sum(dz, axis=0, keepdims=True))
    sums_ref[...] = jnp.broadcast_to(jnp.concatenate(gains + shifts, axis=0)[None], sums_ref.shape)


def total_of(got_ref):
    total = got_ref[0]
    for source in range(1, got_ref.shape[0]):
        total = total + got_ref[source]
    return total


def norm_back(values, dz, norm, mask, gain_grad, shift_grad):
    scaled = (values - norm[0:1, :]) * norm[1:2, :]
    gain = norm[2:3, :]
    return norm[1:2, :] * (
        gain * dz - mask * (gain / norm[4:5, :]) * (shift_grad + scaled * gain_grad)
    )


def second_back_kernel(
    dz_ref, wide_ref, norm_ref, got_ref, mask_ref, basis_ref, grad_ref, right_ref, sums_ref
):
    total = total_of(got_ref)
    sums_ref[...] = total
    groups = total.shape[0] // 2
    for group in range(groups):
        lanes = slice(group * LANES, (group + 1) * LANES)
        grad_ref[:, lanes] = norm_back(
            wide_ref[:, lanes], dz_ref[:, lanes], norm_ref[:, lanes], mask_ref[...],
            total[group : group + 1, :], total[groups + group : groups + group + 1, :],
        ).astype(BF)
    right_ref[...] = jnp.transpose(matmul(grad_ref[...], basis_ref[...])).astype(BF)


def conv_back_kernel(grad_ref, weight_ref, first_ref, norm_ref, mask_ref, dz_ref, sums_ref, sum_ref):
    rows, channels = grad_ref.shape
    part = rows // PIX
    sum_ref[...] = jnp.zeros_like(sum_ref)
    for tap in range(TAPS):
        product = matmul(grad_ref[...], weight_ref[tap], NT)
        row_step, col_step = OFFSETS[tap]
        for to_row, from_row, length in runs(-row_step, -col_step, part):
            sum_ref[to_row : to_row + length, :] += product[from_row : from_row + length, :]
    mask = mask_ref[...]
    gains, shifts = [], []
    for lane in range(0, channels, LANES):
        lanes = slice(lane, lane + LANES)
        norm = norm_ref[:, lanes]
        scaled = (first_ref[:, lanes].astype(F32) - norm[0:1, :]) * norm[1:2, :]
        _, slope = gelu_parts(norm[2:3, :] * scaled + norm[3:4, :])
        dz = slope * mask * sum_ref[:, lanes]
        dz_ref[:, lanes] = dz
        gains.append(jnp.sum(dz * scaled, axis=0, keepdims=True))
        shifts.append(jnp.sum(dz, axis=0, keepdims=True))
    sums_ref[...] = jnp.broadcast_to(jnp.concatenate(gains + shifts, axis=0)[None], sums_ref.shape)


def first_back_kernel(
    dz_ref, first_ref, norm_ref, got_ref, mask_ref, basis_ref, right_ref, sums_ref, grad_ref
):
    total = total_of(got_ref)
    sums_ref[...] = total
    groups = total.shape[0] // 2
    for group in range(groups):
        lanes = slice(group * LANES, (group + 1) * LANES)
        grad_ref[:, lanes] = norm_back(
            first_ref[:, lanes].astype(F32), dz_ref[:, lanes], norm_ref[:, lanes], mask_ref[...],
            total[group : group + 1, :], total[groups + group : groups + group + 1, :],
        ).astype(BF)
    product = matmul(grad_ref[...], basis_ref[...])
    for group in range(groups):
        right_ref[group] = product[:, group * LANES : (group + 1) * LANES].astype(BF)


def left_first_kernel(place_ref, images_ref, masks_ref, basis_ref, left_ref, mask_ref, inputs_ref, part_ref):
    slots = left_ref.shape[0]
    count = masks_ref.shape[1]
    part = count // slots
    me = place_ref[0]
    fill_mask(masks_ref, mask_ref)
    fill_inputs(images_ref, mask_ref, inputs_ref)
    for step in range(slots):
        for pixel in range(PIX):
            base = pl.multiple_of(pixel * count + (me ^ step) * part, part)
            part_ref[pixel * part : (pixel + 1) * part, :] = inputs_ref[pl.ds(base, part), :]
        left_ref[step] = jnp.transpose(matmul(part_ref[...], basis_ref[...])).astype(BF)


def left_second_kernel(hidden_ref, basis_ref, left_ref):
    product = matmul(hidden_ref[...], basis_ref[...])
    for group in range(left_ref.shape[0]):
        left_ref[group] = product[:, group * LANES : (group + 1) * LANES].astype(BF)


def weight_kernel(place_ref, near_refs, far_refs, weight_ref):
    me, side = place_ref[0], place_ref[1]
    depth, half = near_refs[0].shape[1:]
    for refs, at in ((near_refs, side), (far_refs, 1 - side)):
        lanes = pl.ds(pl.multiple_of(at * half, half), half)
        for step, slot_ref in enumerate(refs):
            span = pl.ds(pl.multiple_of((me ^ step) * depth, depth), depth)
            for tap in range(TAPS):
                weight_ref[tap, span, lanes] = slot_ref[tap]


def taps_kernel(turned, sign, big_refs, small_refs, out_ref, left_ref, right_ref):
    rows, width = small_refs[0].shape
    channels = big_refs[0].shape[0]
    part = rows // PIX
    right_ref[...] = jnp.zeros_like(right_ref)
    for slot, (big_ref, small_ref) in enumerate(zip(big_refs, small_refs)):
        base = slot * rows
        left_ref[:, base : base + rows] = big_ref[...]
        for tap, (row_step, col_step) in enumerate(OFFSETS):
            for to_row, from_row, length in runs(sign * row_step, sign * col_step, part):
                right_ref[base + to_row : base + to_row + length, tap * width : (tap + 1) * width] = (
                    small_ref[from_row : from_row + length, :]
                )
    for tap in range(0, TAPS, 2):
        taps = min(2, TAPS - tap)
        product = matmul(left_ref[...], right_ref[:, tap * width : (tap + taps) * width])
        if turned:
            out_ref[tap * width : (tap + taps) * width, :] = jnp.transpose(product).astype(BF)
        else:
            for nth in range(taps):
                out_ref[(tap + nth) * channels : (tap + nth + 1) * channels, :] = product[
                    :, nth * width : (nth + 1) * width
                ].astype(BF)


def scales_kernel(place_ref, coeff_ref, scales_ref, scales_out_ref, ratio_ref):
    half = ratio_ref.shape[1]
    columns = pl.ds(pl.multiple_of(place_ref[1] * half, half), half)
    coeff = coeff_ref[...].astype(F32)
    scales_out_ref[...] = SCALE_DECAY * scales_ref[...] + (1.0 - SCALE_DECAY) * coeff * coeff
    ratio_ref[...] = (
        coeff_ref[:, columns].astype(F32) / (scales_out_ref[:, columns] + DAMPING)
    ).astype(BF)


def middle_second_kernel(basis_ref, slot_refs, out_ref, stack_ref):
    width = basis_ref.shape[0]
    for tap in range(TAPS):
        for step, slot_ref in enumerate(slot_refs):
            stack_ref[step * width : (step + 1) * width, :] = slot_ref[tap * width : (tap + 1) * width, :]
        out_ref[tap * width : (tap + 1) * width, :] = matmul(basis_ref[...], stack_ref[...]).astype(BF)


def add_squares(total, values):
    return total + jnp.sum((values * values).reshape(-1, 8, LANES), axis=0)


def restore_kernel(
    place_ref, basis_in_ref, middle_first_ref, basis_out_ref, near_ref, far_ref, sums_first_ref, sums_second_ref,
    head_ref, first_ref, second_ref, squares_ref, stack_ref, wide_ref,
):
    me, side = place_ref[0], place_ref[1]
    channels = basis_in_ref.shape[0]
    half = near_ref.shape[1]
    wide_ref[:, pl.ds(pl.multiple_of(side * half, half), half)] = near_ref[...]
    wide_ref[:, pl.ds(pl.multiple_of((1 - side) * half, half), half)] = far_ref[...]
    total = jnp.zeros((8, LANES), F32)
    for tap in range(TAPS):
        stack_ref[:, tap * LANES : (tap + 1) * LANES] = middle_first_ref[
            tap * channels : (tap + 1) * channels, :
        ]
    for tap in range(0, TAPS, 2):
        taps = min(2, TAPS - tap)
        product = matmul(basis_in_ref[...], stack_ref[:, tap * LANES : (tap + taps) * LANES])
        for nth in range(taps):
            block = product[:, nth * LANES : (nth + 1) * LANES]
            first_ref[tap + nth] = block.astype(BF)
            total = add_squares(total, block)
    for tap in range(TAPS):
        product = matmul(wide_ref[tap * LANES : (tap + 1) * LANES, :], basis_out_ref[...], NT)
        second_ref[tap] = product.astype(BF)
        for lane in range(0, channels, LANES):
            total = add_squares(total, product[:, lane : lane + LANES])
    groups = sums_first_ref.shape[0] // 2
    row = lax.broadcasted_iota(jnp.int32, (8, LANES), 0)
    mine = (row == me) | (row == me + groups)
    for ref in (sums_first_ref, sums_second_ref):
        total = total + jnp.where(mine, ref[...] * ref[...], 0.0)
    line = lax.broadcasted_iota(jnp.int32, (16, LANES), 0)
    lane = lax.broadcasted_iota(jnp.int32, (16, LANES), 1)
    counted = (line < CLASSES) | ((line == CLASSES) & (lane < CLASSES) & (me == 0))
    head = jnp.where(counted, head_ref[...], 0.0)
    squares_ref[...] = add_squares(total, head)


def update_kernel(
    place_ref, square_refs, weight_refs, mean_refs, square_moment_refs, grad_refs, small_refs,
    weight_outs, mean_outs, square_outs, small_outs, norm_out_ref,
):
    parts = [ref[...] for ref in square_refs]
    while len(parts) > 1:
        parts = [parts[at] + parts[at + 1] for at in range(0, len(parts), 2)]
    total = jnp.sum(jnp.sum(parts[0], axis=1, keepdims=True), axis=0, keepdims=True)
    grad_norm = jnp.sqrt(total)
    factor = CLIP_NORM / jnp.maximum(grad_norm, CLIP_NORM)

    def moments(gradient, mean_old, square_old):
        mean_new = BETA_ONE * mean_old + (1.0 - BETA_ONE) * gradient
        square_new = BETA_TWO * square_old + (1.0 - BETA_TWO) * gradient * gradient
        return mean_new, square_new

    for at in range(len(weight_refs)):
        gradient = grad_refs[at][...].astype(F32) * factor[None]
        mean_new, square_new = moments(gradient, mean_refs[at][...], square_moment_refs[at][...])
        mean_outs[at][...] = mean_new
        square_outs[at][...] = square_new
        step = (mean_new * (1.0 / (1.0 - BETA_ONE**STEP))) / (
            jnp.sqrt(square_new * (1.0 / (1.0 - BETA_TWO**STEP))) + ADAM_EPS
        )
        weight = weight_refs[at][...]
        weight_outs[at][...] = weight - LEARN_RATE * (step + WEIGHT_DECAY * weight)

    @pl.when(pl.program_id(0) == 0)
    def _():
        norm_out_ref[...] = jnp.broadcast_to(grad_norm, norm_out_ref.shape)
        norm_grad, norm_mean, norm_square, head_grad, head_mean, head_square, bias_grad, bias_mean, bias_square = small_refs
        (first_mean, first_square, second_mean, second_square, head_mean_out, head_square_out,
         bias_mean_out, bias_square_out) = small_outs
        mean_new, square_new = moments(norm_grad[...] * factor, norm_mean[...], norm_square[...])
        first_mean[...] = mean_new[0:2, :]
        second_mean[...] = mean_new[2:4, :]
        first_square[...] = square_new[0:2, :]
        second_square[...] = square_new[2:4, :]
        mean_new, square_new = moments(head_grad[...] * factor, head_mean[...], head_square[...])
        head_mean_out[...] = mean_new
        head_square_out[...] = square_new
        mean_new, square_new = moments(bias_grad[...] * factor, bias_mean[...], bias_square[...])
        bias_mean_out[...] = mean_new
        bias_square_out[...] = square_new


def swap(values, axis, step):
    count = lax.axis_size(axis)
    return lax.ppermute(values, axis, [(here, here ^ step) for here in range(count)])


def gathered(values, axis):
    return [values] + [swap(values, axis, step) for step in range(1, lax.axis_size(axis))]


def exchanged(block_of, axis):
    me = lax.axis_index(axis)
    return [block_of(me)] + [
        swap(block_of(me ^ step), axis, step) for step in range(1, lax.axis_size(axis))
    ]


def picked(values, index):
    return lax.dynamic_index_in_dim(values, index, 0, keepdims=False)


def in_order(slots, axis):
    me = lax.axis_index(axis)
    stacked = jnp.stack(slots)
    return jnp.stack([picked(stacked, me ^ place) for place in range(len(slots))])


def every_device(tiles):
    return lax.all_to_all(tiles, EVERY, 0, 0, tiled=True)


def batch_split(partial):
    count_dp, count_cin = lax.axis_size("dp"), lax.axis_size("cin")
    rows, width = partial.shape
    split = partial.reshape(count_cin, rows // count_cin, width)
    slots = exchanged(functools.partial(picked, split), "cin")
    near = sum(slot.astype(F32) for slot in slots).astype(BF)
    split = near.reshape(count_dp, -1, width)
    slots = exchanged(functools.partial(picked, split), "dp")
    return sum(slot.astype(F32) for slot in slots)


def batch_gather(block):
    far = in_order(gathered(block, "dp"), "dp").reshape(-1, block.shape[-1])
    return in_order(gathered(far, "cin"), "cin").reshape(-1, block.shape[-1])


def batch_rows(values):
    count_dp = lax.axis_size("dp")
    place = lax.axis_index("cin") * count_dp + lax.axis_index("dp")
    rows = values.shape[0] // (count_dp * lax.axis_size("cin"))
    return lax.dynamic_slice_in_dim(values, place * rows, rows, 0)


def local(
    images,
    masks,
    labels,
    w_first,
    w_second,
    norm_params,
    head_w,
    head_b,
    bases,
    scales_first,
    scales_second,
    w_first_mean,
    w_first_square,
    w_second_mean,
    w_second_square,
    norm_mean,
    norm_square,
    head_w_mean,
    head_w_square,
    head_b_mean,
    head_b_square,
):
    me = lax.axis_index("cout")
    side = lax.axis_index("cin") % 2
    place = jnp.stack([me, side]).astype(jnp.int32)
    sizes = tuple(lax.axis_size(name) for name in EVERY)
    groups = sizes[1]
    devices = sizes[0] * sizes[1] * sizes[2]
    channels = w_first.shape[1]
    width = w_first.shape[2]
    half = channels // 2
    count = images.shape[1]
    part = count // groups
    rows = PIX * part
    tile = shape((devices, 8, LANES), F32)
    wide = (rows, channels)
    basis_in_first, basis_out_first = bases[0, 0], bases[0, 1]
    basis_in_second, basis_out_second = bases[1, 0], bases[1, 1]

    piece = lax.dynamic_slice_in_dim(w_second, side * half, half, 2).astype(BF)
    near_weights = gathered(piece, "cout")
    head_rows = jnp.concatenate([head_w.T, jnp.zeros((16 - CLASSES, width), F32)], axis=0)
    head_full = lax.all_gather(head_rows, "cout")
    own_labels = lax.dynamic_slice_in_dim(labels, me * part, part, 0)[:, None]
    bias_row = jnp.pad(head_b, (0, LANES - CLASSES))[None]

    flat_images = images.reshape(PIX * count, channels)
    first_low, stats, mask = call(
        functools.partial(first_kernel, groups),
        [shape((groups, rows, width), BF), tile, shape((rows, LANES), F32)],
        [place, flat_images, masks, w_first, norm_params],
        [
            pltpu.VMEM((PIX * count, LANES), F32),
            pltpu.VMEM((PIX * count, channels), BF),
            pltpu.VMEM((channels, TAPS * width), BF),
            pltpu.VMEM((PIX * count, width), F32),
        ],
        flops=2 * PIX * count * channels * width * TAPS,
    )
    first_slots = exchanged(functools.partial(picked, first_low), "cout")
    got = every_device(stats)
    other_mask = swap(mask, "cin", 1)
    hidden, first_out, norm_first = call(
        lambda place_ref, *refs: first_norm_kernel(sizes, place_ref, refs[:groups], *refs[groups:]),
        [shape(wide, BF), shape(wide, BF), shape((8, channels), F32)],
        [place, *first_slots, got, mask],
    )
    other_hidden = swap(hidden, "cin", 1)
    mine, theirs, stats = call(
        lambda p, a, b, c, d, e, *refs: second_kernel(
            p, a, b, c, d, e, refs[:groups], *refs[groups:]
        ),
        [shape((rows, half), F32), shape((rows, half), F32), tile],
        [place, hidden, other_hidden, mask, other_mask, norm_params, *near_weights],
        [
            pltpu.VMEM((2 * rows, channels), BF),
            pltpu.VMEM((channels, TAPS * half), BF),
            pltpu.VMEM((2 * rows, half), F32),
        ],
        flops=4 * rows * channels * half * TAPS,
    )
    from_other = swap(theirs, "cin", 1)
    got = every_device(stats)
    second_out, norm_second, dz_second, sums, head_blocks = call(
        functools.partial(head_kernel, sizes),
        [
            shape(wide, F32),
            shape((8, channels), F32),
            shape(wide, F32),
            tile,
            shape((groups, 16, width), F32),
        ],
        [place, mine, from_other, got, norm_first, mask, head_full, bias_row, own_labels],
        [
            pltpu.VMEM(wide, F32),
            pltpu.VMEM((part, channels), F32),
            pltpu.VMEM((LANES, channels), F32),
        ],
    )
    got = every_device(sums)
    grad_second, right_turned, sums_second = call(
        second_back_kernel,
        [shape(wide, BF), shape((channels, rows), BF), shape((8, LANES), F32)],
        [dz_second, second_out, norm_second, got, mask, basis_out_second],
        scalars=0,
    )
    far_weights = [swap(slot, "cin", 1) for slot in near_weights]
    (weight_full,) = call(
        lambda p, *refs: weight_kernel(p, refs[:groups], refs[groups : 2 * groups], refs[-1]),
        [shape((TAPS, channels, channels), BF)],
        [place, *near_weights, *far_weights],
    )
    dz_first, sums = call(
        conv_back_kernel,
        [shape(wide, F32), tile],
        [grad_second, weight_full, first_out, norm_first, mask],
        [pltpu.VMEM(wide, F32)],
        flops=2 * rows * channels * channels * TAPS,
        scalars=0,
    )
    right_slots = gathered(right_turned, "cout")
    (left_blocks,) = call(
        left_second_kernel,
        [shape((groups, rows, width), BF)],
        [hidden, basis_in_second],
        scalars=0,
    )
    left_slots = exchanged(functools.partial(picked, left_blocks), "cout")
    (left_turned,) = call(
        left_first_kernel,
        [shape((groups, channels, rows), BF)],
        [place, flat_images, masks, basis_in_first],
        [
            pltpu.VMEM((PIX * count, LANES), F32),
            pltpu.VMEM((PIX * count, channels), BF),
            pltpu.VMEM((rows, channels), BF),
        ],
    )
    got = every_device(sums)
    right_blocks, sums_first = call(
        first_back_kernel,
        [shape((groups, rows, width), BF), shape((8, LANES), F32)],
        [dz_first, first_out, norm_first, got, mask, basis_out_first],
        [pltpu.VMEM(wide, BF)],
        scalars=0,
    )

    def products(turned, sign, big, small):
        (out,) = call(
            lambda *refs: taps_kernel(turned, sign, refs[:groups], refs[groups : 2 * groups], *refs[2 * groups :]),
            [shape((TAPS * width, channels) if turned else (TAPS * channels, width), BF)],
            [*big, *small],
            [
                pltpu.VMEM((channels, groups * rows), BF),
                pltpu.VMEM((groups * rows, TAPS * width), BF),
            ],
            flops=2 * groups * rows * channels * width * TAPS,
            scalars=0,
        )
        return out

    coeff_own = batch_split(products(True, 1, right_slots, left_slots)).astype(BF)
    coeff_second = batch_gather(coeff_own)
    flat_scales = scales_second.reshape(TAPS * width, channels)
    scales_second_new, ratio = call(
        scales_kernel,
        [shape(flat_scales.shape, F32), shape((TAPS * width, half), BF)],
        [place, coeff_second, flat_scales],
    )
    ratio_slots = gathered(ratio, "cout")
    basis_rows = lax.dynamic_slice_in_dim(basis_in_second, me * width, width, 0)

    def in_slots(values):
        return jnp.concatenate(
            [lax.dynamic_slice_in_dim(values, (me ^ step) * width, width, 1) for step in range(groups)], 1
        )

    (near_middle,) = call(
        lambda basis_ref, *refs: middle_second_kernel(basis_ref, refs[:groups], *refs[groups:]),
        [shape((TAPS * width, half), BF)],
        [in_slots(basis_rows), *ratio_slots],
        [pltpu.VMEM((channels, half), BF)],
        scalars=0,
    )
    far_middle = swap(near_middle, "cin", 1)

    right_parts = exchanged(functools.partial(picked, right_blocks), "cout")
    left_parts = [left_turned[step] for step in range(groups)]
    own = batch_split(products(False, -1, left_parts, right_parts))
    flat_scales = scales_first.reshape(TAPS * channels, width)
    scales_own = SCALE_DECAY * batch_rows(flat_scales) + (1.0 - SCALE_DECAY) * own * own
    ratio = jnp.concatenate(gathered((own / (scales_own + DAMPING)).astype(BF), "cout"), axis=1)
    basis_rows = lax.dynamic_slice_in_dim(basis_out_first, me * width, width, 0)
    middle = matmul(ratio, in_slots(basis_rows), NT).astype(BF)
    middle_first = batch_gather(middle)
    coeff_first = batch_gather(own.astype(BF)).astype(F32)
    scales_first_new = SCALE_DECAY * flat_scales + (1.0 - SCALE_DECAY) * coeff_first * coeff_first

    sent = jnp.broadcast_to(head_blocks[None, :, None], sizes + head_blocks.shape[1:])
    head_sums = jnp.sum(every_device(sent.reshape((devices,) + head_blocks.shape[1:])), axis=0)
    head_w_grad = head_sums[:CLASSES].T
    head_b_grad = head_sums[CLASSES : CLASSES + 1, :CLASSES]
    loss_total = head_sums[CLASSES, CLASSES]
    norm_grad = jnp.stack(
        [picked(total, at) for total in (sums_first, sums_second) for at in (me, groups + me)]
    )

    first_grad, second_grad, squares = call(
        restore_kernel,
        [shape((TAPS, channels, width), BF), shape((TAPS, width, channels), BF), shape((8, LANES), F32)],
        [
            place,
            basis_in_first,
            middle_first,
            basis_out_second,
            near_middle,
            far_middle,
            sums_first,
            sums_second,
            head_sums,
        ],
        [pltpu.VMEM((channels, TAPS * width), BF), pltpu.VMEM((TAPS * width, channels), BF)],
        flops=4 * TAPS * channels * channels * width,
    )
    square_slots = gathered(squares, "cout")

    smalls = [
        norm_grad, norm_mean, norm_square, head_w_grad, head_w_mean, head_w_square,
        head_b_grad, head_b_mean[None], head_b_square[None],
    ]
    small_outs = [shape((2, width), F32)] * 4 + [shape(head_w.shape, F32)] * 2 + [shape((1, CLASSES), F32)] * 2
    first_spec = pl.BlockSpec((1, channels, width), lambda tap: (tap, 0, 0))
    second_spec = pl.BlockSpec((1, width, channels), lambda tap: (tap, 0, 0))
    pair = [first_spec, second_spec]
    first_like, second_like = shape(w_first.shape, F32), shape(w_second.shape, F32)

    def whole(leaf):
        return pl.BlockSpec(leaf.shape, lambda tap: (0,) * len(leaf.shape))

    def update(*refs):
        at = [0]

        def take(number):
            at[0] += number
            return refs[at[0] - number : at[0]]

        update_kernel(
            None, take(groups), take(2), take(2), take(2), take(2), take(len(smalls)),
            take(2), take(2), take(2), take(len(small_outs)), take(1)[0],
        )

    results = pl.pallas_call(
        update,
        grid=(TAPS,),
        in_specs=[whole(leaf) for leaf in square_slots] + pair * 4 + [whole(leaf) for leaf in smalls],
        out_specs=pair * 3 + [whole(leaf) for leaf in small_outs] + [whole(shape((8, LANES), F32))],
        out_shape=[first_like, second_like] * 3 + small_outs + [shape((8, LANES), F32)],
        compiler_params=pltpu.CompilerParams(vmem_limit_bytes=VMEM_BYTES),
    )(
        *square_slots, w_first, w_second, w_first_mean, w_second_mean, w_first_square, w_second_square,
        first_grad, second_grad, *smalls,
    )
    (first_new, second_new, first_mean_new, second_mean_new, first_square_new, second_square_new,
     norm_first_mean, norm_first_square, norm_second_mean, norm_second_square,
     head_mean_new, head_square_new, bias_mean_new, bias_square_new, norm_tile) = results
    return (
        loss_total,
        norm_tile[0, 0],
        first_new,
        first_mean_new,
        first_square_new,
        second_new,
        second_mean_new,
        second_square_new,
        norm_first_mean,
        norm_first_square,
        norm_second_mean,
        norm_second_square,
        head_mean_new,
        head_square_new,
        bias_mean_new[0],
        bias_square_new[0],
        scales_first_new.reshape(scales_first.shape),
        scales_second_new.reshape(scales_second.shape),
    )


def solution(mesh):
    return jax.shard_map(
        local,
        mesh=mesh,
        in_specs=(
            P(None, ("dp", "cin"), None),
            P(None, ("dp", "cin")),
            P(("dp", "cin")),
            P(None, None, "cout"),
            P(None, "cout", None),
            P(None, "cout"),
            P("cout", None),
            P(),
            P(),
            P(None, None, "cout"),
            P(None, "cout", None),
            P(None, None, "cout"),
            P(None, None, "cout"),
            P(None, "cout", None),
            P(None, "cout", None),
            P(None, "cout"),
            P(None, "cout"),
            P("cout", None),
            P("cout", None),
            P(),
            P(),
        ),
        out_specs=(
            P(),
            P(),
            P(None, None, "cout"),
            P(None, None, "cout"),
            P(None, None, "cout"),
            P(None, "cout", None),
            P(None, "cout", None),
            P(None, "cout", None),
            P(None, "cout"),
            P(None, "cout"),
            P(None, "cout"),
            P(None, "cout"),
            P("cout", None),
            P("cout", None),
            P(),
            P(),
            P(None, None, "cout"),
            P(None, "cout", None),
        ),
        check_vma=False,
    )
```

```python
import functools
import math

import jax
import jax.numpy as jnp
from jax import lax
from jax.experimental import pallas as pl
from jax.experimental.pallas import tpu as pltpu
from jax.sharding import PartitionSpec as P

CLASSES = 10
SIDE = 4
PIX = 16
TAPS = 9
STEP = 10
LANES = 128

EPS_NORM = 1e-05
SCALE_DECAY = 0.95
DAMPING = 0.001
CLIP_NORM = 1.0
LEARN_RATE = 0.01
BETA_ONE = 0.9
BETA_TWO = 0.999
ADAM_EPS = 1e-08
WEIGHT_DECAY = 0.01
SMOOTH = 0.1
OFFSETS = [(row_step, col_step) for row_step in (-1, 0, 1) for col_step in (-1, 0, 1)]
EVERY = ("dp", "cout", "cin")
BF = jnp.bfloat16
F32 = jnp.float32
PRECISE = lax.Precision.HIGHEST
NN = (((1,), (0,)), ((), ()))
NT = (((1,), (1,)), ((), ()))
TN = (((0,), (0,)), ((), ()))


def matmul(left, right, dims=NN, precision=None):
    return lax.dot_general(
        left, right, dims, precision=precision, preferred_element_type=F32
    )


def runs(row_step, col_step, count):
    low, high = max(0, -col_step), min(SIDE, SIDE - col_step)
    found = []
    for row in range(max(0, -row_step), min(SIDE, SIDE - row_step)):
        to_row = (row * SIDE + low) * count
        from_row = ((row + row_step) * SIDE + low + col_step) * count
        length = (high - low) * count
        if found and found[-1][0] + found[-1][2] == to_row and found[-1][1] + found[-1][2] == from_row:
            found[-1] = (found[-1][0], found[-1][1], found[-1][2] + length)
        else:
            found.append((to_row, from_row, length))
    return found


class Late:
    def __init__(self, ref, copy):
        self.ref, self.copy, self.shape = ref, copy, ref.shape
        copy.start()

    def settle(self):
        if self.copy is not None:
            self.copy.wait()
        self.copy = None

    def __getitem__(self, index):
        self.settle()
        return self.ref[index]


class Result:
    def __init__(self, ref, copy):
        self.ref, self.copy, self.shape, self.sent = ref, copy, ref.shape, False

    def __getitem__(self, index):
        return self.ref[index]

    def __setitem__(self, index, values):
        self.ref[index] = values

    def send(self):
        if not self.sent:
            self.copy.start()
        self.sent = True


def call(kernel, outs, args, scratch=(), scalars=1, near=(), raw=(), near_out=(), flops=0, room=60):
    n_in, n_out = len(args), len(outs)
    copied = [at for at in range(scalars, n_in) if at not in near and at not in raw]
    copied_out = [at for at in range(n_out) if at not in near_out]

    def body(*refs):
        ins, results = list(refs[:n_in]), list(refs[n_in : n_in + n_out])
        rest = refs[n_in + n_out :]
        held, held_out = rest[: len(copied)], rest[len(copied) : len(copied) + len(copied_out)]
        own, arrived = rest[len(copied) + len(copied_out) : -1], rest[-1]
        for nth, at in enumerate(copied):
            ins[at] = Late(held[nth], pltpu.make_async_copy(ins[at], held[nth], arrived.at[nth]))
        for nth, at in enumerate(copied_out):
            copy = pltpu.make_async_copy(held_out[nth], results[at], arrived.at[len(copied) + nth])
            results[at] = Result(held_out[nth], copy)
        kernel(*ins, *results, *own)
        for at in copied:
            ins[at].settle()
        for at in copied_out:
            results[at].send()
        for at in copied_out:
            results[at].copy.wait()

    specs = [pl.BlockSpec(memory_space=pltpu.SMEM)] * scalars
    specs += [
        pl.BlockSpec(memory_space=pltpu.VMEM if at in near else pltpu.HBM) for at in range(scalars, n_in)
    ]
    moved = sum(math.prod(a.shape) * a.dtype.itemsize for a in list(args) + list(outs))
    return pl.pallas_call(
        body,
        out_shape=list(outs),
        in_specs=specs,
        out_specs=[
            pl.BlockSpec(memory_space=pltpu.VMEM if at in near_out else pltpu.HBM) for at in range(n_out)
        ],
        scratch_shapes=[pltpu.VMEM(args[at].shape, args[at].dtype) for at in copied]
        + [pltpu.VMEM(outs[at].shape, outs[at].dtype) for at in copied_out]
        + list(scratch)
        + [pltpu.SemaphoreType.DMA((max(1, len(copied) + len(copied_out)),))],
        compiler_params=pltpu.CompilerParams(vmem_limit_bytes=room * 1024 * 1024),
        cost_estimate=pl.CostEstimate(flops=flops, bytes_accessed=moved, transcendentals=0),
    )(*args)


def shape(dims, dtype):
    return jax.ShapeDtypeStruct(dims, dtype)


def gelu_parts(values):
    rate = math.sqrt(2.0 / math.pi)
    bend = jnp.tanh(rate * (values + 0.044715 * values * values * values))
    share = 0.5 * (1.0 + bend)
    slope = share + 0.5 * values * (1.0 - bend * bend) * rate * (1.0 + 0.134145 * values * values)
    return values * share, slope


def fill_mask(masks_ref, mask_ref):
    count = masks_ref.shape[1]
    same = lax.broadcasted_iota(jnp.int32, (count, count), 0) == lax.broadcasted_iota(
        jnp.int32, (count, count), 1
    )
    for pixel in range(PIX):
        row = masks_ref[pixel : pixel + 1, :].astype(F32)
        column = jnp.sum(jnp.where(same, row, 0.0), axis=1, keepdims=True)
        mask_ref[pixel * count : (pixel + 1) * count, :] = jnp.broadcast_to(column, (count, LANES))


def fill_inputs(images_ref, mask_ref, inputs_ref):
    low = mask_ref[...].astype(BF)
    for lane in range(0, images_ref.shape[1], LANES):
        inputs_ref[:, lane : lane + LANES] = images_ref[:, lane : lane + LANES] * low


def first_kernel(
    groups, place_ref, images_ref, masks_ref, weight_ref, params_ref, head_ref,
    send_refs, stats_ref, own_mask_ref, mask_ref, inputs_ref, low_ref, sum_ref, wide_ref, arrived,
):
    count = masks_ref.shape[1]
    part = count // groups
    me = place_ref[0]
    copies = [
        pltpu.make_async_copy(weight_ref.at[at : at + 3], wide_ref.at[at : at + 3], arrived.at[at // 3])
        for at in range(0, TAPS, 3)
    ]
    for copy in copies:
        copy.start()
    fill_mask(masks_ref, mask_ref)
    fill_inputs(images_ref, mask_ref, inputs_ref)
    for tap in range(TAPS):
        if tap % 3 == 0:
            copies[tap // 3].wait()
        low_ref[:, tap * LANES : (tap + 1) * LANES] = wide_ref[tap].astype(BF)
    sum_ref[...] = jnp.zeros_like(sum_ref)
    for tap in range(0, TAPS, 2):
        taps = min(2, TAPS - tap)
        product = matmul(inputs_ref[...], low_ref[:, tap * LANES : (tap + taps) * LANES])
        for nth in range(taps):
            for to_row, from_row, length in runs(*OFFSETS[tap + nth], count):
                sum_ref[to_row : to_row + length, :] += product[
                    from_row : from_row + length, nth * LANES : (nth + 1) * LANES
                ]
    mask = mask_ref[...]
    total = sum_ref[...]
    masked = total * mask
    tile = jnp.concatenate(
        [
            jnp.sum(masked, axis=0, keepdims=True),
            jnp.sum(masked * total, axis=0, keepdims=True),
            jnp.sum(mask, axis=0, keepdims=True),
            params_ref[0:2, :],
            jnp.zeros((3, LANES), F32),
        ],
        axis=0,
    )
    stats_ref[...] = jnp.broadcast_to(tile[None], stats_ref.shape)
    head = jnp.concatenate([head_ref[...], jnp.zeros((16 - CLASSES, LANES), F32)], axis=0).astype(BF)
    for step, send_ref in enumerate(send_refs):
        send_ref[PIX * part : PIX * part + 16, :] = head
        for pixel in range(PIX):
            base = pl.multiple_of(pixel * count + (me ^ step) * part, part)
            send_ref[pixel * part : (pixel + 1) * part, :] = sum_ref[pl.ds(base, part), :].astype(BF)
    for pixel in range(PIX):
        own = pl.multiple_of(pixel * count + me * part, part)
        own_mask_ref[pixel * part : (pixel + 1) * part, :] = mask_ref[pl.ds(own, part), :]


def first_norm_kernel(sizes, place_ref, slot_refs, got_ref, mask_ref, hidden_ref, first_ref, norm_ref, head_ref):
    rows = mask_ref.shape[0]
    count_dp, groups, count_cin = sizes
    me = place_ref[0]
    tiles = []
    for group in range(groups):
        total = None
        for far in range(count_dp):
            for near in range(count_cin):
                tile = got_ref[(far * groups + group) * count_cin + near]
                total = tile if total is None else total + tile
        tiles.append((total, got_ref[group * count_cin]))
    kept = tiles[0][0][2:3, :]
    for group, (total, single) in enumerate(tiles):
        lanes = slice(group * LANES, (group + 1) * LANES)
        mean = total[0:1, :] / kept
        norm_ref[0:1, lanes] = mean
        norm_ref[1:2, lanes] = lax.rsqrt(total[1:2, :] / kept - mean * mean + EPS_NORM)
        norm_ref[2:4, lanes] = single[3:5, :]
        norm_ref[4:5, lanes] = kept
        norm_ref[5:8, lanes] = jnp.zeros((3, LANES), F32)
    for step, slot_ref in enumerate(slot_refs):
        lanes = pl.ds(pl.multiple_of((me ^ step) * LANES, LANES), LANES)
        head_ref[:, lanes] = slot_ref[rows : rows + 16, :]
        low = slot_ref[0:rows, :]
        scaled = (low.astype(F32) - norm_ref[0:1, lanes]) * norm_ref[1:2, lanes]
        value, _ = gelu_parts(norm_ref[2:3, lanes] * scaled + norm_ref[3:4, lanes])
        hidden_ref[:, lanes] = (value * mask_ref[...]).astype(BF)
        first_ref[:, lanes] = low


def second_kernel(
    place_ref, own_ref, other_ref, own_mask_ref, other_mask_ref, params_ref, basis_ref, slot_refs,
    mine_ref, theirs_ref, stats_ref, left_refs, wide_ref, inputs_ref, weight_ref, sum_ref, arrived,
):
    me = place_ref[0]
    rows = own_ref.shape[0]
    part = rows // PIX
    depth, half = slot_refs[0].shape[1:]
    copies = []
    for step, slot_ref in enumerate(slot_refs):
        span = pl.ds(pl.multiple_of((me ^ step) * depth, depth), depth)
        copies.append(pltpu.make_async_copy(slot_ref, weight_ref.at[:, span, :], arrived.at[step]))
        copies[-1].start()
    inputs_ref[0:rows, :] = own_ref[...]
    wide_ref[...] = matmul(own_ref[...], basis_ref[...])
    send_columns(me, wide_ref, left_refs)
    for left_ref in left_refs:
        left_ref.send()
    inputs_ref[rows : 2 * rows, :] = other_ref[...]
    sum_ref[...] = jnp.zeros_like(sum_ref)
    for copy in copies:
        copy.wait()
    for tap in range(TAPS):
        product = matmul(inputs_ref[...], weight_ref[tap])
        for to_row, from_row, length in runs(*OFFSETS[tap], part):
            for base in (0, rows):
                sum_ref[base + to_row : base + to_row + length, :] += product[
                    base + from_row : base + from_row + length, :
                ]
    mine_ref[...] = sum_ref[0:rows, :]
    theirs_ref[...] = sum_ref[rows : 2 * rows, :]
    lines = [[], []]
    for lane in range(0, half, LANES):
        first = square = None
        for base, mask_ref in ((0, own_mask_ref), (rows, other_mask_ref)):
            total = sum_ref[base : base + rows, lane : lane + LANES]
            masked = total * mask_ref[...]
            first_part = jnp.sum(masked, axis=0, keepdims=True)
            square_part = jnp.sum(masked * total, axis=0, keepdims=True)
            first = first_part if first is None else first + first_part
            square = square_part if square is None else square + square_part
        lines[0].append(first)
        lines[1].append(square)
    spare = 8 - 2 * (half // LANES) - 2
    tile = jnp.concatenate(
        lines[0] + lines[1] + [params_ref[2:4, :], jnp.zeros((spare, LANES), F32)], axis=0
    )
    stats_ref[...] = jnp.broadcast_to(tile[None], stats_ref.shape)


def head_kernel(
    sizes, place_ref, mine_ref, got_ref_rows, got_ref, norm_first_ref, mask_ref, head_ref, bias_ref, labels_ref,
    wide_ref, norm_ref, dz_ref, sums_ref, head_out_ref, slope_ref, pooled_ref, weight_ref,
):
    count_dp, groups, count_cin = sizes
    side = place_ref[1]
    rows, half = mine_ref.shape
    part = rows // PIX
    blocks = half // LANES
    wide_ref[:, pl.ds(pl.multiple_of(side * half, half), half)] = mine_ref[...]
    wide_ref[:, pl.ds(pl.multiple_of((1 - side) * half, half), half)] = got_ref_rows[...]
    totals = [None, None]
    for source in range(count_dp * groups * count_cin):
        which = source % count_cin % 2
        tile = got_ref[source]
        totals[which] = tile if totals[which] is None else totals[which] + tile
    kept = norm_first_ref[4:5, 0:LANES]
    mask = mask_ref[...]
    for group in range(groups):
        lanes = slice(group * LANES, (group + 1) * LANES)
        total, line = totals[group // blocks], group % blocks
        mean = total[line : line + 1, :] / kept
        rstd = lax.rsqrt(total[blocks + line : blocks + line + 1, :] / kept - mean * mean + EPS_NORM)
        single = got_ref[group * count_cin]
        gain = single[2 * blocks : 2 * blocks + 1, :]
        shift = single[2 * blocks + 1 : 2 * blocks + 2, :]
        norm_ref[0:1, lanes] = mean
        norm_ref[1:2, lanes] = rstd
        norm_ref[2:3, lanes] = gain
        norm_ref[3:4, lanes] = shift
        norm_ref[4:8, lanes] = jnp.broadcast_to(kept, (4, LANES))
        value, slope = gelu_parts(gain * ((wide_ref[:, lanes] - mean) * rstd) + shift)
        slope_ref[:, lanes] = slope * mask * (1.0 / PIX)
        pooled_ref[:, lanes] = jnp.sum((value * mask).reshape(PIX, part, LANES), axis=0) * (1.0 / PIX)
    wide_ref.send()
    norm_ref.send()
    weight_ref[0:16, :] = head_ref[...]
    weight_ref[16:LANES, :] = jnp.zeros((LANES - 16, weight_ref.shape[1]), BF)
    pooled = pooled_ref[...].astype(BF)
    head = weight_ref[...]
    class_index = lax.broadcasted_iota(jnp.int32, (part, LANES), 1)
    logits = matmul(pooled, head, NT) + bias_ref[...]
    logits = jnp.where(class_index < CLASSES, logits, -1e30)
    logits = logits - jnp.max(logits, axis=1, keepdims=True)
    log_probs = logits - jnp.log(jnp.sum(jnp.exp(logits), axis=1, keepdims=True))
    wanted = jnp.where(class_index == labels_ref[...], 1.0 - SMOOTH, 0.0) + SMOOTH / CLASSES
    wanted = jnp.where(class_index < CLASSES, wanted, 0.0)
    loss = -jnp.sum(jnp.sum(wanted * log_probs, axis=1, keepdims=True), axis=0, keepdims=True)
    logit_grad = jnp.exp(log_probs) - wanted
    head_grad = matmul(logit_grad, pooled.astype(F32), TN, PRECISE)
    pooled_grad = matmul(logit_grad, head.astype(F32), NN, PRECISE)
    extra = jnp.sum(logit_grad, axis=0, keepdims=True)
    extra = jnp.where(class_index[0:1, :] == CLASSES, loss, extra)
    line = lax.broadcasted_iota(jnp.int32, (16, LANES), 0)
    gains, shifts = [], []
    for group in range(groups):
        lanes = slice(group * LANES, (group + 1) * LANES)
        head_out_ref[group] = jnp.where(line == CLASSES, extra, head_grad[0:16, lanes])
        spread = jnp.broadcast_to(pooled_grad[:, lanes][None], (PIX, part, LANES)).reshape(rows, LANES)
        dz = slope_ref[:, lanes] * spread
        dz_ref[:, lanes] = dz
        scaled = (wide_ref[:, lanes] - norm_ref[0:1, lanes]) * norm_ref[1:2, lanes]
        gains.append(jnp.sum(dz * scaled, axis=0, keepdims=True))
        shifts.append(jnp.sum(dz, axis=0, keepdims=True))
    sums_ref[...] = jnp.broadcast_to(jnp.concatenate(gains + shifts, axis=0)[None], sums_ref.shape)


def total_of(got_ref):
    total = got_ref[0]
    for source in range(1, got_ref.shape[0]):
        total = total + got_ref[source]
    return total


def norm_back(values, dz, norm, mask, gain_grad, shift_grad):
    scaled = (values - norm[0:1, :]) * norm[1:2, :]
    gain = norm[2:3, :]
    return norm[1:2, :] * (
        gain * dz - mask * (gain / norm[4:5, :]) * (shift_grad + scaled * gain_grad)
    )


def second_back_kernel(
    place_ref, dz_ref, wide_ref, norm_ref, got_ref, mask_ref, basis_ref, first_ref, norm_first_ref, head_ref, near_refs, far_refs,
    right_ref, sums_out_ref, dz_first_ref, sums_ref, grad_ref, weight_ref, sum_ref, arrived,
):
    me, side = place_ref[0], place_ref[1]
    depth, half = near_refs[0].shape[1:]
    copies = []
    for refs, at in ((near_refs, side), (far_refs, 1 - side)):
        lanes = pl.ds(pl.multiple_of(at * half, half), half)
        for step, slot_ref in enumerate(refs):
            span = pl.ds(pl.multiple_of((me ^ step) * depth, depth), depth)
            copies.append(
                pltpu.make_async_copy(slot_ref, weight_ref.at[:, span, lanes], arrived.at[len(copies)])
            )
            copies[-1].start()
    total = total_of(got_ref)
    sums_out_ref[...] = total
    groups = total.shape[0] // 2
    mask = mask_ref[...]
    for group in range(groups):
        lanes = slice(group * LANES, (group + 1) * LANES)
        grad_ref[:, lanes] = norm_back(
            wide_ref[:, lanes], dz_ref[:, lanes], norm_ref[:, lanes], mask,
            total[group : group + 1, :], total[groups + group : groups + group + 1, :],
        ).astype(BF)
    right_ref[...] = jnp.transpose(matmul(grad_ref[...], basis_ref[...])).astype(BF)
    right_ref.send()
    sums_out_ref.send()
    for copy in copies:
        copy.wait()
    rows, channels = grad_ref.shape
    part = rows // PIX
    sum_ref[...] = jnp.zeros_like(sum_ref)
    for tap in range(TAPS):
        product = matmul(grad_ref[...], weight_ref[tap], NT)
        row_step, col_step = OFFSETS[tap]
        for to_row, from_row, length in runs(-row_step, -col_step, part):
            sum_ref[to_row : to_row + length, :] += product[from_row : from_row + length, :]
    gains, shifts = [], []
    for lane in range(0, channels, LANES):
        lanes = slice(lane, lane + LANES)
        norm = norm_first_ref[:, lanes]
        scaled = (first_ref[:, lanes].astype(F32) - norm[0:1, :]) * norm[1:2, :]
        _, slope = gelu_parts(norm[2:3, :] * scaled + norm[3:4, :])
        dz = slope * mask * sum_ref[:, lanes]
        dz_first_ref[:, lanes] = dz
        gains.append(jnp.sum(dz * scaled, axis=0, keepdims=True))
        shifts.append(jnp.sum(dz, axis=0, keepdims=True))
    dz_first_ref.send()
    count_dp, _, count_cin = sums_ref.shape[:3]
    for group in range(groups):
        tile = jnp.concatenate(gains + shifts + [head_ref[group], jnp.zeros((8, LANES), F32)], axis=0)
        tile = tile.astype(BF)
        for far in range(count_dp):
            for near in range(count_cin):
                sums_ref[far, group, near] = tile


def first_back_kernel(
    place_ref, dz_ref, first_ref, norm_ref, got_ref, mask_ref, basis_ref, old_refs,
    send_refs, sums_ref, small_ref, grad_ref, product_ref,
):
    whole = got_ref[0].astype(F32)
    for source in range(1, got_ref.shape[0]):
        whole = whole + got_ref[source].astype(F32)
    total = whole[0:8, :]
    sums_ref[...] = total
    small_ref[...] = jnp.zeros(small_ref.shape, F32)
    small_ref[8:24, :] = whole[8:24, :]
    for at, row in enumerate((24, 28, 32, 48, 64, 65)):
        rows, lanes = old_refs[at].shape
        small_ref[row : row + rows, 0:lanes] = old_refs[at][...]
    groups = total.shape[0] // 2
    for group in range(groups):
        lanes = slice(group * LANES, (group + 1) * LANES)
        grad_ref[:, lanes] = norm_back(
            first_ref[:, lanes].astype(F32), dz_ref[:, lanes], norm_ref[:, lanes], mask_ref[...],
            total[group : group + 1, :], total[groups + group : groups + group + 1, :],
        ).astype(BF)
    product_ref[...] = matmul(grad_ref[...], basis_ref[...])
    send_columns(place_ref[0], product_ref, send_refs)


def send_columns(me, product_ref, send_refs):
    for step, send_ref in enumerate(send_refs):
        lanes = pl.ds(pl.multiple_of((me ^ step) * LANES, LANES), LANES)
        send_ref[...] = product_ref[:, lanes].astype(BF)


def left_first_kernel(place_ref, images_ref, masks_ref, basis_ref, left_ref, mask_ref, inputs_ref, part_ref):
    slots = left_ref.shape[0]
    count = masks_ref.shape[1]
    part = count // slots
    me = place_ref[0]
    fill_mask(masks_ref, mask_ref)
    fill_inputs(images_ref, mask_ref, inputs_ref)
    for step in range(slots):
        for pixel in range(PIX):
            base = pl.multiple_of(pixel * count + (me ^ step) * part, part)
            part_ref[pixel * part : (pixel + 1) * part, :] = inputs_ref[pl.ds(base, part), :]
        left_ref[step] = jnp.transpose(matmul(part_ref[...], basis_ref[...])).astype(BF)


def taps_kernel(sign, big_refs, small_refs, out_ref, left_ref, right_ref):
    rows, width = small_refs[0].shape
    channels = big_refs[0].shape[0]
    part = rows // PIX
    right_ref[...] = jnp.zeros_like(right_ref)
    for slot, (big_ref, small_ref) in enumerate(zip(big_refs, small_refs)):
        base = slot * rows
        left_ref[:, base : base + rows] = big_ref[...]
        for tap, (row_step, col_step) in enumerate(OFFSETS):
            for to_row, from_row, length in runs(sign * row_step, sign * col_step, part):
                right_ref[base + to_row : base + to_row + length, tap * width : (tap + 1) * width] = (
                    small_ref[from_row : from_row + length, :]
                )
    for tap in range(0, TAPS, 2):
        taps = min(2, TAPS - tap)
        product = matmul(left_ref[...], right_ref[:, tap * width : (tap + taps) * width])
        for nth in range(taps):
            out_ref[(tap + nth) * channels : (tap + nth + 1) * channels, :] = product[
                :, nth * width : (nth + 1) * width
            ].astype(BF)


def ratio_kernel(own_refs, scales_ref, coeff_ref, ratio_ref):
    coeff = None
    for ref in own_refs:
        coeff = ref[...].astype(F32) if coeff is None else coeff + ref[...].astype(F32)
    scales = SCALE_DECAY * scales_ref[...] + (1.0 - SCALE_DECAY) * coeff * coeff
    coeff_ref[...] = coeff.astype(BF)
    ratio_ref[...] = (coeff / (scales + DAMPING)).astype(BF)


def middle_kernel(basis_ref, slot_refs, out_ref):
    width = slot_refs[0].shape[1]
    ratio = jnp.concatenate([ref[...] for ref in slot_refs], axis=1)
    out_ref[...] = matmul(ratio, basis_ref[...], NT).astype(BF)


def scales_kernel(turned, coeff_ref, scales_ref, out_ref):
    taps = out_ref.shape[0]
    rows = coeff_ref.shape[0] // taps
    for tap in range(taps):
        coeff = coeff_ref[tap * rows : (tap + 1) * rows, :].astype(F32)
        if turned:
            coeff = jnp.transpose(coeff)
        out_ref[tap] = SCALE_DECAY * scales_ref[tap] + (1.0 - SCALE_DECAY) * coeff * coeff


def add_squares(total, values):
    return total + jnp.sum((values * values).reshape(-1, 8, LANES), axis=0)


def restore_kernel(
    place_ref, basis_in_ref, middle_first_ref, basis_out_ref, middle_second_ref, sums_first_ref, sums_second_ref,
    old_ref, first_ref, second_ref, squares_ref, small_ref, stack_ref,
):
    me = place_ref[0]
    channels = basis_in_ref.shape[0]
    total = jnp.zeros((8, LANES), F32)
    for tap in range(TAPS):
        product = matmul(
            middle_second_ref[tap * channels : (tap + 1) * channels, :], basis_out_ref[...], (((0,), (1,)), ((), ()))
        )
        second_ref[tap] = product.astype(BF)
        for lane in range(0, channels, LANES):
            total = add_squares(total, product[:, lane : lane + LANES])
    for tap in range(TAPS):
        stack_ref[:, tap * LANES : (tap + 1) * LANES] = middle_first_ref[
            tap * channels : (tap + 1) * channels, :
        ]
    for tap in range(0, TAPS, 2):
        taps = min(2, TAPS - tap)
        product = matmul(basis_in_ref[...], stack_ref[:, tap * LANES : (tap + taps) * LANES])
        for nth in range(taps):
            block = product[:, nth * LANES : (nth + 1) * LANES]
            first_ref[tap + nth] = block.astype(BF)
            total = add_squares(total, block)
    groups = sums_first_ref.shape[0] // 2
    row = lax.broadcasted_iota(jnp.int32, (8, LANES), 0)
    mine = (row == me) | (row == me + groups)
    for ref in (sums_first_ref, sums_second_ref):
        total = total + jnp.where(mine, ref[...] * ref[...], 0.0)
    line = lax.broadcasted_iota(jnp.int32, (16, LANES), 0)
    lane = lax.broadcasted_iota(jnp.int32, (16, LANES), 1)
    counted = (line < CLASSES) | ((line == CLASSES) & (lane < CLASSES) & (me == 0))
    head = jnp.where(counted, old_ref[8:24, :], 0.0)
    small_ref[...] = old_ref[...]
    for at, ref in enumerate((sums_first_ref, sums_second_ref)):
        small_ref[2 * at : 2 * at + 1, :] = ref[pl.ds(me, 1), :]
        small_ref[2 * at + 1 : 2 * at + 2, :] = ref[pl.ds(me + groups, 1), :]
    squares_ref[...] = add_squares(total, head)


def update_kernel(
    square_refs, weight_refs, mean_refs, square_moment_refs, grad_refs, small_refs,
    weight_outs, mean_outs, square_outs, small_outs, scalar_outs,
):
    parts = [ref[...] for ref in square_refs]
    while len(parts) > 1:
        parts = [parts[at] + parts[at + 1] for at in range(0, len(parts), 2)]
    total = jnp.sum(jnp.sum(parts[0], axis=1, keepdims=True), axis=0, keepdims=True)
    grad_norm = jnp.sqrt(total)
    factor = CLIP_NORM / jnp.maximum(grad_norm, CLIP_NORM)

    def moments(gradient, mean_old, square_old):
        mean_new = BETA_ONE * mean_old + (1.0 - BETA_ONE) * gradient
        square_new = BETA_TWO * square_old + (1.0 - BETA_TWO) * gradient * gradient
        return mean_new, square_new

    taps = mean_outs[0].shape[0]
    for at in range(len(weight_refs)):
        for nth in range(taps):
            tap = pl.program_id(0) * taps + nth
            gradient = grad_refs[at][tap].astype(F32) * factor
            mean_new, square_new = moments(gradient, mean_refs[at][tap], square_moment_refs[at][tap])
            mean_outs[at][nth] = mean_new
            square_outs[at][nth] = square_new
            square_hat = square_new * (1.0 / (1.0 - BETA_TWO**STEP))
            size = square_hat * lax.rsqrt(square_hat) + ADAM_EPS
            step = mean_new * (LEARN_RATE / (1.0 - BETA_ONE**STEP)) * pl.reciprocal(size, approx=True)
            weight_outs[at][nth] = weight_refs[at][tap] * (1.0 - LEARN_RATE * WEIGHT_DECAY) - step

    @pl.when(pl.program_id(0) == 0)
    def _():
        norm_out, loss_out = scalar_outs
        norm_out[...] = grad_norm
        (small,) = small_refs
        loss_out[...] = small[8 + CLASSES : 9 + CLASSES, CLASSES : CLASSES + 1]
        results = moments(small[0:4, :] * factor, small[24:28, :], small[28:32, :])
        for at in range(2):
            small_outs[at][...] = results[at][0:2, :]
            small_outs[2 + at][...] = results[at][2:4, :]
        results = moments(
            small[8 : 8 + CLASSES, :] * factor, small[32 : 32 + CLASSES, :], small[48 : 48 + CLASSES, :]
        )
        for at in range(2):
            small_outs[4 + at][...] = results[at]
        lanes = slice(0, CLASSES)
        results = moments(small[8 + CLASSES : 9 + CLASSES, lanes] * factor, small[64:65, lanes], small[65:66, lanes])
        for at in range(2):
            small_outs[6 + at][...] = results[at]


def swap(values, axis, step):
    count = lax.axis_size(axis)
    return lax.ppermute(values, axis, [(here, here ^ step) for here in range(count)])


def gathered(values, axis):
    return [values] + [swap(values, axis, step) for step in range(1, lax.axis_size(axis))]


def exchanged(sends, axis):
    return [sends[0]] + [swap(sends[step], axis, step) for step in range(1, len(sends))]


def picked(values, index):
    return lax.dynamic_index_in_dim(values, index, 0, keepdims=False)


def after(values, *others):
    return lax.optimization_barrier((values,) + others)[0]


def tree_sum(slots):
    while len(slots) > 1:
        slots = [slots[at] + slots[at + 1] for at in range(0, len(slots), 2)]
    return slots[0]


def every_device(tiles):
    return lax.all_to_all(tiles, EVERY, 0, 0, tiled=True)


def bits_of(axis):
    return range(lax.axis_size(axis).bit_length() - 1)


def halved(values, axis, bit):
    own = (lax.axis_index(axis) >> bit) & 1
    values = values.reshape(2, -1, values.shape[-1])
    return [picked(values, own), swap(picked(values, 1 - own), axis, 1 << bit)]


def doubled(values, axis, bit):
    own = (lax.axis_index(axis) >> bit) & 1
    other = swap(values, axis, 1 << bit)
    first = jnp.where(own == 0, values, other)
    return jnp.concatenate([first, jnp.where(own == 0, other, values)], axis=0)


def joined(terms):
    return terms[0] if len(terms) == 1 else (terms[0].astype(F32) + terms[1].astype(F32)).astype(BF)


def batch_gather(block, axes=("dp", "cin"), first=()):
    for order in reversed(first):
        block = doubled(block, *order)
    for axis in axes:
        for bit in reversed(bits_of(axis)):
            block = doubled(block, axis, bit)
    return block


def batch_rows(values):
    place = jnp.int32(0)
    for axis in ("cin", "dp"):
        for bit in bits_of(axis):
            place = place * 2 + ((lax.axis_index(axis) >> bit) & 1)
    rows = values.shape[0] // (lax.axis_size("dp") * lax.axis_size("cin"))
    return lax.dynamic_slice_in_dim(values, place * rows, rows, 0)


def local(
    images,
    masks,
    labels,
    w_first,
    w_second,
    norm_params,
    head_w,
    head_b,
    bases,
    scales_first,
    scales_second,
    w_first_mean,
    w_first_square,
    w_second_mean,
    w_second_square,
    norm_mean,
    norm_square,
    head_w_mean,
    head_w_square,
    head_b_mean,
    head_b_square,
):
    me = lax.axis_index("cout")
    side = lax.axis_index("cin") % 2
    place = jnp.stack([me, side]).astype(jnp.int32)
    sizes = tuple(lax.axis_size(name) for name in EVERY)
    groups = sizes[1]
    devices = sizes[0] * sizes[1] * sizes[2]
    channels = w_first.shape[1]
    width = w_first.shape[2]
    half = channels // 2
    count = images.shape[1]
    part = count // groups
    rows = PIX * part
    tile = shape((devices, 8, LANES), F32)
    wide = (rows, channels)
    basis_in_first, basis_out_first = bases[0, 0], bases[0, 1]
    basis_in_second, basis_out_second = bases[1, 0], bases[1, 1]
    bases_all = (basis_in_first, basis_out_first, basis_in_second, basis_out_second)

    piece = lax.dynamic_slice_in_dim(w_second, side * half, half, 2).astype(BF)
    own_labels = lax.dynamic_slice_in_dim(labels, me * part, part, 0)[:, None]
    bias_row = jnp.pad(head_b, (0, LANES - CLASSES))[None]

    flat_images = images.reshape(PIX * count, channels)
    sends = [shape((rows + 16, width), BF)] * groups
    *first_sends, stats, mask = call(
        lambda *refs: first_kernel(groups, *refs[:6], refs[6 : 6 + groups], *refs[6 + groups :]),
        sends + [tile, shape((rows, LANES), F32)],
        [place, flat_images, masks, w_first, norm_params, head_w.T],
        [
            pltpu.VMEM((PIX * count, LANES), F32),
            pltpu.VMEM((PIX * count, channels), BF),
            pltpu.VMEM((channels, TAPS * width), BF),
            pltpu.VMEM((PIX * count, width), F32),
            pltpu.VMEM((TAPS, channels, width), F32),
            pltpu.SemaphoreType.DMA((3,)),
        ],
        near=(1, 2, 4, 5),
        raw=(3,),
        room=56,
        flops=2 * PIX * count * channels * width * TAPS,
    )
    first_slots = exchanged(first_sends, "cout")
    got = every_device(after(stats, *first_slots))
    (left_turned,) = call(
        left_first_kernel,
        [shape((groups, channels, rows), BF)],
        [place, after(flat_images, stats), masks, basis_in_first],
        [
            pltpu.VMEM((PIX * count, LANES), F32),
            pltpu.VMEM((PIX * count, channels), BF),
            pltpu.VMEM((rows, channels), BF),
        ],
        near=(1, 2, 3),
        room=20,
    )
    near_weights = [piece]
    for step in range(1, groups):
        ready = piece if step < groups - 1 else after(piece, *first_slots)
        near_weights.append(swap(ready, "cout", step))
    other_mask = swap(mask, "cin", 1)
    first_mask = after(mask, left_turned, *near_weights[1:-1], *bases_all)
    hidden, first_out, norm_first, head_full = call(
        lambda place_ref, *refs: first_norm_kernel(sizes, place_ref, refs[:groups], *refs[groups:]),
        [shape(wide, BF), shape(wide, BF), shape((8, channels), F32), shape((16, channels), BF)],
        [place, *first_slots, got, first_mask],
        near_out=(0,),
    )
    other_hidden = swap(hidden, "cin", 1)
    mine, theirs, stats, *left_sends = call(
        lambda *refs: second_kernel(
            *refs[:7], refs[7 : 7 + groups], *refs[7 + groups : 10 + groups],
            refs[10 + groups : 10 + 2 * groups], *refs[10 + 2 * groups :],
        ),
        [shape((rows, half), F32), shape((rows, half), F32), tile] + [shape((rows, width), BF)] * groups,
        [place, hidden, other_hidden, mask, other_mask, norm_params, basis_in_second, *near_weights],
        [
            pltpu.VMEM(wide, F32),
            pltpu.VMEM((2 * rows, channels), BF),
            pltpu.VMEM((TAPS, channels, half), BF),
            pltpu.VMEM((2 * rows, half), F32),
            pltpu.SemaphoreType.DMA((groups,)),
        ],
        near=(1, 2),
        raw=tuple(range(7, 7 + groups)),
        flops=4 * rows * channels * half * TAPS,
    )
    from_other = swap(theirs, "cin", 1)
    got = every_device(stats)
    far_weights = [swap(after(slot, mine), "cin", 1) for slot in near_weights]
    left_slots = exchanged(left_sends, "cout")
    head_mask = after(mask, *far_weights)
    second_out, norm_second, dz_second, sums, head_blocks = call(
        functools.partial(head_kernel, sizes),
        [
            shape(wide, F32),
            shape((8, channels), F32),
            shape(wide, F32),
            tile,
            shape((groups, 16, width), F32),
        ],
        [place, mine, from_other, got, norm_first, head_mask, head_full, bias_row, own_labels],
        [
            pltpu.VMEM(wide, F32),
            pltpu.VMEM((part, channels), F32),
            pltpu.VMEM((LANES, channels), BF),
        ],
    )
    got = every_device(sums)
    right_turned, sums_second, dz_first, sums = call(
        lambda *refs: second_back_kernel(
            *refs[:10], refs[10 : 10 + groups], refs[10 + groups : 10 + 2 * groups], *refs[10 + 2 * groups :]
        ),
        [shape((channels, rows), BF), shape((8, LANES), F32), shape(wide, F32), shape(sizes + (32, LANES), BF)],
        [
            place, dz_second, second_out, norm_second, got, after(mask, *left_slots), basis_out_second, first_out, norm_first, head_blocks,
            *near_weights, *far_weights,
        ],
        [
            pltpu.VMEM(wide, BF),
            pltpu.VMEM((TAPS, channels, channels), BF),
            pltpu.VMEM(wide, F32),
            pltpu.SemaphoreType.DMA((2 * groups,)),
        ],
        raw=tuple(range(10, 10 + 2 * groups)),
        flops=2 * rows * channels * channels * TAPS,
    )
    right_slots = gathered(right_turned, "cout")
    def products(sign, big, small, near=()):
        (out,) = call(
            lambda *refs: taps_kernel(sign, refs[:groups], refs[groups : 2 * groups], *refs[2 * groups :]),
            [shape((TAPS * channels, width), BF)],
            [*big, *small],
            [
                pltpu.VMEM((channels, groups * rows), BF),
                pltpu.VMEM((groups * rows, TAPS * width), BF),
            ],
            scalars=0,
            near=near,
            near_out=(0,),
            room=56,
            flops=2 * groups * rows * channels * width * TAPS,
        )
        return out

    got = every_device(sums.reshape(devices, 32, LANES))
    orders = [(axis, bit) for axis in ("cin", "dp") for bit in bits_of(axis)]
    small_old = [norm_mean, norm_square, head_w_mean.T, head_w_square.T, head_b_mean[None], head_b_square[None]]
    *right_sends, sums_first, smalls = call(
        lambda *refs: first_back_kernel(*refs[:7], refs[7:13], refs[13 : 13 + groups], *refs[13 + groups :]),
        [shape((rows, width), BF)] * groups + [shape((8, LANES), F32), shape((72, LANES), F32)],
        [place, dz_first, first_out, norm_first, got, after(mask, *right_slots), basis_out_first, *small_old],
        [pltpu.VMEM(wide, BF), pltpu.VMEM(wide, F32)],
        near_out=tuple(range(groups)),
    )

    def hold(*values):
        def copy_in(*refs):
            arrived = refs[-1]
            copies = [
                pltpu.make_async_copy(refs[at], refs[len(values) + at], arrived.at[at])
                for at in range(len(values))
            ]
            for copy in copies:
                copy.start()
            for copy in copies:
                copy.wait()

        return call(
            lambda *refs: copy_in(*refs),
            [shape(value.shape, value.dtype) for value in values],
            values,
            [pltpu.SemaphoreType.DMA((len(values),))],
            scalars=0,
            raw=tuple(range(len(values))),
            near_out=tuple(range(len(values))),
            room=16,
        )

    def ratio_of(terms, scales_own):
        chunk = shape(scales_own.shape, BF)
        return call(
            lambda *refs: ratio_kernel(refs[: len(terms)], *refs[len(terms) :]),
            [chunk, chunk],
            [*terms, scales_own],
            scalars=0,
            near=tuple(range(len(terms) + 1)),
            near_out=(0, 1),
            room=16,
        )

    def middle_of(ratio, basis):
        slots = gathered(ratio, "cout")
        (out,) = call(
            lambda basis_ref, *refs: middle_kernel(basis_ref, refs[:groups], refs[-1]),
            [shape(ratio.shape, BF)],
            [basis, *slots],
            scalars=0,
            near=tuple(range(groups + 1)),
            near_out=(0,),
            room=16,
        )
        return out

    near_steps = len(bits_of("cin"))
    right_parts = exchanged(right_sends, "cout")
    left_parts = [left_turned[step] for step in range(groups)]
    products_first = products(-1, left_parts, right_parts, tuple(range(groups, 2 * groups)))
    terms_first = [products_first]
    for order in orders[:near_steps]:
        terms_first = halved(joined(terms_first), *order)
    near_first = joined(terms_first)
    products_second = products(1, [after(right_slots[0], near_first)] + right_slots[1:], left_slots)
    terms_first, terms_second = [near_first], [products_second]
    for order in orders[:near_steps]:
        terms_second = halved(joined(terms_second), *order)
    for order in orders[near_steps:-1]:
        terms_first = halved(joined(terms_first), *order)
        terms_second = halved(after(joined(terms_second), *terms_first), *order)
    filler = terms_first[1]
    terms_first = halved(joined(terms_first), *orders[-1])

    def in_slots(values):
        return jnp.concatenate(
            [lax.dynamic_slice_in_dim(values, (me ^ step) * width, width, 1) for step in range(groups)], 1
        )

    def basis_rows(basis):
        return in_slots(lax.dynamic_slice_in_dim(basis, me * width, width, 0))

    scales_turned = batch_rows(
        jnp.swapaxes(after(scales_second, filler), 1, 2).reshape(TAPS * channels, width)
    )
    scales_chunk = batch_rows(after(scales_first, filler).reshape(TAPS * channels, width))
    rows_first = basis_rows(after(basis_out_first, filler))
    rows_second = basis_rows(after(basis_in_second, filler))
    weights = hold(after(w_first, filler), w_second)
    own_first, ratio_first = ratio_of(terms_first, after(scales_chunk, *weights, *terms_second))
    means = hold(after(w_first_mean, own_first), w_second_mean)
    terms_second = halved(after(joined(terms_second), own_first), *orders[-1])
    own_second, ratio_second = ratio_of(terms_second, after(scales_turned, *means))
    coeff_first = doubled(own_first, *orders[-1])
    middle_first = middle_of(ratio_first, after(rows_first, own_second))
    gathered_first = doubled(middle_first, *orders[-1])
    middle_second = middle_of(ratio_second, after(rows_second, coeff_first, gathered_first))
    squares_old = hold(after(w_first_square, middle_second), w_second_square)
    gathered_second = doubled(middle_second, *orders[-1])
    coeff_second = own_second
    for order in reversed(orders[near_steps:-1]):
        gathered_first = doubled(gathered_first, *order)
        gathered_second = doubled(after(gathered_second, gathered_first), *order)
    gathered_first = batch_gather(gathered_first, ("cin",))
    gathered_second = batch_gather(gathered_second, ("cin",))
    coeff_first = batch_gather(coeff_first, ("cin",), orders[near_steps:-1])
    coeff_second = batch_gather(coeff_second)

    def scales_of(turned, coeff, scales):
        spec = pl.BlockSpec((3,) + scales.shape[1:], lambda tap: (tap, 0, 0))
        return pl.pallas_call(
            functools.partial(scales_kernel, turned),
            grid=(TAPS // 3,),
            in_specs=[pl.BlockSpec((3 * channels, width), lambda tap: (tap, 0)), spec],
            out_specs=spec,
            out_shape=shape(scales.shape, F32),
            compiler_params=pltpu.CompilerParams(vmem_limit_bytes=12 * 1024 * 1024),
        )(coeff, scales)

    scales_second_new = scales_of(True, coeff_second, scales_second)
    scales_first_new = scales_of(False, coeff_first, scales_first)

    first_grad, second_grad, squares, small_grads = call(
        restore_kernel,
        [shape((TAPS, channels, width), BF), shape((TAPS, width, channels), BF), shape((8, LANES), F32), shape((72, LANES), F32)],
        [
            place,
            basis_in_first,
            after(gathered_first, coeff_first),
            basis_out_second,
            gathered_second,
            sums_first,
            sums_second,
            smalls,
        ],
        [pltpu.VMEM((channels, TAPS * width), BF)],
        near=tuple(range(1, 8)),
        near_out=(0, 1, 2, 3),
        room=16,
        flops=4 * TAPS * channels * channels * width,
    )
    square_slots = gathered(squares, "cout")
    square_slots[0] = after(square_slots[0], coeff_second)

    smalls = [small_grads]
    small_outs = [shape((2, width), F32)] * 4 + [shape((CLASSES, width), F32)] * 2 + [shape((1, CLASSES), F32)] * 2
    small_outs += [shape((1, 1), F32)] * 2
    first_spec = pl.BlockSpec((1, channels, width), lambda tap: (tap, 0, 0))
    second_spec = pl.BlockSpec((1, width, channels), lambda tap: (tap, 0, 0))
    pair = [first_spec, second_spec]
    first_like, second_like = shape(w_first.shape, F32), shape(w_second.shape, F32)

    def whole(leaf):
        return pl.BlockSpec(leaf.shape, lambda tap: (0,) * len(leaf.shape))

    def update(*refs):
        at = [0]

        def take(number):
            at[0] += number
            return refs[at[0] - number : at[0]]

        update_kernel(
            take(groups), take(2), take(2), take(2), take(2), take(len(smalls)),
            take(2), take(2), take(2), take(len(small_outs) - 2), take(2),
        )

    results = pl.pallas_call(
        update,
        grid=(TAPS,),
        in_specs=[pl.BlockSpec(memory_space=pltpu.VMEM)] * (groups + 8 + len(smalls)),
        out_specs=pair * 3 + [whole(leaf) for leaf in small_outs],
        out_shape=[first_like, second_like] * 3 + small_outs,
        compiler_params=pltpu.CompilerParams(vmem_limit_bytes=16 * 1024 * 1024),
    )(
        *square_slots, *weights, *means, *squares_old,
        first_grad, second_grad, *smalls,
    )
    (first_new, second_new, first_mean_new, second_mean_new, first_square_new, second_square_new,
     norm_first_mean, norm_first_square, norm_second_mean, norm_second_square,
     head_mean_new, head_square_new, bias_mean_new, bias_square_new, grad_norm, loss_total) = results
    return (
        loss_total.reshape(()),
        grad_norm.reshape(()),
        first_new,
        first_mean_new,
        first_square_new,
        second_new,
        second_mean_new,
        second_square_new,
        norm_first_mean,
        norm_first_square,
        norm_second_mean,
        norm_second_square,
        head_mean_new.T,
        head_square_new.T,
        bias_mean_new[0],
        bias_square_new[0],
        scales_first_new,
        scales_second_new,
    )


def solution(mesh):
    return jax.shard_map(
        local,
        mesh=mesh,
        in_specs=(
            P(None, ("dp", "cin"), None),
            P(None, ("dp", "cin")),
            P(("dp", "cin")),
            P(None, None, "cout"),
            P(None, "cout", None),
            P(None, "cout"),
            P("cout", None),
            P(),
            P(),
            P(None, None, "cout"),
            P(None, "cout", None),
            P(None, None, "cout"),
            P(None, None, "cout"),
            P(None, "cout", None),
            P(None, "cout", None),
            P(None, "cout"),
            P(None, "cout"),
            P("cout", None),
            P("cout", None),
            P(),
            P(),
        ),
        out_specs=(
            P(),
            P(),
            P(None, None, "cout"),
            P(None, None, "cout"),
            P(None, None, "cout"),
            P(None, "cout", None),
            P(None, "cout", None),
            P(None, "cout", None),
            P(None, "cout"),
            P(None, "cout"),
            P(None, "cout"),
            P(None, "cout"),
            P("cout", None),
            P("cout", None),
            P(),
            P(),
            P(None, None, "cout"),
            P(None, "cout", None),
        ),
        check_vma=False,
    )
```

```python
import functools
import math

import jax
import jax.numpy as jnp
from jax import lax
from jax.experimental import pallas as pl
from jax.experimental.pallas import tpu as pltpu
from jax.sharding import PartitionSpec as P

CLASSES = 10
SIDE = 4
PIX = 16
TAPS = 9
STEP = 10
LANES = 128

EPS_NORM = 1e-05
SCALE_DECAY = 0.95
DAMPING = 0.001
CLIP_NORM = 1.0
LEARN_RATE = 0.01
BETA_ONE = 0.9
BETA_TWO = 0.999
ADAM_EPS = 1e-08
WEIGHT_DECAY = 0.01
SMOOTH = 0.1
OFFSETS = [(row_step, col_step) for row_step in (-1, 0, 1) for col_step in (-1, 0, 1)]
EVERY = ("dp", "cout", "cin")
BF = jnp.bfloat16
F32 = jnp.float32
PRECISE = lax.Precision.HIGHEST
NN = (((1,), (0,)), ((), ()))
NT = (((1,), (1,)), ((), ()))
TN = (((0,), (0,)), ((), ()))


def matmul(left, right, dims=NN, precision=None):
    return lax.dot_general(
        left, right, dims, precision=precision, preferred_element_type=F32
    )


def runs(row_step, col_step, count):
    low, high = max(0, -col_step), min(SIDE, SIDE - col_step)
    found = []
    for row in range(max(0, -row_step), min(SIDE, SIDE - row_step)):
        to_row = (row * SIDE + low) * count
        from_row = ((row + row_step) * SIDE + low + col_step) * count
        length = (high - low) * count
        if found and found[-1][0] + found[-1][2] == to_row and found[-1][1] + found[-1][2] == from_row:
            found[-1] = (found[-1][0], found[-1][1], found[-1][2] + length)
        else:
            found.append((to_row, from_row, length))
    return found


class Late:
    def __init__(self, ref, copy):
        self.ref, self.copy, self.shape = ref, copy, ref.shape
        copy.start()

    def settle(self):
        if self.copy is not None:
            self.copy.wait()
        self.copy = None

    def __getitem__(self, index):
        self.settle()
        return self.ref[index]


class Result:
    def __init__(self, ref, copy):
        self.ref, self.copy, self.shape, self.sent = ref, copy, ref.shape, False

    def __getitem__(self, index):
        return self.ref[index]

    def __setitem__(self, index, values):
        self.ref[index] = values

    def send(self):
        if not self.sent:
            self.copy.start()
        self.sent = True


def call(kernel, outs, args, scratch=(), scalars=1, near=(), raw=(), near_out=(), flops=0, room=60):
    n_in, n_out = len(args), len(outs)
    copied = [at for at in range(scalars, n_in) if at not in near and at not in raw]
    copied_out = [at for at in range(n_out) if at not in near_out]

    def body(*refs):
        ins, results = list(refs[:n_in]), list(refs[n_in : n_in + n_out])
        rest = refs[n_in + n_out :]
        held, held_out = rest[: len(copied)], rest[len(copied) : len(copied) + len(copied_out)]
        own, arrived = rest[len(copied) + len(copied_out) : -1], rest[-1]
        for nth, at in enumerate(copied):
            ins[at] = Late(held[nth], pltpu.make_async_copy(ins[at], held[nth], arrived.at[nth]))
        for nth, at in enumerate(copied_out):
            copy = pltpu.make_async_copy(held_out[nth], results[at], arrived.at[len(copied) + nth])
            results[at] = Result(held_out[nth], copy)
        kernel(*ins, *results, *own)
        for at in copied:
            ins[at].settle()
        for at in copied_out:
            results[at].send()
        for at in copied_out:
            results[at].copy.wait()

    specs = [pl.BlockSpec(memory_space=pltpu.SMEM)] * scalars
    specs += [
        pl.BlockSpec(memory_space=pltpu.VMEM if at in near else pltpu.HBM) for at in range(scalars, n_in)
    ]
    moved = sum(math.prod(a.shape) * a.dtype.itemsize for a in list(args) + list(outs))
    return pl.pallas_call(
        body,
        out_shape=list(outs),
        in_specs=specs,
        out_specs=[
            pl.BlockSpec(memory_space=pltpu.VMEM if at in near_out else pltpu.HBM) for at in range(n_out)
        ],
        scratch_shapes=[pltpu.VMEM(args[at].shape, args[at].dtype) for at in copied]
        + [pltpu.VMEM(outs[at].shape, outs[at].dtype) for at in copied_out]
        + list(scratch)
        + [pltpu.SemaphoreType.DMA((max(1, len(copied) + len(copied_out)),))],
        compiler_params=pltpu.CompilerParams(vmem_limit_bytes=room * 1024 * 1024),
        cost_estimate=pl.CostEstimate(flops=flops, bytes_accessed=moved, transcendentals=0),
    )(*args)


def shape(dims, dtype):
    return jax.ShapeDtypeStruct(dims, dtype)


def gelu_parts(values):
    rate = math.sqrt(2.0 / math.pi)
    bend = jnp.tanh(rate * (values + 0.044715 * values * values * values))
    share = 0.5 * (1.0 + bend)
    slope = share + 0.5 * values * (1.0 - bend * bend) * rate * (1.0 + 0.134145 * values * values)
    return values * share, slope


def fill_mask(masks_ref, mask_ref):
    count = masks_ref.shape[1]
    same = lax.broadcasted_iota(jnp.int32, (count, count), 0) == lax.broadcasted_iota(
        jnp.int32, (count, count), 1
    )
    for pixel in range(PIX):
        row = masks_ref[pixel : pixel + 1, :].astype(F32)
        column = jnp.sum(jnp.where(same, row, 0.0), axis=1, keepdims=True)
        mask_ref[pixel * count : (pixel + 1) * count, :] = jnp.broadcast_to(column, (count, LANES))


def fill_inputs(images_ref, mask_ref, inputs_ref):
    low = mask_ref[...].astype(BF)
    for lane in range(0, images_ref.shape[1], LANES):
        inputs_ref[:, lane : lane + LANES] = images_ref[:, lane : lane + LANES] * low


def first_kernel(
    groups, place_ref, images_ref, masks_ref, weight_ref,
    sum_ref, all_mask_ref, stats_ref, own_mask_ref, mask_ref, inputs_ref, low_ref, wide_ref, arrived,
):
    count = masks_ref.shape[1]
    part = count // groups
    me = place_ref[0]
    copies = [
        pltpu.make_async_copy(weight_ref.at[at : at + 3], wide_ref.at[at : at + 3], arrived.at[at // 3])
        for at in range(0, TAPS, 3)
    ]
    for copy in copies:
        copy.start()
    fill_mask(masks_ref, mask_ref)
    fill_inputs(images_ref, mask_ref, inputs_ref)
    all_mask_ref[...] = mask_ref[...].astype(BF)
    all_mask_ref.send()
    for pixel in range(PIX):
        own = pl.multiple_of(pixel * count + me * part, part)
        own_mask_ref[pixel * part : (pixel + 1) * part, :] = mask_ref[pl.ds(own, part), :]
    own_mask_ref.send()
    for tap in range(TAPS):
        if tap % 3 == 0:
            copies[tap // 3].wait()
        low_ref[:, tap * LANES : (tap + 1) * LANES] = wide_ref[tap].astype(BF)
    sum_ref[...] = jnp.zeros(sum_ref.shape, F32)
    for tap in range(0, TAPS, 2):
        taps = min(2, TAPS - tap)
        product = matmul(inputs_ref[...], low_ref[:, tap * LANES : (tap + taps) * LANES])
        for nth in range(taps):
            for to_row, from_row, length in runs(*OFFSETS[tap + nth], count):
                sum_ref[to_row : to_row + length, :] += product[
                    from_row : from_row + length, nth * LANES : (nth + 1) * LANES
                ]
    sum_ref.send()
    mask = mask_ref[...]
    total = sum_ref[...]
    masked = total * mask
    tile = jnp.concatenate(
        [
            jnp.sum(masked, axis=0, keepdims=True),
            jnp.sum(masked * total, axis=0, keepdims=True),
            jnp.sum(mask, axis=0, keepdims=True),
            jnp.zeros((5, LANES), F32),
        ],
        axis=0,
    )
    stats_ref[...] = jnp.broadcast_to(tile[None], stats_ref.shape)


def first_norm_kernel(
    place_ref, got_ref, first_ref, mask_ref, params_ref, head_ref, send_refs, kept_ref, hidden_ref, scaled_ref
):
    total = total_of(got_ref)
    kept = total[2:3, :]
    mean = total[0:1, :] / kept
    rstd = lax.rsqrt(total[1:2, :] / kept - mean * mean + EPS_NORM)
    kept_ref[...] = jnp.broadcast_to(kept, kept_ref.shape)
    gain, shift = params_ref[0:1, :], params_ref[1:2, :]
    count = first_ref.shape[0] // PIX
    part = count // len(send_refs)
    scaled = (first_ref[...] - mean) * rstd
    value, _ = gelu_parts(gain * scaled + shift)
    hidden_ref[...] = (value * mask_ref[...].astype(F32)).astype(BF)
    scaled_ref[...] = scaled.astype(BF)
    lines = [head_ref[...]]
    for line in (rstd, gain, shift):
        high = line.astype(BF).astype(F32)
        lines += [high, line - high]
    extra = jnp.concatenate(lines, axis=0).astype(BF)
    rows = PIX * part
    for step, send_ref in enumerate(send_refs):
        for pixel in range(PIX):
            base = pl.ds(pl.multiple_of(pixel * count + (place_ref[0] ^ step) * part, part), part)
            send_ref[pixel * part : (pixel + 1) * part, :] = hidden_ref[base, :]
            send_ref[rows + pixel * part : rows + (pixel + 1) * part, :] = scaled_ref[base, :]
        send_ref[2 * rows : 2 * rows + 16, :] = extra


def hidden_kernel(place_ref, slot_refs, mask_ref, hidden_ref):
    rows = hidden_ref.shape[0]
    for step, slot_ref in enumerate(slot_refs):
        lanes = pl.ds(pl.multiple_of((place_ref[0] ^ step) * LANES, LANES), LANES)
        hidden_ref[:, lanes] = slot_ref[0:rows, :]
    hidden_ref[:, len(slot_refs) * LANES :] = mask_ref[...].astype(BF)


def gather_kernel(place_ref, slot_refs, kept_ref, scaled_ref, norm_ref, head_ref):
    rows = scaled_ref.shape[0]
    norm_ref[0:1, :] = jnp.zeros((1, norm_ref.shape[1]), F32)
    norm_ref[5:8, :] = jnp.zeros((3, norm_ref.shape[1]), F32)
    for step, slot_ref in enumerate(slot_refs):
        lanes = pl.ds(pl.multiple_of((place_ref[0] ^ step) * LANES, LANES), LANES)
        scaled_ref[:, lanes] = slot_ref[rows : 2 * rows, :]
        extra = slot_ref[2 * rows : 2 * rows + 16, :].astype(F32)
        line = lax.broadcasted_iota(jnp.int32, (16, LANES), 0)
        head_ref[:, lanes] = jnp.where(line < CLASSES, extra, 0.0).astype(BF)
        for at in range(3):
            norm_ref[at + 1 : at + 2, lanes] = (
                extra[CLASSES + 2 * at : CLASSES + 2 * at + 1, :] + extra[CLASSES + 2 * at + 1 : CLASSES + 2 * at + 2, :]
            )
        norm_ref[4:5, lanes] = kept_ref[0:1, :]


def second_kernel(
    place_ref, own_ref, other_ref, params_ref, slot_refs,
    mine_ref, theirs_ref, stats_ref, inputs_ref, weight_ref, sum_ref, arrived,
):
    me = place_ref[0]
    rows = own_ref.shape[0]
    part = rows // PIX
    depth, half = slot_refs[0].shape[1:]
    copies = []
    for step, slot_ref in enumerate(slot_refs):
        span = pl.ds(pl.multiple_of((me ^ step) * depth, depth), depth)
        copies.append(pltpu.make_async_copy(slot_ref, weight_ref.at[:, span, :], arrived.at[step]))
        copies[-1].start()
    channels = inputs_ref.shape[1]
    inputs_ref[0:rows, :] = own_ref[:, 0:channels]
    inputs_ref[rows : 2 * rows, :] = other_ref[:, 0:channels]
    sum_ref[...] = jnp.zeros_like(sum_ref)
    for copy in copies:
        copy.wait()
    for tap in range(TAPS):
        product = matmul(inputs_ref[...], weight_ref[tap])
        for to_row, from_row, length in runs(*OFFSETS[tap], part):
            for base in (0, rows):
                sum_ref[base + to_row : base + to_row + length, :] += product[
                    base + from_row : base + from_row + length, :
                ]
    mine_ref[...] = sum_ref[0:rows, :]
    theirs_ref[...] = sum_ref[rows : 2 * rows, :]
    lines = [[], []]
    for lane in range(0, half, LANES):
        first = square = None
        for base, ref in ((0, own_ref), (rows, other_ref)):
            total = sum_ref[base : base + rows, lane : lane + LANES]
            masked = total * ref[:, channels : channels + LANES].astype(F32)
            first_part = jnp.sum(masked, axis=0, keepdims=True)
            square_part = jnp.sum(masked * total, axis=0, keepdims=True)
            first = first_part if first is None else first + first_part
            square = square_part if square is None else square + square_part
        lines[0].append(first)
        lines[1].append(square)
    spare = 8 - 2 * (half // LANES) - 2
    tile = jnp.concatenate(
        lines[0] + lines[1] + [params_ref[2:4, :], jnp.zeros((spare, LANES), F32)], axis=0
    )
    stats_ref[...] = jnp.broadcast_to(tile[None], stats_ref.shape)


def head_kernel(
    sizes, place_ref, mine_ref, got_ref_rows, got_ref, norm_first_ref, mask_ref, head_ref, bias_ref, labels_ref,
    wide_ref, norm_ref, dz_ref, sums_ref, head_out_ref, slope_ref, pooled_ref, weight_ref,
):
    count_dp, groups, count_cin = sizes
    side = place_ref[1]
    rows, half = mine_ref.shape
    part = rows // PIX
    blocks = half // LANES
    wide_ref[:, pl.ds(pl.multiple_of(side * half, half), half)] = mine_ref[...]
    wide_ref[:, pl.ds(pl.multiple_of((1 - side) * half, half), half)] = got_ref_rows[...]
    totals = [None, None]
    for source in range(count_dp * groups * count_cin):
        which = source % count_cin % 2
        tile = got_ref[source]
        totals[which] = tile if totals[which] is None else totals[which] + tile
    kept = norm_first_ref[4:5, 0:LANES]
    mask = mask_ref[...]
    for group in range(groups):
        lanes = slice(group * LANES, (group + 1) * LANES)
        total, line = totals[group // blocks], group % blocks
        mean = total[line : line + 1, :] / kept
        rstd = lax.rsqrt(total[blocks + line : blocks + line + 1, :] / kept - mean * mean + EPS_NORM)
        single = got_ref[group * count_cin]
        gain = single[2 * blocks : 2 * blocks + 1, :]
        shift = single[2 * blocks + 1 : 2 * blocks + 2, :]
        norm_ref[0:1, lanes] = mean
        norm_ref[1:2, lanes] = rstd
        norm_ref[2:3, lanes] = gain
        norm_ref[3:4, lanes] = shift
        norm_ref[4:8, lanes] = jnp.broadcast_to(kept, (4, LANES))
        value, slope = gelu_parts(gain * ((wide_ref[:, lanes] - mean) * rstd) + shift)
        slope_ref[:, lanes] = slope * mask * (1.0 / PIX)
        pooled_ref[:, lanes] = jnp.sum((value * mask).reshape(PIX, part, LANES), axis=0) * (1.0 / PIX)
    wide_ref.send()
    norm_ref.send()
    weight_ref[0:16, :] = head_ref[...]
    weight_ref[16:LANES, :] = jnp.zeros((LANES - 16, weight_ref.shape[1]), BF)
    pooled = pooled_ref[...].astype(BF)
    head = weight_ref[...]
    class_index = lax.broadcasted_iota(jnp.int32, (part, LANES), 1)
    logits = matmul(pooled, head, NT) + bias_ref[...]
    logits = jnp.where(class_index < CLASSES, logits, -1e30)
    logits = logits - jnp.max(logits, axis=1, keepdims=True)
    log_probs = logits - jnp.log(jnp.sum(jnp.exp(logits), axis=1, keepdims=True))
    wanted = jnp.where(class_index == labels_ref[...], 1.0 - SMOOTH, 0.0) + SMOOTH / CLASSES
    wanted = jnp.where(class_index < CLASSES, wanted, 0.0)
    loss = -jnp.sum(jnp.sum(wanted * log_probs, axis=1, keepdims=True), axis=0, keepdims=True)
    logit_grad = jnp.exp(log_probs) - wanted
    head_grad = matmul(logit_grad, pooled.astype(F32), TN, PRECISE)
    pooled_grad = matmul(logit_grad, head.astype(F32), NN, PRECISE)
    extra = jnp.sum(logit_grad, axis=0, keepdims=True)
    extra = jnp.where(class_index[0:1, :] == CLASSES, loss, extra)
    line = lax.broadcasted_iota(jnp.int32, (16, LANES), 0)
    gains, shifts = [], []
    for group in range(groups):
        lanes = slice(group * LANES, (group + 1) * LANES)
        head_out_ref[group] = jnp.where(line == CLASSES, extra, head_grad[0:16, lanes])
        spread = jnp.broadcast_to(pooled_grad[:, lanes][None], (PIX, part, LANES)).reshape(rows, LANES)
        dz = slope_ref[:, lanes] * spread
        dz_ref[:, lanes] = dz
        scaled = (wide_ref[:, lanes] - norm_ref[0:1, lanes]) * norm_ref[1:2, lanes]
        gains.append(jnp.sum(dz * scaled, axis=0, keepdims=True))
        shifts.append(jnp.sum(dz, axis=0, keepdims=True))
    sums_ref[...] = jnp.broadcast_to(jnp.concatenate(gains + shifts, axis=0)[None], sums_ref.shape)


def total_of(got_ref):
    total = got_ref[0]
    for source in range(1, got_ref.shape[0]):
        total = total + got_ref[source]
    return total


def norm_back(scaled, dz, norm, mask, gain_grad, shift_grad):
    gain = norm[2:3, :]
    return norm[1:2, :] * (
        gain * dz - mask * (gain / norm[4:5, :]) * (shift_grad + scaled * gain_grad)
    )


def second_back_kernel(
    place_ref, dz_ref, wide_ref, norm_ref, got_ref, mask_ref, first_ref, norm_first_ref, head_ref, basis_ref, near_refs, far_refs,
    grad_ref, sums_out_ref, sums_ref, send_refs, part_ref, weight_ref, sum_ref, arrived,
):
    me, side = place_ref[0], place_ref[1]
    depth, half = near_refs[0].shape[1:]
    copies = []
    for refs, at in ((near_refs, side), (far_refs, 1 - side)):
        lanes = pl.ds(pl.multiple_of(at * half, half), half)
        for step, slot_ref in enumerate(refs):
            span = pl.ds(pl.multiple_of((me ^ step) * depth, depth), depth)
            copies.append(
                pltpu.make_async_copy(slot_ref, weight_ref.at[:, span, lanes], arrived.at[len(copies)])
            )
            copies[-1].start()
    total = total_of(got_ref)
    sums_out_ref[...] = total
    groups = total.shape[0] // 2
    mask = mask_ref[...]
    for group in range(groups):
        lanes = slice(group * LANES, (group + 1) * LANES)
        norm = norm_ref[:, lanes]
        grad_ref[:, lanes] = norm_back(
            (wide_ref[:, lanes] - norm[0:1, :]) * norm[1:2, :], dz_ref[:, lanes], norm, mask,
            total[group : group + 1, :], total[groups + group : groups + group + 1, :],
        ).astype(BF)
    grad_ref.send()
    sums_out_ref.send()
    for copy in copies:
        copy.wait()
    rows, channels = grad_ref.shape
    part = rows // PIX
    sum_ref[...] = jnp.zeros_like(sum_ref)
    for tap in range(TAPS):
        product = matmul(grad_ref[...], weight_ref[tap], NT)
        row_step, col_step = OFFSETS[tap]
        for to_row, from_row, length in runs(-row_step, -col_step, part):
            sum_ref[to_row : to_row + length, :] += product[from_row : from_row + length, :]
    gains, shifts = [], []
    for lane in range(0, channels, LANES):
        lanes = slice(lane, lane + LANES)
        norm = norm_first_ref[:, lanes]
        scaled = first_ref[:, lanes].astype(F32)
        _, slope = gelu_parts(norm[2:3, :] * scaled + norm[3:4, :])
        dz = slope * mask * sum_ref[:, lanes]
        part_ref[:, lanes] = (norm[1:2, :] * norm[2:3, :] * dz).astype(BF)
        gains.append(jnp.sum(dz * scaled, axis=0, keepdims=True))
        shifts.append(jnp.sum(dz, axis=0, keepdims=True))
    sum_ref[...] = matmul(part_ref[...], basis_ref[...])
    send_columns(me, sum_ref, send_refs)
    count_dp, _, count_cin = sums_ref.shape[:3]
    for group in range(groups):
        tile = jnp.concatenate(gains + shifts + [head_ref[group], jnp.zeros((8, LANES), F32)], axis=0)
        tile = tile.astype(BF)
        for far in range(count_dp):
            for near in range(count_cin):
                sums_ref[far, group, near] = tile


def first_products_kernel(
    place_ref, got_ref, norm_ref, mask_ref, basis_ref, old_refs, big_refs, part_refs, scaled_refs,
    out_ref, sums_ref, small_ref, left_ref, right_ref, slot_ref, column_ref, mask_slot_ref,
):
    me = place_ref[0]
    rows, width = part_refs[0].shape
    part = rows // PIX
    count = mask_ref.shape[0] // PIX
    whole = got_ref[0].astype(F32)
    for source in range(1, got_ref.shape[0]):
        whole = whole + got_ref[source].astype(F32)
    sums_ref[...] = whole[0:8, :]
    small_ref[...] = jnp.zeros(small_ref.shape, F32)
    small_ref[8:24, :] = whole[8:24, :]
    for at, row in enumerate((24, 28, 32, 48, 64, 65)):
        lines, lanes = old_refs[at].shape
        small_ref[row : row + lines, 0:lanes] = old_refs[at][...]
    groups = len(part_refs)
    column_ref[...] = basis_ref[:, pl.ds(pl.multiple_of(me * width, width), width)]
    rates, shifts = [], []
    for group in range(groups):
        lanes = slice(group * LANES, (group + 1) * LANES)
        scale = norm_ref[1:2, lanes] * norm_ref[2:3, lanes] / norm_ref[4:5, lanes]
        rates.append(scale * whole[group : group + 1, :])
        shifts.append(scale * whole[groups + group : groups + group + 1, :])
    rate = jnp.concatenate(rates, axis=1)
    shift = jnp.broadcast_to(jnp.concatenate(shifts, axis=1), (8, groups * LANES))
    fixed = matmul(shift, column_ref[...].astype(F32), NN, PRECISE)[0:1, :]
    for step in range(groups):
        for pixel in range(PIX):
            base = pl.ds(pl.multiple_of(pixel * count + (me ^ step) * part, part), part)
            mask_slot_ref[pixel * part : (pixel + 1) * part, :] = mask_ref[base, :]
        moved = matmul((scaled_refs[step][...].astype(F32) * rate).astype(BF), column_ref[...])
        slot_ref[step] = (
            part_refs[step][...].astype(F32) - mask_slot_ref[...].astype(F32) * (fixed + moved)
        ).astype(BF)
    taps_kernel(-1, big_refs, [slot_ref.at[step] for step in range(groups)], out_ref, left_ref, right_ref)


def left_second_kernel(place_ref, norm_ref, mask_ref, basis_ref, scaled_refs, left_refs, column_ref, wide_ref):
    me = place_ref[0]
    rows, width = left_refs[0].shape
    part = rows // PIX
    count = mask_ref.shape[0] // PIX
    column_ref[...] = basis_ref[:, pl.ds(pl.multiple_of(me * width, width), width)]
    for step, scaled_ref in enumerate(scaled_refs):
        mask = jnp.concatenate(
            [
                mask_ref[pl.ds(pl.multiple_of(pixel * count + (me ^ step) * part, part), part), :]
                for pixel in range(PIX)
            ],
            axis=0,
        ).astype(F32)
        for lane in range(0, wide_ref.shape[1], LANES):
            lanes = slice(lane, lane + LANES)
            value, _ = gelu_parts(
                norm_ref[2:3, lanes] * scaled_ref[:, lanes].astype(F32) + norm_ref[3:4, lanes]
            )
            wide_ref[:, lanes] = (value * mask).astype(BF)
        left_refs[step][...] = matmul(wide_ref[...], column_ref[...]).astype(BF)


def right_kernel(grad_ref, basis_ref, right_ref):
    right_ref[...] = jnp.transpose(matmul(grad_ref[...], basis_ref[...])).astype(BF)


def send_columns(me, product_ref, send_refs):
    for step, send_ref in enumerate(send_refs):
        lanes = pl.ds(pl.multiple_of((me ^ step) * LANES, LANES), LANES)
        send_ref[...] = product_ref[:, lanes].astype(BF)


def left_first_kernel(place_ref, images_ref, masks_ref, basis_ref, left_ref, mask_ref, inputs_ref, part_ref):
    slots = left_ref.shape[0]
    count = masks_ref.shape[1]
    part = count // slots
    me = place_ref[0]
    fill_mask(masks_ref, mask_ref)
    fill_inputs(images_ref, mask_ref, inputs_ref)
    for step in range(slots):
        for pixel in range(PIX):
            base = pl.multiple_of(pixel * count + (me ^ step) * part, part)
            part_ref[pixel * part : (pixel + 1) * part, :] = inputs_ref[pl.ds(base, part), :]
        left_ref[step] = jnp.transpose(matmul(part_ref[...], basis_ref[...])).astype(BF)


def taps_kernel(sign, big_refs, small_refs, out_ref, left_ref, right_ref):
    rows, width = small_refs[0].shape
    channels = big_refs[0].shape[0]
    part = rows // PIX
    right_ref[...] = jnp.zeros_like(right_ref)
    for slot, (big_ref, small_ref) in enumerate(zip(big_refs, small_refs)):
        base = slot * rows
        left_ref[:, base : base + rows] = big_ref[...]
        for tap, (row_step, col_step) in enumerate(OFFSETS):
            for to_row, from_row, length in runs(sign * row_step, sign * col_step, part):
                right_ref[base + to_row : base + to_row + length, tap * width : (tap + 1) * width] = (
                    small_ref[from_row : from_row + length, :]
                )
    for tap in range(0, TAPS, 2):
        taps = min(2, TAPS - tap)
        product = matmul(left_ref[...], right_ref[:, tap * width : (tap + taps) * width])
        for nth in range(taps):
            out_ref[(tap + nth) * channels : (tap + nth + 1) * channels, :] = product[
                :, nth * width : (nth + 1) * width
            ].astype(BF)


def ratio_kernel(own_refs, scales_ref, coeff_ref, ratio_ref):
    coeff = None
    for ref in own_refs:
        coeff = ref[...].astype(F32) if coeff is None else coeff + ref[...].astype(F32)
    scales = SCALE_DECAY * scales_ref[...] + (1.0 - SCALE_DECAY) * coeff * coeff
    coeff_ref[...] = coeff.astype(BF)
    ratio_ref[...] = (coeff / (scales + DAMPING)).astype(BF)


def middle_kernel(basis_ref, slot_refs, out_ref):
    width = slot_refs[0].shape[1]
    ratio = jnp.concatenate([ref[...] for ref in slot_refs], axis=1)
    out_ref[...] = matmul(ratio, basis_ref[...], NT).astype(BF)


def scales_kernel(turned, coeff_ref, scales_ref, out_ref):
    taps = out_ref.shape[0]
    rows = coeff_ref.shape[0] // taps
    for tap in range(taps):
        coeff = coeff_ref[tap * rows : (tap + 1) * rows, :].astype(F32)
        if turned:
            coeff = jnp.transpose(coeff)
        out_ref[tap] = SCALE_DECAY * scales_ref[tap] + (1.0 - SCALE_DECAY) * coeff * coeff


def wide_ratio_kernel(place_ref, coeff_ref, scales_ref, scales_out_ref, ratio_ref):
    half = ratio_ref.shape[0]
    rows = pl.ds(pl.multiple_of(place_ref[1] * half, half), half)
    coeff = coeff_ref[...].astype(F32)
    scales_out_ref[...] = SCALE_DECAY * scales_ref[...] + (1.0 - SCALE_DECAY) * coeff * coeff
    scales_out_ref.send()
    ratio_ref[...] = (coeff_ref[rows, :].astype(F32) / (scales_out_ref[rows, :] + DAMPING)).astype(BF)


def add_squares(total, values):
    return total + jnp.sum((values * values).reshape(-1, 8, LANES), axis=0)


def restore_kernel(
    place_ref, basis_in_ref, middle_first_ref, basis_out_ref, middle_second_ref, sums_first_ref, sums_second_ref,
    old_ref, first_ref, second_ref, squares_ref, small_ref, stack_ref,
):
    me = place_ref[0]
    channels = basis_in_ref.shape[0]
    total = jnp.zeros((8, LANES), F32)
    for tap in range(TAPS):
        product = matmul(
            middle_second_ref[tap * channels : (tap + 1) * channels, :], basis_out_ref[...], (((0,), (1,)), ((), ()))
        )
        second_ref[tap] = product.astype(BF)
        for lane in range(0, channels, LANES):
            total = add_squares(total, product[:, lane : lane + LANES])
    for tap in range(TAPS):
        stack_ref[:, tap * LANES : (tap + 1) * LANES] = middle_first_ref[
            tap * channels : (tap + 1) * channels, :
        ]
    for tap in range(0, TAPS, 2):
        taps = min(2, TAPS - tap)
        product = matmul(basis_in_ref[...], stack_ref[:, tap * LANES : (tap + taps) * LANES])
        for nth in range(taps):
            block = product[:, nth * LANES : (nth + 1) * LANES]
            first_ref[tap + nth] = block.astype(BF)
            total = add_squares(total, block)
    groups = sums_first_ref.shape[0] // 2
    row = lax.broadcasted_iota(jnp.int32, (8, LANES), 0)
    mine = (row == me) | (row == me + groups)
    for ref in (sums_first_ref, sums_second_ref):
        total = total + jnp.where(mine, ref[...] * ref[...], 0.0)
    line = lax.broadcasted_iota(jnp.int32, (16, LANES), 0)
    lane = lax.broadcasted_iota(jnp.int32, (16, LANES), 1)
    counted = (line < CLASSES) | ((line == CLASSES) & (lane < CLASSES) & (me == 0))
    head = jnp.where(counted, old_ref[8:24, :], 0.0)
    small_ref[...] = old_ref[...]
    for at, ref in enumerate((sums_first_ref, sums_second_ref)):
        small_ref[2 * at : 2 * at + 1, :] = ref[pl.ds(me, 1), :]
        small_ref[2 * at + 1 : 2 * at + 2, :] = ref[pl.ds(me + groups, 1), :]
    squares_ref[...] = add_squares(total, head)


def update_kernel(
    square_refs, weight_refs, mean_refs, square_moment_refs, grad_refs, small_refs,
    weight_outs, mean_outs, square_outs, small_outs, scalar_outs,
):
    parts = [ref[...] for ref in square_refs]
    while len(parts) > 1:
        parts = [parts[at] + parts[at + 1] for at in range(0, len(parts), 2)]
    total = jnp.sum(jnp.sum(parts[0], axis=1, keepdims=True), axis=0, keepdims=True)
    grad_norm = jnp.sqrt(total)
    factor = CLIP_NORM / jnp.maximum(grad_norm, CLIP_NORM)

    def moments(gradient, mean_old, square_old):
        mean_new = BETA_ONE * mean_old + (1.0 - BETA_ONE) * gradient
        square_new = BETA_TWO * square_old + (1.0 - BETA_TWO) * gradient * gradient
        return mean_new, square_new

    taps = mean_outs[0].shape[0]
    for at in range(len(weight_refs)):
        for nth in range(taps):
            tap = pl.program_id(0) * taps + nth
            gradient = grad_refs[at][tap].astype(F32) * factor
            mean_new, square_new = moments(gradient, mean_refs[at][tap], square_moment_refs[at][tap])
            mean_outs[at][nth] = mean_new
            square_outs[at][nth] = square_new
            square_hat = square_new * (1.0 / (1.0 - BETA_TWO**STEP))
            size = square_hat * lax.rsqrt(square_hat) + ADAM_EPS
            step = mean_new * (LEARN_RATE / (1.0 - BETA_ONE**STEP)) * pl.reciprocal(size, approx=True)
            weight_outs[at][nth] = weight_refs[at][tap] * (1.0 - LEARN_RATE * WEIGHT_DECAY) - step

    @pl.when(pl.program_id(0) == 0)
    def _():
        norm_out, loss_out = scalar_outs
        norm_out[...] = grad_norm
        (small,) = small_refs
        loss_out[...] = small[8 + CLASSES : 9 + CLASSES, CLASSES : CLASSES + 1]
        results = moments(small[0:4, :] * factor, small[24:28, :], small[28:32, :])
        for at in range(2):
            small_outs[at][...] = results[at][0:2, :]
            small_outs[2 + at][...] = results[at][2:4, :]
        results = moments(
            small[8 : 8 + CLASSES, :] * factor, small[32 : 32 + CLASSES, :], small[48 : 48 + CLASSES, :]
        )
        for at in range(2):
            small_outs[4 + at][...] = results[at]
        lanes = slice(0, CLASSES)
        results = moments(small[8 + CLASSES : 9 + CLASSES, lanes] * factor, small[64:65, lanes], small[65:66, lanes])
        for at in range(2):
            small_outs[6 + at][...] = results[at]


def swap(values, axis, step):
    count = lax.axis_size(axis)
    return lax.ppermute(values, axis, [(here, here ^ step) for here in range(count)])


def gathered(values, axis):
    return [values] + [swap(values, axis, step) for step in range(1, lax.axis_size(axis))]


def exchanged(sends, axis):
    return [sends[0]] + [swap(sends[step], axis, step) for step in range(1, len(sends))]


def picked(values, index):
    return lax.dynamic_index_in_dim(values, index, 0, keepdims=False)


def after(values, *others):
    return lax.optimization_barrier((values,) + others)[0]


def tree_sum(slots):
    while len(slots) > 1:
        slots = [slots[at] + slots[at + 1] for at in range(0, len(slots), 2)]
    return slots[0]


def every_device(tiles):
    return lax.all_to_all(tiles, EVERY, 0, 0, tiled=True)


def bits_of(axis):
    return range(lax.axis_size(axis).bit_length() - 1)


def halved(values, axis, bit):
    own = (lax.axis_index(axis) >> bit) & 1
    values = values.reshape(2, -1, values.shape[-1])
    return [picked(values, own), swap(picked(values, 1 - own), axis, 1 << bit)]


def doubled(values, axis, bit):
    own = (lax.axis_index(axis) >> bit) & 1
    other = swap(values, axis, 1 << bit)
    first = jnp.where(own == 0, values, other)
    return jnp.concatenate([first, jnp.where(own == 0, other, values)], axis=0)


def joined(terms):
    return terms[0] if len(terms) == 1 else (terms[0].astype(F32) + terms[1].astype(F32)).astype(BF)


def batch_gather(block, axes=("dp", "cin"), first=()):
    for order in reversed(first):
        block = doubled(block, *order)
    for axis in axes:
        for bit in reversed(bits_of(axis)):
            block = doubled(block, axis, bit)
    return block


def batch_rows(values):
    place = jnp.int32(0)
    for axis in ("cin", "dp"):
        for bit in bits_of(axis):
            place = place * 2 + ((lax.axis_index(axis) >> bit) & 1)
    rows = values.shape[0] // (lax.axis_size("dp") * lax.axis_size("cin"))
    return lax.dynamic_slice_in_dim(values, place * rows, rows, 0)


def local(
    images,
    masks,
    labels,
    w_first,
    w_second,
    norm_params,
    head_w,
    head_b,
    bases,
    scales_first,
    scales_second,
    w_first_mean,
    w_first_square,
    w_second_mean,
    w_second_square,
    norm_mean,
    norm_square,
    head_w_mean,
    head_w_square,
    head_b_mean,
    head_b_square,
):
    me = lax.axis_index("cout")
    side = lax.axis_index("cin") % 2
    place = jnp.stack([me, side]).astype(jnp.int32)
    sizes = tuple(lax.axis_size(name) for name in EVERY)
    groups = sizes[1]
    devices = sizes[0] * sizes[1] * sizes[2]
    channels = w_first.shape[1]
    width = w_first.shape[2]
    half = channels // 2
    count = images.shape[1]
    part = count // groups
    rows = PIX * part
    tile = shape((devices, 8, LANES), F32)
    wide = (rows, channels)
    basis_in_first, basis_out_first = bases[0, 0], bases[0, 1]
    basis_in_second, basis_out_second = bases[1, 0], bases[1, 1]
    bases_all = (basis_in_first, basis_out_first, basis_in_second, basis_out_second)

    piece = lax.dynamic_slice_in_dim(w_second, side * half, half, 2).astype(BF)
    own_labels = lax.dynamic_slice_in_dim(labels, me * part, part, 0)[:, None]
    bias_row = jnp.pad(head_b, (0, LANES - CLASSES))[None]

    flat_images = images.reshape(PIX * count, channels)
    first_out, all_mask, stats, mask = call(
        functools.partial(first_kernel, groups),
        [
            shape((PIX * count, width), F32),
            shape((PIX * count, LANES), BF),
            shape((sizes[0] * sizes[2], 8, LANES), F32),
            shape((rows, LANES), F32),
        ],
        [place, flat_images, masks, w_first],
        [
            pltpu.VMEM((PIX * count, LANES), F32),
            pltpu.VMEM((PIX * count, channels), BF),
            pltpu.VMEM((channels, TAPS * width), BF),
            pltpu.VMEM((TAPS, channels, width), F32),
            pltpu.SemaphoreType.DMA((3,)),
        ],
        near=(1, 2),
        raw=(3,),
        room=56,
        flops=2 * PIX * count * channels * width * TAPS,
    )
    got = lax.all_to_all(stats, ("dp", "cin"), 0, 0, tiled=True)
    (left_turned,) = call(
        left_first_kernel,
        [shape((groups, channels, rows), BF)],
        [place, after(flat_images, stats), masks, basis_in_first],
        [
            pltpu.VMEM((PIX * count, LANES), F32),
            pltpu.VMEM((PIX * count, channels), BF),
            pltpu.VMEM((rows, channels), BF),
        ],
        near=(1, 2, 3),
        room=20,
    )
    near_weights = [piece]
    for step in range(1, groups):
        ready = piece if step < groups - 1 else after(piece, stats)
        near_weights.append(swap(ready, "cout", step))
    first_mask = after(all_mask, left_turned, *near_weights[1:-1], *bases_all)
    *first_sends, kept = call(
        lambda *refs: first_norm_kernel(*refs[:6], refs[6 : 6 + groups], *refs[6 + groups :]),
        [shape((2 * rows + 16, width), BF)] * groups + [shape((8, LANES), F32)],
        [place, got, first_out, first_mask, norm_params, head_w.T],
        [pltpu.VMEM((PIX * count, LANES), BF), pltpu.VMEM((PIX * count, LANES), BF)],
        near_out=tuple(range(groups)),
    )
    def in_slots(values):
        return jnp.concatenate(
            [lax.dynamic_slice_in_dim(values, (me ^ step) * width, width, 1) for step in range(groups)], 1
        )

    def basis_rows(basis):
        return in_slots(lax.dynamic_slice_in_dim(basis, me * width, width, 0))

    scales_turned = batch_rows(
        jnp.swapaxes(after(scales_second, kept), 1, 2).reshape(TAPS * channels, width)
    )
    rows_first = basis_rows(after(basis_out_first, kept))
    rows_second = basis_rows(after(basis_in_second, kept))
    kept = after(kept, scales_turned, rows_first, rows_second)
    first_slots = exchanged(first_sends, "cout")
    (hidden,) = call(
        lambda *refs: hidden_kernel(refs[0], refs[1 : 1 + groups], *refs[1 + groups :]),
        [shape((rows, channels + LANES), BF)],
        [place, *first_slots, after(mask, kept)],
        near=tuple(range(1, 1 + groups)),
        near_out=(0,),
    )
    other_hidden = swap(hidden, "cin", 1)
    mine, theirs, stats = call(
        lambda *refs: second_kernel(*refs[:4], refs[4 : 4 + groups], *refs[4 + groups :]),
        [shape((rows, half), F32), shape((rows, half), F32), tile],
        [place, hidden, other_hidden, norm_params, *near_weights],
        [
            pltpu.VMEM((2 * rows, channels), BF),
            pltpu.VMEM((TAPS, channels, half), BF),
            pltpu.VMEM((2 * rows, half), F32),
            pltpu.SemaphoreType.DMA((groups,)),
        ],
        near=(1, 2),
        raw=tuple(range(4, 4 + groups)),
        flops=4 * rows * channels * half * TAPS,
    )
    scaled_first, norm_first, head_full = call(
        lambda *refs: gather_kernel(refs[0], refs[1 : 1 + groups], *refs[1 + groups :]),
        [shape(wide, BF), shape((8, channels), F32), shape((16, channels), BF)],
        [place, *first_slots, after(kept, mine)],
    )
    from_other = swap(theirs, "cin", 1)
    got_second = every_device(stats)
    far_weights = [swap(after(slot, mine), "cin", 1) for slot in near_weights]
    head_mask = after(mask, *far_weights)
    second_out, norm_second, dz_second, sums, head_blocks = call(
        functools.partial(head_kernel, sizes),
        [
            shape(wide, F32),
            shape((8, channels), F32),
            shape(wide, F32),
            tile,
            shape((groups, 16, width), F32),
        ],
        [place, mine, from_other, got_second, norm_first, head_mask, head_full, bias_row, own_labels],
        [
            pltpu.VMEM(wide, F32),
            pltpu.VMEM((part, channels), F32),
            pltpu.VMEM((LANES, channels), BF),
        ],
    )
    got = every_device(sums)
    scaled_slots = gathered(after(scaled_first, got_second), "cout")
    grad_second, sums_second, sums, *right_sends = call(
        lambda *refs: second_back_kernel(
            *refs[:10], refs[10 : 10 + groups], refs[10 + groups : 10 + 2 * groups],
            *refs[10 + 2 * groups : 13 + 2 * groups], refs[13 + 2 * groups : 13 + 3 * groups], *refs[13 + 3 * groups :]
        ),
        [shape(wide, BF), shape((8, LANES), F32), shape(sizes + (32, LANES), BF)] + [shape((rows, width), BF)] * groups,
        [
            place, dz_second, second_out, norm_second, got, after(mask, *scaled_slots), scaled_first,
            norm_first, head_blocks, basis_out_first, *near_weights, *far_weights,
        ],
        [
            pltpu.VMEM(wide, BF),
            pltpu.VMEM((TAPS, channels, channels), BF),
            pltpu.VMEM(wide, F32),
            pltpu.SemaphoreType.DMA((2 * groups,)),
        ],
        raw=tuple(range(10, 10 + 2 * groups)),
        flops=2 * rows * channels * channels * TAPS,
    )
    left_slots = call(
        lambda *refs: left_second_kernel(*refs[:4], refs[4 : 4 + groups], refs[4 + groups : 4 + 2 * groups], *refs[4 + 2 * groups :]),
        [shape((rows, width), BF)] * groups,
        [place, norm_first, after(all_mask, sums_second), basis_in_second, *scaled_slots],
        [pltpu.VMEM((channels, width), BF), pltpu.VMEM(wide, BF)],
    )
    (right_turned,) = call(
        right_kernel, [shape((channels, rows), BF)], [grad_second, basis_out_second], scalars=0
    )

    def products(sign, big, small, near=()):
        (out,) = call(
            lambda *refs: taps_kernel(sign, refs[:groups], refs[groups : 2 * groups], *refs[2 * groups :]),
            [shape((TAPS * channels, width), BF)],
            [*big, *small],
            [
                pltpu.VMEM((channels, groups * rows), BF),
                pltpu.VMEM((groups * rows, TAPS * width), BF),
            ],
            scalars=0,
            near=near,
            near_out=(0,),
            room=56,
            flops=2 * groups * rows * channels * width * TAPS,
        )
        return out

    right_parts = exchanged(right_sends, "cout")
    got = every_device(sums.reshape(devices, 32, LANES))
    right_slots = gathered(after(right_turned, got), "cout")
    orders = [(axis, bit) for axis in ("cin", "dp") for bit in bits_of(axis)]
    small_old = [norm_mean, norm_square, head_w_mean.T, head_w_square.T, head_b_mean[None], head_b_square[None]]
    def hold(*values):
        def copy_in(*refs):
            arrived = refs[-1]
            copies = [
                pltpu.make_async_copy(refs[at], refs[len(values) + at], arrived.at[at])
                for at in range(len(values))
            ]
            for copy in copies:
                copy.start()
            for copy in copies:
                copy.wait()

        return call(
            lambda *refs: copy_in(*refs),
            [shape(value.shape, value.dtype) for value in values],
            values,
            [pltpu.SemaphoreType.DMA((len(values),))],
            scalars=0,
            raw=tuple(range(len(values))),
            near_out=tuple(range(len(values))),
            room=16,
        )

    def ratio_of(terms, scales_own):
        chunk = shape(scales_own.shape, BF)
        return call(
            lambda *refs: ratio_kernel(refs[: len(terms)], *refs[len(terms) :]),
            [chunk, chunk],
            [*terms, scales_own],
            scalars=0,
            near=tuple(range(len(terms) + 1)),
            near_out=(0, 1),
            room=16,
        )

    def middle_of(slots, basis):
        (out,) = call(
            lambda basis_ref, *refs: middle_kernel(basis_ref, refs[:groups], refs[-1]),
            [shape(slots[0].shape, BF)],
            [basis, *slots],
            scalars=0,
            near=tuple(range(groups + 1)),
            near_out=(0,),
            room=16,
        )
        return out

    near_steps = len(bits_of("cin"))
    left_parts = [left_turned[step] for step in range(groups)]
    products_first, sums_first, smalls = call(
        lambda *refs: first_products_kernel(
            *refs[:5], refs[5:11], *[refs[11 + at * groups : 11 + (at + 1) * groups] for at in range(3)],
            *refs[11 + 3 * groups :]
        ),
        [shape((TAPS * channels, width), BF), shape((8, LANES), F32), shape((72, LANES), F32)],
        [
            place, after(got, right_turned, *left_slots), norm_first, all_mask, basis_out_first, *small_old, *left_parts, *right_parts, *scaled_slots,
        ],
        [
            pltpu.VMEM((channels, groups * rows), BF),
            pltpu.VMEM((groups * rows, TAPS * width), BF),
            pltpu.VMEM((groups, rows, width), BF),
            pltpu.VMEM((channels, width), BF),
            pltpu.VMEM((rows, LANES), BF),
        ],
        near_out=(0,),
        room=56,
        flops=2 * groups * rows * channels * width * TAPS,
    )
    terms_first = [products_first]
    for order in orders[:-1]:
        terms_first = halved(joined(terms_first), *order)
    near_first = joined(terms_first)
    terms_first = halved(near_first, *orders[-1])

    own_first = joined([after(terms_first[0], *right_slots), terms_first[1]])
    coeff_first = doubled(own_first, *orders[-1])
    products_second = products(1, [after(right_slots[0], own_first)] + right_slots[1:], left_slots)
    terms_second = [products_second]
    for order in orders[:near_steps]:
        terms_second = halved(joined(terms_second), *order)
    near_second = joined(terms_second)
    terms_second = [near_second]
    for order in orders[near_steps:-1]:
        terms_second = halved(joined(terms_second), *order)
    terms_far = terms_second
    for order in reversed(orders[near_steps:-1]):
        coeff_first = doubled(after(coeff_first, near_second), *order)
    coeff_first = batch_gather(coeff_first, ("cin",))
    flat_scales = scales_first.reshape(TAPS * channels, width)
    scales_first_new, ratio_first = call(
        wide_ratio_kernel,
        [shape(flat_scales.shape, F32), shape((TAPS * channels // 2, width), BF)],
        [place, coeff_first, flat_scales],
        near=(1, 2),
        near_out=(1,),
        room=16,
    )
    slots_first = gathered(ratio_first, "cout")
    terms_second = halved(joined(terms_second), *orders[-1])
    own_second, ratio_second = ratio_of(terms_second, after(scales_turned, ratio_first))
    weights = hold(after(w_first, own_second), w_second)
    coeff_second = doubled(own_second, *orders[-1])
    middle_second = middle_of(gathered(ratio_second, "cout"), after(rows_second, coeff_second, ratio_first))
    means = hold(after(w_first_mean, weights[0]), w_second_mean)
    middle_first = middle_of(slots_first, after(rows_first, *means))
    gathered_first = doubled(middle_first, "cin", 0)
    squares_old = hold(after(w_first_square, middle_second), w_second_square)
    gathered_second = doubled(middle_second, *orders[-1])
    for order in reversed(orders[near_steps:-1]):
        coeff_second = doubled(coeff_second, *order)
        gathered_second = doubled(after(gathered_second, *squares_old), *order)
    gathered_second = batch_gather(gathered_second, ("cin",))
    coeff_second = batch_gather(coeff_second, ("cin",))

    def scales_of(turned, coeff, scales):
        spec = pl.BlockSpec((3,) + scales.shape[1:], lambda tap: (tap, 0, 0))
        return pl.pallas_call(
            functools.partial(scales_kernel, turned),
            grid=(TAPS // 3,),
            in_specs=[pl.BlockSpec((3 * channels, width), lambda tap: (tap, 0)), spec],
            out_specs=spec,
            out_shape=shape(scales.shape, F32),
            compiler_params=pltpu.CompilerParams(vmem_limit_bytes=12 * 1024 * 1024),
        )(coeff, scales)

    scales_second_new = scales_of(True, coeff_second, scales_second)

    first_grad, second_grad, squares, small_grads = call(
        restore_kernel,
        [shape((TAPS, channels, width), BF), shape((TAPS, width, channels), BF), shape((8, LANES), F32), shape((72, LANES), F32)],
        [
            place,
            basis_in_first,
            gathered_first,
            basis_out_second,
            gathered_second,
            sums_first,
            sums_second,
            smalls,
        ],
        [pltpu.VMEM((channels, TAPS * width), BF)],
        near=tuple(range(1, 8)),
        near_out=(0, 1, 2, 3),
        room=16,
        flops=4 * TAPS * channels * channels * width,
    )
    square_slots = gathered(squares, "cout")
    square_slots[0] = after(square_slots[0], coeff_second)

    smalls = [small_grads]
    small_outs = [shape((2, width), F32)] * 4 + [shape((CLASSES, width), F32)] * 2 + [shape((1, CLASSES), F32)] * 2
    small_outs += [shape((1, 1), F32)] * 2
    first_spec = pl.BlockSpec((1, channels, width), lambda tap: (tap, 0, 0))
    second_spec = pl.BlockSpec((1, width, channels), lambda tap: (tap, 0, 0))
    pair = [first_spec, second_spec]
    first_like, second_like = shape(w_first.shape, F32), shape(w_second.shape, F32)

    def whole(leaf):
        return pl.BlockSpec(leaf.shape, lambda tap: (0,) * len(leaf.shape))

    def update(*refs):
        at = [0]

        def take(number):
            at[0] += number
            return refs[at[0] - number : at[0]]

        update_kernel(
            take(groups), take(2), take(2), take(2), take(2), take(len(smalls)),
            take(2), take(2), take(2), take(len(small_outs) - 2), take(2),
        )

    results = pl.pallas_call(
        update,
        grid=(TAPS,),
        in_specs=[pl.BlockSpec(memory_space=pltpu.VMEM)] * (groups + 8 + len(smalls)),
        out_specs=pair * 3 + [whole(leaf) for leaf in small_outs],
        out_shape=[first_like, second_like] * 3 + small_outs,
        compiler_params=pltpu.CompilerParams(vmem_limit_bytes=16 * 1024 * 1024),
    )(
        *square_slots, *weights, *means, *squares_old,
        first_grad, second_grad, *smalls,
    )
    (first_new, second_new, first_mean_new, second_mean_new, first_square_new, second_square_new,
     norm_first_mean, norm_first_square, norm_second_mean, norm_second_square,
     head_mean_new, head_square_new, bias_mean_new, bias_square_new, grad_norm, loss_total) = results
    return (
        loss_total.reshape(()),
        grad_norm.reshape(()),
        first_new,
        first_mean_new,
        first_square_new,
        second_new,
        second_mean_new,
        second_square_new,
        norm_first_mean,
        norm_first_square,
        norm_second_mean,
        norm_second_square,
        head_mean_new.T,
        head_square_new.T,
        bias_mean_new[0],
        bias_square_new[0],
        scales_first_new.reshape(scales_first.shape),
        scales_second_new,
    )


def solution(mesh):
    return jax.shard_map(
        local,
        mesh=mesh,
        in_specs=(
            P(None, ("dp", "cin"), None),
            P(None, ("dp", "cin")),
            P(("dp", "cin")),
            P(None, None, "cout"),
            P(None, "cout", None),
            P(None, "cout"),
            P("cout", None),
            P(),
            P(),
            P(None, None, "cout"),
            P(None, "cout", None),
            P(None, None, "cout"),
            P(None, None, "cout"),
            P(None, "cout", None),
            P(None, "cout", None),
            P(None, "cout"),
            P(None, "cout"),
            P("cout", None),
            P("cout", None),
            P(),
            P(),
        ),
        out_specs=(
            P(),
            P(),
            P(None, None, "cout"),
            P(None, None, "cout"),
            P(None, None, "cout"),
            P(None, "cout", None),
            P(None, "cout", None),
            P(None, "cout", None),
            P(None, "cout"),
            P(None, "cout"),
            P(None, "cout"),
            P(None, "cout"),
            P("cout", None),
            P("cout", None),
            P(),
            P(),
            P(None, None, "cout"),
            P(None, "cout", None),
        ),
        check_vma=False,
    )
```

```python
import functools
import math

import jax
import jax.numpy as jnp
from jax import lax
from jax.experimental import pallas as pl
from jax.experimental.pallas import tpu as pltpu
from jax.sharding import PartitionSpec as P

CLASSES = 10
SIDE = 4
PIX = 16
TAPS = 9
STEP = 10
LANES = 128

EPS_NORM = 1e-05
SCALE_DECAY = 0.95
DAMPING = 0.001
CLIP_NORM = 1.0
LEARN_RATE = 0.01
BETA_ONE = 0.9
BETA_TWO = 0.999
ADAM_EPS = 1e-08
WEIGHT_DECAY = 0.01
SMOOTH = 0.1
OFFSETS = [(row_step, col_step) for row_step in (-1, 0, 1) for col_step in (-1, 0, 1)]
EVERY = ("dp", "cout", "cin")
BF = jnp.bfloat16
F32 = jnp.float32
PRECISE = lax.Precision.HIGHEST
NN = (((1,), (0,)), ((), ()))
NT = (((1,), (1,)), ((), ()))
TN = (((0,), (0,)), ((), ()))


def matmul(left, right, dims=NN, precision=None):
    return lax.dot_general(
        left, right, dims, precision=precision, preferred_element_type=F32
    )


def runs(row_step, col_step, count):
    low, high = max(0, -col_step), min(SIDE, SIDE - col_step)
    found = []
    for row in range(max(0, -row_step), min(SIDE, SIDE - row_step)):
        to_row = (row * SIDE + low) * count
        from_row = ((row + row_step) * SIDE + low + col_step) * count
        length = (high - low) * count
        if found and found[-1][0] + found[-1][2] == to_row and found[-1][1] + found[-1][2] == from_row:
            found[-1] = (found[-1][0], found[-1][1], found[-1][2] + length)
        else:
            found.append((to_row, from_row, length))
    return found


class Late:
    def __init__(self, ref, copy):
        self.ref, self.copy, self.shape = ref, copy, ref.shape
        copy.start()

    def settle(self):
        if self.copy is not None:
            self.copy.wait()
        self.copy = None

    def __getitem__(self, index):
        self.settle()
        return self.ref[index]


class Result:
    def __init__(self, ref, copy):
        self.ref, self.copy, self.shape, self.sent = ref, copy, ref.shape, False

    def __getitem__(self, index):
        return self.ref[index]

    def __setitem__(self, index, values):
        self.ref[index] = values

    def send(self):
        if not self.sent:
            self.copy.start()
        self.sent = True


def call(kernel, outs, args, scratch=(), scalars=1, near=(), raw=(), near_out=(), flops=0, room=60):
    n_in, n_out = len(args), len(outs)
    copied = [at for at in range(scalars, n_in) if at not in near and at not in raw]
    copied_out = [at for at in range(n_out) if at not in near_out]

    def body(*refs):
        ins, results = list(refs[:n_in]), list(refs[n_in : n_in + n_out])
        rest = refs[n_in + n_out :]
        held, held_out = rest[: len(copied)], rest[len(copied) : len(copied) + len(copied_out)]
        own, arrived = rest[len(copied) + len(copied_out) : -1], rest[-1]
        for nth, at in enumerate(copied):
            ins[at] = Late(held[nth], pltpu.make_async_copy(ins[at], held[nth], arrived.at[nth]))
        for nth, at in enumerate(copied_out):
            copy = pltpu.make_async_copy(held_out[nth], results[at], arrived.at[len(copied) + nth])
            results[at] = Result(held_out[nth], copy)
        kernel(*ins, *results, *own)
        for at in copied:
            ins[at].settle()
        for at in copied_out:
            results[at].send()
        for at in copied_out:
            results[at].copy.wait()

    specs = [pl.BlockSpec(memory_space=pltpu.SMEM)] * scalars
    specs += [
        pl.BlockSpec(memory_space=pltpu.VMEM if at in near else pltpu.HBM) for at in range(scalars, n_in)
    ]
    moved = sum(math.prod(a.shape) * a.dtype.itemsize for a in list(args) + list(outs))
    return pl.pallas_call(
        body,
        out_shape=list(outs),
        in_specs=specs,
        out_specs=[
            pl.BlockSpec(memory_space=pltpu.VMEM if at in near_out else pltpu.HBM) for at in range(n_out)
        ],
        scratch_shapes=[pltpu.VMEM(args[at].shape, args[at].dtype) for at in copied]
        + [pltpu.VMEM(outs[at].shape, outs[at].dtype) for at in copied_out]
        + list(scratch)
        + [pltpu.SemaphoreType.DMA((max(1, len(copied) + len(copied_out)),))],
        compiler_params=pltpu.CompilerParams(vmem_limit_bytes=room * 1024 * 1024),
        cost_estimate=pl.CostEstimate(flops=flops, bytes_accessed=moved, transcendentals=0),
    )(*args)


def shape(dims, dtype):
    return jax.ShapeDtypeStruct(dims, dtype)


def gelu_parts(values):
    rate = math.sqrt(2.0 / math.pi)
    bend = jnp.tanh(rate * (values + 0.044715 * values * values * values))
    share = 0.5 * (1.0 + bend)
    slope = share + 0.5 * values * (1.0 - bend * bend) * rate * (1.0 + 0.134145 * values * values)
    return values * share, slope


def fill_mask(masks_ref, mask_ref):
    count = masks_ref.shape[1]
    same = lax.broadcasted_iota(jnp.int32, (count, count), 0) == lax.broadcasted_iota(
        jnp.int32, (count, count), 1
    )
    for pixel in range(PIX):
        row = masks_ref[pixel : pixel + 1, :].astype(F32)
        column = jnp.sum(jnp.where(same, row, 0.0), axis=1, keepdims=True)
        mask_ref[pixel * count : (pixel + 1) * count, :] = jnp.broadcast_to(column, (count, LANES))


def fill_inputs(images_ref, mask_ref, inputs_ref):
    low = mask_ref[...].astype(BF)
    for lane in range(0, images_ref.shape[1], LANES):
        inputs_ref[:, lane : lane + LANES] = images_ref[:, lane : lane + LANES] * low


def first_kernel(
    groups, place_ref, images_ref, masks_ref, weight_ref,
    sum_ref, all_mask_ref, stats_ref, own_mask_ref, mask_ref, inputs_ref, low_ref, wide_ref, arrived,
):
    count = masks_ref.shape[1]
    part = count // groups
    me = place_ref[0]
    copies = [
        pltpu.make_async_copy(weight_ref.at[at : at + 3], wide_ref.at[at : at + 3], arrived.at[at // 3])
        for at in range(0, TAPS, 3)
    ]
    for copy in copies:
        copy.start()
    fill_mask(masks_ref, mask_ref)
    fill_inputs(images_ref, mask_ref, inputs_ref)
    all_mask_ref[...] = mask_ref[...].astype(BF)
    all_mask_ref.send()
    for pixel in range(PIX):
        own = pl.multiple_of(pixel * count + me * part, part)
        own_mask_ref[pixel * part : (pixel + 1) * part, :] = mask_ref[pl.ds(own, part), :]
    own_mask_ref.send()
    for tap in range(TAPS):
        if tap % 3 == 0:
            copies[tap // 3].wait()
        low_ref[:, tap * LANES : (tap + 1) * LANES] = wide_ref[tap].astype(BF)
    sum_ref[...] = jnp.zeros(sum_ref.shape, F32)
    for tap in range(0, TAPS, 2):
        taps = min(2, TAPS - tap)
        product = matmul(inputs_ref[...], low_ref[:, tap * LANES : (tap + taps) * LANES])
        for nth in range(taps):
            for to_row, from_row, length in runs(*OFFSETS[tap + nth], count):
                sum_ref[to_row : to_row + length, :] += product[
                    from_row : from_row + length, nth * LANES : (nth + 1) * LANES
                ]
    sum_ref.send()
    mask = mask_ref[...]
    total = sum_ref[...]
    masked = total * mask
    tile = jnp.concatenate(
        [
            jnp.sum(masked, axis=0, keepdims=True),
            jnp.sum(masked * total, axis=0, keepdims=True),
            jnp.sum(mask, axis=0, keepdims=True),
            jnp.zeros((5, LANES), F32),
        ],
        axis=0,
    )
    stats_ref[...] = jnp.broadcast_to(tile[None], stats_ref.shape)


def first_norm_kernel(
    place_ref, got_ref, first_ref, mask_ref, params_ref, head_ref, send_refs, kept_ref, hidden_ref, scaled_ref
):
    total = total_of(got_ref)
    kept = total[2:3, :]
    mean = total[0:1, :] / kept
    rstd = lax.rsqrt(total[1:2, :] / kept - mean * mean + EPS_NORM)
    kept_ref[...] = jnp.broadcast_to(kept, kept_ref.shape)
    gain, shift = params_ref[0:1, :], params_ref[1:2, :]
    count = first_ref.shape[0] // PIX
    part = count // len(send_refs)
    scaled = (first_ref[...] - mean) * rstd
    value, _ = gelu_parts(gain * scaled + shift)
    hidden_ref[...] = (value * mask_ref[...].astype(F32)).astype(BF)
    scaled_ref[...] = scaled.astype(BF)
    lines = [head_ref[...]]
    for line in (rstd, gain, shift):
        high = line.astype(BF).astype(F32)
        lines += [high, line - high]
    extra = jnp.concatenate(lines, axis=0).astype(BF)
    rows = PIX * part
    for step, send_ref in enumerate(send_refs):
        for pixel in range(PIX):
            base = pl.ds(pl.multiple_of(pixel * count + (place_ref[0] ^ step) * part, part), part)
            send_ref[pixel * part : (pixel + 1) * part, :] = hidden_ref[base, :]
            send_ref[rows + pixel * part : rows + (pixel + 1) * part, :] = scaled_ref[base, :]
        send_ref[2 * rows : 2 * rows + 16, :] = extra


def hidden_kernel(place_ref, slot_refs, mask_ref, hidden_ref):
    rows = hidden_ref.shape[0]
    for step, slot_ref in enumerate(slot_refs):
        lanes = pl.ds(pl.multiple_of((place_ref[0] ^ step) * LANES, LANES), LANES)
        hidden_ref[:, lanes] = slot_ref[0:rows, :]
    hidden_ref[:, len(slot_refs) * LANES :] = mask_ref[...].astype(BF)


def gather_kernel(place_ref, slot_refs, kept_ref, scaled_ref, norm_ref, head_ref):
    rows = scaled_ref.shape[0]
    norm_ref[0:1, :] = jnp.zeros((1, norm_ref.shape[1]), F32)
    norm_ref[5:8, :] = jnp.zeros((3, norm_ref.shape[1]), F32)
    for step, slot_ref in enumerate(slot_refs):
        lanes = pl.ds(pl.multiple_of((place_ref[0] ^ step) * LANES, LANES), LANES)
        scaled_ref[:, lanes] = slot_ref[rows : 2 * rows, :]
        extra = slot_ref[2 * rows : 2 * rows + 16, :].astype(F32)
        line = lax.broadcasted_iota(jnp.int32, (16, LANES), 0)
        head_ref[:, lanes] = jnp.where(line < CLASSES, extra, 0.0).astype(BF)
        for at in range(3):
            norm_ref[at + 1 : at + 2, lanes] = (
                extra[CLASSES + 2 * at : CLASSES + 2 * at + 1, :] + extra[CLASSES + 2 * at + 1 : CLASSES + 2 * at + 2, :]
            )
        norm_ref[4:5, lanes] = kept_ref[0:1, :]


def second_kernel(
    place_ref, own_ref, other_ref, params_ref, slot_refs,
    mine_ref, theirs_ref, stats_ref, inputs_ref, weight_ref, sum_ref, arrived,
):
    me = place_ref[0]
    rows = own_ref.shape[0]
    part = rows // PIX
    depth, half = slot_refs[0].shape[1:]
    copies = []
    for step, slot_ref in enumerate(slot_refs):
        span = pl.ds(pl.multiple_of((me ^ step) * depth, depth), depth)
        copies.append(pltpu.make_async_copy(slot_ref, weight_ref.at[:, span, :], arrived.at[step]))
        copies[-1].start()
    channels = inputs_ref.shape[1]
    inputs_ref[0:rows, :] = own_ref[:, 0:channels]
    inputs_ref[rows : 2 * rows, :] = other_ref[:, 0:channels]
    sum_ref[...] = jnp.zeros_like(sum_ref)
    for copy in copies:
        copy.wait()
    for tap in range(TAPS):
        product = matmul(inputs_ref[...], weight_ref[tap])
        for to_row, from_row, length in runs(*OFFSETS[tap], part):
            for base in (0, rows):
                sum_ref[base + to_row : base + to_row + length, :] += product[
                    base + from_row : base + from_row + length, :
                ]
    mine_ref[...] = sum_ref[0:rows, :]
    theirs_ref[...] = sum_ref[rows : 2 * rows, :]
    lines = [[], []]
    for lane in range(0, half, LANES):
        first = square = None
        for base, ref in ((0, own_ref), (rows, other_ref)):
            total = sum_ref[base : base + rows, lane : lane + LANES]
            masked = total * ref[:, channels : channels + LANES].astype(F32)
            first_part = jnp.sum(masked, axis=0, keepdims=True)
            square_part = jnp.sum(masked * total, axis=0, keepdims=True)
            first = first_part if first is None else first + first_part
            square = square_part if square is None else square + square_part
        lines[0].append(first)
        lines[1].append(square)
    spare = 8 - 2 * (half // LANES) - 2
    tile = jnp.concatenate(
        lines[0] + lines[1] + [params_ref[2:4, :], jnp.zeros((spare, LANES), F32)], axis=0
    )
    stats_ref[...] = jnp.broadcast_to(tile[None], stats_ref.shape)


def head_kernel(
    sizes, place_ref, mine_ref, got_ref_rows, got_ref, norm_first_ref, mask_ref, head_ref, bias_ref, labels_ref,
    wide_ref, norm_ref, dz_ref, sums_ref, head_out_ref, slope_ref, pooled_ref, weight_ref,
):
    count_dp, groups, count_cin = sizes
    side = place_ref[1]
    rows, half = mine_ref.shape
    part = rows // PIX
    blocks = half // LANES
    wide_ref[:, pl.ds(pl.multiple_of(side * half, half), half)] = mine_ref[...]
    wide_ref[:, pl.ds(pl.multiple_of((1 - side) * half, half), half)] = got_ref_rows[...]
    totals = [None, None]
    for source in range(count_dp * groups * count_cin):
        which = source % count_cin % 2
        tile = got_ref[source]
        totals[which] = tile if totals[which] is None else totals[which] + tile
    kept = norm_first_ref[4:5, 0:LANES]
    mask = mask_ref[...]
    for group in range(groups):
        lanes = slice(group * LANES, (group + 1) * LANES)
        total, line = totals[group // blocks], group % blocks
        mean = total[line : line + 1, :] / kept
        rstd = lax.rsqrt(total[blocks + line : blocks + line + 1, :] / kept - mean * mean + EPS_NORM)
        single = got_ref[group * count_cin]
        gain = single[2 * blocks : 2 * blocks + 1, :]
        shift = single[2 * blocks + 1 : 2 * blocks + 2, :]
        norm_ref[0:1, lanes] = mean
        norm_ref[1:2, lanes] = rstd
        norm_ref[2:3, lanes] = gain
        norm_ref[3:4, lanes] = shift
        norm_ref[4:8, lanes] = jnp.broadcast_to(kept, (4, LANES))
        value, slope = gelu_parts(gain * ((wide_ref[:, lanes] - mean) * rstd) + shift)
        slope_ref[:, lanes] = slope * mask * (1.0 / PIX)
        pooled_ref[:, lanes] = jnp.sum((value * mask).reshape(PIX, part, LANES), axis=0) * (1.0 / PIX)
    wide_ref.send()
    norm_ref.send()
    weight_ref[0:16, :] = head_ref[...]
    weight_ref[16:LANES, :] = jnp.zeros((LANES - 16, weight_ref.shape[1]), BF)
    pooled = pooled_ref[...].astype(BF)
    head = weight_ref[...]
    class_index = lax.broadcasted_iota(jnp.int32, (part, LANES), 1)
    logits = matmul(pooled, head, NT) + bias_ref[...]
    logits = jnp.where(class_index < CLASSES, logits, -1e30)
    logits = logits - jnp.max(logits, axis=1, keepdims=True)
    log_probs = logits - jnp.log(jnp.sum(jnp.exp(logits), axis=1, keepdims=True))
    wanted = jnp.where(class_index == labels_ref[...], 1.0 - SMOOTH, 0.0) + SMOOTH / CLASSES
    wanted = jnp.where(class_index < CLASSES, wanted, 0.0)
    loss = -jnp.sum(jnp.sum(wanted * log_probs, axis=1, keepdims=True), axis=0, keepdims=True)
    logit_grad = jnp.exp(log_probs) - wanted
    head_grad = matmul(logit_grad, pooled.astype(F32), TN, PRECISE)
    pooled_grad = matmul(logit_grad, head.astype(F32), NN, PRECISE)
    extra = jnp.sum(logit_grad, axis=0, keepdims=True)
    extra = jnp.where(class_index[0:1, :] == CLASSES, loss, extra)
    line = lax.broadcasted_iota(jnp.int32, (16, LANES), 0)
    gains, shifts = [], []
    for group in range(groups):
        lanes = slice(group * LANES, (group + 1) * LANES)
        head_out_ref[group] = jnp.where(line == CLASSES, extra, head_grad[0:16, lanes])
        spread = jnp.broadcast_to(pooled_grad[:, lanes][None], (PIX, part, LANES)).reshape(rows, LANES)
        dz = slope_ref[:, lanes] * spread
        dz_ref[:, lanes] = dz
        scaled = (wide_ref[:, lanes] - norm_ref[0:1, lanes]) * norm_ref[1:2, lanes]
        gains.append(jnp.sum(dz * scaled, axis=0, keepdims=True))
        shifts.append(jnp.sum(dz, axis=0, keepdims=True))
    sums_ref[...] = jnp.broadcast_to(jnp.concatenate(gains + shifts, axis=0)[None], sums_ref.shape)


def total_of(got_ref):
    total = got_ref[0]
    for source in range(1, got_ref.shape[0]):
        total = total + got_ref[source]
    return total


def norm_back(scaled, dz, norm, mask, gain_grad, shift_grad):
    gain = norm[2:3, :]
    return norm[1:2, :] * (
        gain * dz - mask * (gain / norm[4:5, :]) * (shift_grad + scaled * gain_grad)
    )


def second_back_kernel(
    place_ref, dz_ref, wide_ref, norm_ref, got_ref, mask_ref, first_ref, norm_first_ref, head_ref, basis_ref, near_refs, far_refs,
    grad_ref, sums_out_ref, sums_ref, send_refs, part_ref, weight_ref, sum_ref, arrived,
):
    me, side = place_ref[0], place_ref[1]
    depth, half = near_refs[0].shape[1:]
    copies = []
    for refs, at in ((near_refs, side), (far_refs, 1 - side)):
        lanes = pl.ds(pl.multiple_of(at * half, half), half)
        for step, slot_ref in enumerate(refs):
            span = pl.ds(pl.multiple_of((me ^ step) * depth, depth), depth)
            copies.append(
                pltpu.make_async_copy(slot_ref, weight_ref.at[:, span, lanes], arrived.at[len(copies)])
            )
            copies[-1].start()
    total = total_of(got_ref)
    sums_out_ref[...] = total
    groups = total.shape[0] // 2
    mask = mask_ref[...]
    for group in range(groups):
        lanes = slice(group * LANES, (group + 1) * LANES)
        norm = norm_ref[:, lanes]
        grad_ref[:, lanes] = norm_back(
            (wide_ref[:, lanes] - norm[0:1, :]) * norm[1:2, :], dz_ref[:, lanes], norm, mask,
            total[group : group + 1, :], total[groups + group : groups + group + 1, :],
        ).astype(BF)
    grad_ref.send()
    sums_out_ref.send()
    for copy in copies:
        copy.wait()
    rows, channels = grad_ref.shape
    part = rows // PIX
    sum_ref[...] = jnp.zeros_like(sum_ref)
    for tap in range(TAPS):
        product = matmul(grad_ref[...], weight_ref[tap], NT)
        row_step, col_step = OFFSETS[tap]
        for to_row, from_row, length in runs(-row_step, -col_step, part):
            sum_ref[to_row : to_row + length, :] += product[from_row : from_row + length, :]
    gains, shifts = [], []
    for lane in range(0, channels, LANES):
        lanes = slice(lane, lane + LANES)
        norm = norm_first_ref[:, lanes]
        scaled = first_ref[:, lanes].astype(F32)
        _, slope = gelu_parts(norm[2:3, :] * scaled + norm[3:4, :])
        dz = slope * mask * sum_ref[:, lanes]
        part_ref[:, lanes] = (norm[1:2, :] * norm[2:3, :] * dz).astype(BF)
        gains.append(jnp.sum(dz * scaled, axis=0, keepdims=True))
        shifts.append(jnp.sum(dz, axis=0, keepdims=True))
    sum_ref[...] = matmul(part_ref[...], basis_ref[...])
    send_columns(me, sum_ref, send_refs)
    count_dp, _, count_cin = sums_ref.shape[:3]
    for group in range(groups):
        tile = jnp.concatenate(gains + shifts + [head_ref[group], jnp.zeros((8, LANES), F32)], axis=0)
        tile = tile.astype(BF)
        for far in range(count_dp):
            for near in range(count_cin):
                sums_ref[far, group, near] = tile


def first_products_kernel(
    place_ref, got_ref, norm_ref, mask_ref, basis_ref, old_refs, big_refs, part_refs, scaled_refs,
    out_ref, sums_ref, small_ref, left_ref, right_ref, slot_ref, column_ref, mask_slot_ref,
):
    me = place_ref[0]
    rows, width = part_refs[0].shape
    part = rows // PIX
    count = mask_ref.shape[0] // PIX
    whole = got_ref[0].astype(F32)
    for source in range(1, got_ref.shape[0]):
        whole = whole + got_ref[source].astype(F32)
    sums_ref[...] = whole[0:8, :]
    small_ref[...] = jnp.zeros(small_ref.shape, F32)
    small_ref[8:24, :] = whole[8:24, :]
    for at, row in enumerate((24, 28, 32, 48, 64, 65)):
        lines, lanes = old_refs[at].shape
        small_ref[row : row + lines, 0:lanes] = old_refs[at][...]
    groups = len(part_refs)
    column_ref[...] = basis_ref[:, pl.ds(pl.multiple_of(me * width, width), width)]
    rates, shifts = [], []
    for group in range(groups):
        lanes = slice(group * LANES, (group + 1) * LANES)
        scale = norm_ref[1:2, lanes] * norm_ref[2:3, lanes] / norm_ref[4:5, lanes]
        rates.append(scale * whole[group : group + 1, :])
        shifts.append(scale * whole[groups + group : groups + group + 1, :])
    rate = jnp.concatenate(rates, axis=1)
    shift = jnp.broadcast_to(jnp.concatenate(shifts, axis=1), (8, groups * LANES))
    fixed = matmul(shift, column_ref[...].astype(F32), NN, PRECISE)[0:1, :]
    for step in range(groups):
        for pixel in range(PIX):
            base = pl.ds(pl.multiple_of(pixel * count + (me ^ step) * part, part), part)
            mask_slot_ref[pixel * part : (pixel + 1) * part, :] = mask_ref[base, :]
        moved = matmul((scaled_refs[step][...].astype(F32) * rate).astype(BF), column_ref[...])
        slot_ref[step] = (
            part_refs[step][...].astype(F32) - mask_slot_ref[...].astype(F32) * (fixed + moved)
        ).astype(BF)
    taps_kernel(-1, big_refs, [slot_ref.at[step] for step in range(groups)], out_ref, left_ref, right_ref)


def left_second_kernel(place_ref, norm_ref, mask_ref, basis_ref, scaled_refs, left_refs, column_ref, wide_ref):
    me = place_ref[0]
    rows, width = left_refs[0].shape
    part = rows // PIX
    count = mask_ref.shape[0] // PIX
    column_ref[...] = basis_ref[:, pl.ds(pl.multiple_of(me * width, width), width)]
    for step, scaled_ref in enumerate(scaled_refs):
        mask = jnp.concatenate(
            [
                mask_ref[pl.ds(pl.multiple_of(pixel * count + (me ^ step) * part, part), part), :]
                for pixel in range(PIX)
            ],
            axis=0,
        ).astype(F32)
        for lane in range(0, wide_ref.shape[1], LANES):
            lanes = slice(lane, lane + LANES)
            value, _ = gelu_parts(
                norm_ref[2:3, lanes] * scaled_ref[:, lanes].astype(F32) + norm_ref[3:4, lanes]
            )
            wide_ref[:, lanes] = (value * mask).astype(BF)
        left_refs[step][...] = matmul(wide_ref[...], column_ref[...]).astype(BF)


def right_kernel(grad_ref, basis_ref, right_ref):
    right_ref[...] = jnp.transpose(matmul(grad_ref[...], basis_ref[...])).astype(BF)


def send_columns(me, product_ref, send_refs):
    for step, send_ref in enumerate(send_refs):
        lanes = pl.ds(pl.multiple_of((me ^ step) * LANES, LANES), LANES)
        send_ref[...] = product_ref[:, lanes].astype(BF)


def left_first_kernel(place_ref, images_ref, masks_ref, basis_ref, left_ref, mask_ref, inputs_ref, part_ref):
    slots = left_ref.shape[0]
    count = masks_ref.shape[1]
    part = count // slots
    me = place_ref[0]
    fill_mask(masks_ref, mask_ref)
    fill_inputs(images_ref, mask_ref, inputs_ref)
    for step in range(slots):
        for pixel in range(PIX):
            base = pl.multiple_of(pixel * count + (me ^ step) * part, part)
            part_ref[pixel * part : (pixel + 1) * part, :] = inputs_ref[pl.ds(base, part), :]
        left_ref[step] = jnp.transpose(matmul(part_ref[...], basis_ref[...])).astype(BF)


def pick_kernel(own_ref, full_ref, kept_ref, sent_ref):
    half = kept_ref.shape[0]
    kept_ref[...] = full_ref[pl.ds(pl.multiple_of(own_ref[0] * half, half), half), :]
    sent_ref[...] = full_ref[pl.ds(pl.multiple_of((1 - own_ref[0]) * half, half), half), :]


def split_kernel(own_ref, here_ref, came_ref, kept_ref, sent_ref):
    half = kept_ref.shape[0]
    for which, ref in ((own_ref[0], kept_ref), (1 - own_ref[0], sent_ref)):
        rows = pl.ds(pl.multiple_of(which * half, half), half)
        ref[...] = (here_ref[rows, :].astype(F32) + came_ref[rows, :].astype(F32)).astype(BF)


def merge_kernel(own_ref, here_ref, came_ref, out_ref):
    rows = here_ref.shape[0]
    for choice in range(2):

        @pl.when(own_ref[0] == choice)
        def _():
            out_ref[choice * rows : (choice + 1) * rows, :] = here_ref[...]
            out_ref[(1 - choice) * rows : (2 - choice) * rows, :] = came_ref[...]


def taps_kernel(sign, big_refs, small_refs, out_ref, left_ref, right_ref):
    rows, width = small_refs[0].shape
    channels = big_refs[0].shape[0]
    part = rows // PIX
    right_ref[...] = jnp.zeros_like(right_ref)
    for slot, (big_ref, small_ref) in enumerate(zip(big_refs, small_refs)):
        base = slot * rows
        left_ref[:, base : base + rows] = big_ref[...]
        for tap, (row_step, col_step) in enumerate(OFFSETS):
            for to_row, from_row, length in runs(sign * row_step, sign * col_step, part):
                right_ref[base + to_row : base + to_row + length, tap * width : (tap + 1) * width] = (
                    small_ref[from_row : from_row + length, :]
                )
    for tap in range(0, TAPS, 2):
        taps = min(2, TAPS - tap)
        product = matmul(left_ref[...], right_ref[:, tap * width : (tap + taps) * width])
        for nth in range(taps):
            out_ref[(tap + nth) * channels : (tap + nth + 1) * channels, :] = product[
                :, nth * width : (nth + 1) * width
            ].astype(BF)


def ratio_kernel(own_refs, scales_ref, coeff_ref, ratio_ref):
    coeff = None
    for ref in own_refs:
        coeff = ref[...].astype(F32) if coeff is None else coeff + ref[...].astype(F32)
    scales = SCALE_DECAY * scales_ref[...] + (1.0 - SCALE_DECAY) * coeff * coeff
    coeff_ref[...] = coeff.astype(BF)
    ratio_ref[...] = (coeff / (scales + DAMPING)).astype(BF)


def middle_kernel(basis_ref, slot_refs, out_ref):
    width = slot_refs[0].shape[1]
    ratio = jnp.concatenate([ref[...] for ref in slot_refs], axis=1)
    out_ref[...] = matmul(ratio, basis_ref[...], NT).astype(BF)


def scales_kernel(turned, coeff_ref, scales_ref, out_ref):
    taps = out_ref.shape[0]
    rows = coeff_ref.shape[0] // taps
    for tap in range(taps):
        coeff = coeff_ref[tap * rows : (tap + 1) * rows, :].astype(F32)
        if turned:
            coeff = jnp.transpose(coeff)
        out_ref[tap] = SCALE_DECAY * scales_ref[tap] + (1.0 - SCALE_DECAY) * coeff * coeff


def wide_ratio_kernel(place_ref, coeff_ref, scales_ref, scales_out_ref, ratio_ref):
    half = ratio_ref.shape[0]
    rows = pl.ds(pl.multiple_of(place_ref[1] * half, half), half)
    coeff = coeff_ref[...].astype(F32)
    scales_out_ref[...] = SCALE_DECAY * scales_ref[...] + (1.0 - SCALE_DECAY) * coeff * coeff
    scales_out_ref.send()
    ratio_ref[...] = (coeff_ref[rows, :].astype(F32) / (scales_out_ref[rows, :] + DAMPING)).astype(BF)


def add_squares(total, values):
    return total + jnp.sum((values * values).reshape(-1, 8, LANES), axis=0)


def restore_kernel(
    place_ref, basis_in_ref, middle_first_ref, basis_out_ref, middle_second_ref, sums_first_ref, sums_second_ref,
    old_ref, first_ref, second_ref, squares_ref, small_ref, stack_ref,
):
    me = place_ref[0]
    channels = basis_in_ref.shape[0]
    total = jnp.zeros((8, LANES), F32)
    for tap in range(TAPS):
        product = matmul(
            middle_second_ref[tap * channels : (tap + 1) * channels, :], basis_out_ref[...], (((0,), (1,)), ((), ()))
        )
        second_ref[tap] = product.astype(BF)
        for lane in range(0, channels, LANES):
            total = add_squares(total, product[:, lane : lane + LANES])
    for tap in range(TAPS):
        stack_ref[:, tap * LANES : (tap + 1) * LANES] = middle_first_ref[
            tap * channels : (tap + 1) * channels, :
        ]
    for tap in range(0, TAPS, 2):
        taps = min(2, TAPS - tap)
        product = matmul(basis_in_ref[...], stack_ref[:, tap * LANES : (tap + taps) * LANES])
        for nth in range(taps):
            block = product[:, nth * LANES : (nth + 1) * LANES]
            first_ref[tap + nth] = block.astype(BF)
            total = add_squares(total, block)
    groups = sums_first_ref.shape[0] // 2
    row = lax.broadcasted_iota(jnp.int32, (8, LANES), 0)
    mine = (row == me) | (row == me + groups)
    for ref in (sums_first_ref, sums_second_ref):
        total = total + jnp.where(mine, ref[...] * ref[...], 0.0)
    line = lax.broadcasted_iota(jnp.int32, (16, LANES), 0)
    lane = lax.broadcasted_iota(jnp.int32, (16, LANES), 1)
    counted = (line < CLASSES) | ((line == CLASSES) & (lane < CLASSES) & (me == 0))
    head = jnp.where(counted, old_ref[8:24, :], 0.0)
    small_ref[...] = old_ref[...]
    for at, ref in enumerate((sums_first_ref, sums_second_ref)):
        small_ref[2 * at : 2 * at + 1, :] = ref[pl.ds(me, 1), :]
        small_ref[2 * at + 1 : 2 * at + 2, :] = ref[pl.ds(me + groups, 1), :]
    squares_ref[...] = add_squares(total, head)


def update_kernel(
    square_refs, weight_refs, mean_refs, square_moment_refs, grad_refs, small_refs,
    weight_outs, mean_outs, square_outs, small_outs, scalar_outs,
):
    parts = [ref[...] for ref in square_refs]
    while len(parts) > 1:
        parts = [parts[at] + parts[at + 1] for at in range(0, len(parts), 2)]
    total = jnp.sum(jnp.sum(parts[0], axis=1, keepdims=True), axis=0, keepdims=True)
    grad_norm = jnp.sqrt(total)
    factor = CLIP_NORM / jnp.maximum(grad_norm, CLIP_NORM)

    def moments(gradient, mean_old, square_old):
        mean_new = BETA_ONE * mean_old + (1.0 - BETA_ONE) * gradient
        square_new = BETA_TWO * square_old + (1.0 - BETA_TWO) * gradient * gradient
        return mean_new, square_new

    taps = mean_outs[0].shape[0]
    for at in range(len(weight_refs)):
        for nth in range(taps):
            tap = pl.program_id(0) * taps + nth
            gradient = grad_refs[at][tap].astype(F32) * factor
            mean_new, square_new = moments(gradient, mean_refs[at][tap], square_moment_refs[at][tap])
            mean_outs[at][nth] = mean_new
            square_outs[at][nth] = square_new
            square_hat = square_new * (1.0 / (1.0 - BETA_TWO**STEP))
            size = square_hat * lax.rsqrt(square_hat) + ADAM_EPS
            step = mean_new * (LEARN_RATE / (1.0 - BETA_ONE**STEP)) * pl.reciprocal(size, approx=True)
            weight_outs[at][nth] = weight_refs[at][tap] * (1.0 - LEARN_RATE * WEIGHT_DECAY) - step

    @pl.when(pl.program_id(0) == 0)
    def _():
        norm_out, loss_out = scalar_outs
        norm_out[...] = grad_norm
        (small,) = small_refs
        loss_out[...] = small[8 + CLASSES : 9 + CLASSES, CLASSES : CLASSES + 1]
        results = moments(small[0:4, :] * factor, small[24:28, :], small[28:32, :])
        for at in range(2):
            small_outs[at][...] = results[at][0:2, :]
            small_outs[2 + at][...] = results[at][2:4, :]
        results = moments(
            small[8 : 8 + CLASSES, :] * factor, small[32 : 32 + CLASSES, :], small[48 : 48 + CLASSES, :]
        )
        for at in range(2):
            small_outs[4 + at][...] = results[at]
        lanes = slice(0, CLASSES)
        results = moments(small[8 + CLASSES : 9 + CLASSES, lanes] * factor, small[64:65, lanes], small[65:66, lanes])
        for at in range(2):
            small_outs[6 + at][...] = results[at]


def swap(values, axis, step):
    count = lax.axis_size(axis)
    return lax.ppermute(values, axis, [(here, here ^ step) for here in range(count)])


def gathered(values, axis):
    return [values] + [swap(values, axis, step) for step in range(1, lax.axis_size(axis))]


def exchanged(sends, axis):
    return [sends[0]] + [swap(sends[step], axis, step) for step in range(1, len(sends))]


def picked(values, index):
    return lax.dynamic_index_in_dim(values, index, 0, keepdims=False)


def after(values, *others):
    return lax.optimization_barrier((values,) + others)[0]


def tree_sum(slots):
    while len(slots) > 1:
        slots = [slots[at] + slots[at + 1] for at in range(0, len(slots), 2)]
    return slots[0]


def every_device(tiles):
    return lax.all_to_all(tiles, EVERY, 0, 0, tiled=True)


def bits_of(axis):
    return range(lax.axis_size(axis).bit_length() - 1)


def bit_of(axis, bit):
    return (lax.axis_index(axis) >> bit) & 1


def crossed(parts, axis, bit):
    return [parts[0], swap(parts[1], axis, 1 << bit)]


def halved(terms, axis, bit):
    rows, width = terms[0].shape
    own = bit_of(axis, bit)
    if rows // 2 % 16:
        total = joined(terms).reshape(2, rows // 2, width)
        return crossed([picked(total, own), picked(total, 1 - own)], axis, bit)
    half = shape((rows // 2, width), BF)
    parts = call(
        pick_kernel if len(terms) == 1 else split_kernel,
        [half, half],
        [own[None], *terms],
        near=tuple(range(1, 1 + len(terms))),
        near_out=(0, 1),
        room=16,
    )
    return crossed(parts, axis, bit)


def doubled(values, axis, bit):
    own = bit_of(axis, bit)
    rows, width = values.shape
    other = swap(values, axis, 1 << bit)
    (out,) = call(
        merge_kernel, [shape((2 * rows, width), BF)], [own[None], values, other], near=(1, 2), near_out=(0,), room=16
    )
    return out


def joined(terms):
    return terms[0] if len(terms) == 1 else (terms[0].astype(F32) + terms[1].astype(F32)).astype(BF)


def batch_gather(block, axes=("dp", "cin"), first=()):
    for order in reversed(first):
        block = doubled(block, *order)
    for axis in axes:
        for bit in reversed(bits_of(axis)):
            block = doubled(block, axis, bit)
    return block


def batch_rows(values):
    place = jnp.int32(0)
    for axis in ("cin", "dp"):
        for bit in bits_of(axis):
            place = place * 2 + ((lax.axis_index(axis) >> bit) & 1)
    rows = values.shape[0] // (lax.axis_size("dp") * lax.axis_size("cin"))
    return lax.dynamic_slice_in_dim(values, place * rows, rows, 0)


def local(
    images,
    masks,
    labels,
    w_first,
    w_second,
    norm_params,
    head_w,
    head_b,
    bases,
    scales_first,
    scales_second,
    w_first_mean,
    w_first_square,
    w_second_mean,
    w_second_square,
    norm_mean,
    norm_square,
    head_w_mean,
    head_w_square,
    head_b_mean,
    head_b_square,
):
    me = lax.axis_index("cout")
    side = lax.axis_index("cin") % 2
    place = jnp.stack([me, side]).astype(jnp.int32)
    sizes = tuple(lax.axis_size(name) for name in EVERY)
    groups = sizes[1]
    devices = sizes[0] * sizes[1] * sizes[2]
    channels = w_first.shape[1]
    width = w_first.shape[2]
    half = channels // 2
    count = images.shape[1]
    part = count // groups
    rows = PIX * part
    tile = shape((devices, 8, LANES), F32)
    wide = (rows, channels)
    basis_in_first, basis_out_first = bases[0, 0], bases[0, 1]
    basis_in_second, basis_out_second = bases[1, 0], bases[1, 1]
    bases_all = (basis_in_first, basis_out_first, basis_in_second, basis_out_second)

    piece = lax.dynamic_slice_in_dim(w_second, side * half, half, 2).astype(BF)
    own_labels = lax.dynamic_slice_in_dim(labels, me * part, part, 0)[:, None]
    bias_row = jnp.pad(head_b, (0, LANES - CLASSES))[None]

    flat_images = images.reshape(PIX * count, channels)
    first_out, all_mask, stats, mask = call(
        functools.partial(first_kernel, groups),
        [
            shape((PIX * count, width), F32),
            shape((PIX * count, LANES), BF),
            shape((sizes[0] * sizes[2], 8, LANES), F32),
            shape((rows, LANES), F32),
        ],
        [place, flat_images, masks, w_first],
        [
            pltpu.VMEM((PIX * count, LANES), F32),
            pltpu.VMEM((PIX * count, channels), BF),
            pltpu.VMEM((channels, TAPS * width), BF),
            pltpu.VMEM((TAPS, channels, width), F32),
            pltpu.SemaphoreType.DMA((3,)),
        ],
        near=(1, 2),
        raw=(3,),
        room=56,
        flops=2 * PIX * count * channels * width * TAPS,
    )
    got = lax.all_to_all(stats, ("dp", "cin"), 0, 0, tiled=True)
    (left_turned,) = call(
        left_first_kernel,
        [shape((groups, channels, rows), BF)],
        [place, after(flat_images, stats), masks, basis_in_first],
        [
            pltpu.VMEM((PIX * count, LANES), F32),
            pltpu.VMEM((PIX * count, channels), BF),
            pltpu.VMEM((rows, channels), BF),
        ],
        near=(1, 2, 3),
        room=20,
    )
    near_weights = [piece]
    for step in range(1, groups):
        ready = piece if step < groups - 1 else after(piece, stats)
        near_weights.append(swap(ready, "cout", step))
    first_mask = after(all_mask, left_turned, *near_weights[1:-1], *bases_all)
    *first_sends, kept = call(
        lambda *refs: first_norm_kernel(*refs[:6], refs[6 : 6 + groups], *refs[6 + groups :]),
        [shape((2 * rows + 16, width), BF)] * groups + [shape((8, LANES), F32)],
        [place, got, first_out, first_mask, norm_params, head_w.T],
        [pltpu.VMEM((PIX * count, LANES), BF), pltpu.VMEM((PIX * count, LANES), BF)],
        near_out=tuple(range(groups)),
    )
    def in_slots(values):
        return jnp.concatenate(
            [lax.dynamic_slice_in_dim(values, (me ^ step) * width, width, 1) for step in range(groups)], 1
        )

    def basis_rows(basis):
        return in_slots(lax.dynamic_slice_in_dim(basis, me * width, width, 0))

    scales_turned = batch_rows(
        jnp.swapaxes(after(scales_second, kept), 1, 2).reshape(TAPS * channels, width)
    )
    rows_first = basis_rows(after(basis_out_first, kept))
    rows_second = basis_rows(after(basis_in_second, kept))
    kept = after(kept, scales_turned, rows_first, rows_second)
    first_slots = exchanged(first_sends, "cout")
    (hidden,) = call(
        lambda *refs: hidden_kernel(refs[0], refs[1 : 1 + groups], *refs[1 + groups :]),
        [shape((rows, channels + LANES), BF)],
        [place, *first_slots, after(mask, kept)],
        near=tuple(range(1, 1 + groups)),
        near_out=(0,),
    )
    other_hidden = swap(hidden, "cin", 1)
    mine, theirs, stats = call(
        lambda *refs: second_kernel(*refs[:4], refs[4 : 4 + groups], *refs[4 + groups :]),
        [shape((rows, half), F32), shape((rows, half), F32), tile],
        [place, hidden, other_hidden, norm_params, *near_weights],
        [
            pltpu.VMEM((2 * rows, channels), BF),
            pltpu.VMEM((TAPS, channels, half), BF),
            pltpu.VMEM((2 * rows, half), F32),
            pltpu.SemaphoreType.DMA((groups,)),
        ],
        near=(1, 2),
        raw=tuple(range(4, 4 + groups)),
        flops=4 * rows * channels * half * TAPS,
    )
    scaled_first, norm_first, head_full = call(
        lambda *refs: gather_kernel(refs[0], refs[1 : 1 + groups], *refs[1 + groups :]),
        [shape(wide, BF), shape((8, channels), F32), shape((16, channels), BF)],
        [place, *first_slots, after(kept, mine)],
    )
    from_other = swap(theirs, "cin", 1)
    got_second = every_device(stats)
    far_weights = [swap(after(slot, mine), "cin", 1) for slot in near_weights]
    head_mask = after(mask, *far_weights)
    second_out, norm_second, dz_second, sums, head_blocks = call(
        functools.partial(head_kernel, sizes),
        [
            shape(wide, F32),
            shape((8, channels), F32),
            shape(wide, F32),
            tile,
            shape((groups, 16, width), F32),
        ],
        [place, mine, from_other, got_second, norm_first, head_mask, head_full, bias_row, own_labels],
        [
            pltpu.VMEM(wide, F32),
            pltpu.VMEM((part, channels), F32),
            pltpu.VMEM((LANES, channels), BF),
        ],
    )
    got = every_device(sums)
    scaled_slots = gathered(after(scaled_first, got_second), "cout")
    grad_second, sums_second, sums, *right_sends = call(
        lambda *refs: second_back_kernel(
            *refs[:10], refs[10 : 10 + groups], refs[10 + groups : 10 + 2 * groups],
            *refs[10 + 2 * groups : 13 + 2 * groups], refs[13 + 2 * groups : 13 + 3 * groups], *refs[13 + 3 * groups :]
        ),
        [shape(wide, BF), shape((8, LANES), F32), shape(sizes + (32, LANES), BF)] + [shape((rows, width), BF)] * groups,
        [
            place, dz_second, second_out, norm_second, got, after(mask, *scaled_slots), scaled_first,
            norm_first, head_blocks, basis_out_first, *near_weights, *far_weights,
        ],
        [
            pltpu.VMEM(wide, BF),
            pltpu.VMEM((TAPS, channels, channels), BF),
            pltpu.VMEM(wide, F32),
            pltpu.SemaphoreType.DMA((2 * groups,)),
        ],
        raw=tuple(range(10, 10 + 2 * groups)),
        flops=2 * rows * channels * channels * TAPS,
    )
    left_slots = call(
        lambda *refs: left_second_kernel(*refs[:4], refs[4 : 4 + groups], refs[4 + groups : 4 + 2 * groups], *refs[4 + 2 * groups :]),
        [shape((rows, width), BF)] * groups,
        [place, norm_first, after(all_mask, sums_second), basis_in_second, *scaled_slots],
        [pltpu.VMEM((channels, width), BF), pltpu.VMEM(wide, BF)],
    )
    (right_turned,) = call(
        right_kernel, [shape((channels, rows), BF)], [grad_second, basis_out_second], scalars=0
    )

    def products(sign, big, small, near=()):
        (out,) = call(
            lambda *refs: taps_kernel(sign, refs[:groups], refs[groups : 2 * groups], *refs[2 * groups :]),
            [shape((TAPS * channels, width), BF)],
            [*big, *small],
            [
                pltpu.VMEM((channels, groups * rows), BF),
                pltpu.VMEM((groups * rows, TAPS * width), BF),
            ],
            scalars=0,
            near=near,
            near_out=(0,),
            room=44,
            flops=2 * groups * rows * channels * width * TAPS,
        )
        return out

    right_parts = exchanged(right_sends, "cout")
    got = every_device(sums.reshape(devices, 32, LANES))
    right_slots = gathered(after(right_turned, got), "cout")
    orders = [(axis, bit) for axis in ("cin", "dp") for bit in bits_of(axis)]
    small_old = [norm_mean, norm_square, head_w_mean.T, head_w_square.T, head_b_mean[None], head_b_square[None]]
    def hold(*values):
        def copy_in(*refs):
            arrived = refs[-1]
            copies = [
                pltpu.make_async_copy(refs[at], refs[len(values) + at], arrived.at[at])
                for at in range(len(values))
            ]
            for copy in copies:
                copy.start()
            for copy in copies:
                copy.wait()

        return call(
            lambda *refs: copy_in(*refs),
            [shape(value.shape, value.dtype) for value in values],
            values,
            [pltpu.SemaphoreType.DMA((len(values),))],
            scalars=0,
            raw=tuple(range(len(values))),
            near_out=tuple(range(len(values))),
            room=16,
        )

    def ratio_of(terms, scales_own):
        chunk = shape(scales_own.shape, BF)
        return call(
            lambda *refs: ratio_kernel(refs[: len(terms)], *refs[len(terms) :]),
            [chunk, chunk],
            [*terms, scales_own],
            scalars=0,
            near=tuple(range(len(terms) + 1)),
            near_out=(0, 1),
            room=16,
        )

    def middle_of(slots, basis):
        (out,) = call(
            lambda basis_ref, *refs: middle_kernel(basis_ref, refs[:groups], refs[-1]),
            [shape(slots[0].shape, BF)],
            [basis, *slots],
            scalars=0,
            near=tuple(range(groups + 1)),
            near_out=(0,),
            room=16,
        )
        return out

    near_steps = len(bits_of("cin"))
    left_parts = [left_turned[step] for step in range(groups)]
    products_first, sums_first, smalls = call(
        lambda *refs: first_products_kernel(
            *refs[:5], refs[5:11], *[refs[11 + at * groups : 11 + (at + 1) * groups] for at in range(3)],
            *refs[11 + 3 * groups :]
        ),
        [shape((TAPS * channels, width), BF), shape((8, LANES), F32), shape((72, LANES), F32)],
        [
            place, after(got, right_turned, *left_slots), norm_first, all_mask, basis_out_first, *small_old, *left_parts, *right_parts, *scaled_slots,
        ],
        [
            pltpu.VMEM((channels, groups * rows), BF),
            pltpu.VMEM((groups * rows, TAPS * width), BF),
            pltpu.VMEM((groups, rows, width), BF),
            pltpu.VMEM((channels, width), BF),
            pltpu.VMEM((rows, LANES), BF),
        ],
        near_out=(0,),
        room=56,
        flops=2 * groups * rows * channels * width * TAPS,
    )
    terms_first = [products_first]
    for order in orders:
        terms_first = halved(terms_first, *order)
    own_first = joined([after(terms_first[0], *right_slots), terms_first[1]])
    coeff_first = doubled(own_first, *orders[-1])
    terms_second = [products(1, [after(right_slots[0], own_first)] + right_slots[1:], left_slots)]
    for order in orders:
        terms_second = halved(terms_second, *order)
    for order in reversed(orders[near_steps:-1]):
        coeff_first = doubled(coeff_first, *order)
    coeff_first = batch_gather(coeff_first, ("cin",))
    flat_scales = scales_first.reshape(TAPS * channels, width)
    scales_first_new, ratio_first = call(
        wide_ratio_kernel,
        [shape(flat_scales.shape, F32), shape((TAPS * channels // 2, width), BF)],
        [place, coeff_first, flat_scales],
        near=(1, 2),
        near_out=(1,),
        room=16,
    )
    slots_first = gathered(ratio_first, "cout")
    own_second, ratio_second = ratio_of(terms_second, after(scales_turned, ratio_first))
    weights = hold(after(w_first, own_second), w_second)
    coeff_second = doubled(own_second, *orders[-1])
    middle_second = middle_of(gathered(ratio_second, "cout"), after(rows_second, coeff_second, ratio_first))
    means = hold(after(w_first_mean, weights[0]), w_second_mean)
    middle_first = middle_of(slots_first, after(rows_first, *means))
    gathered_first = doubled(middle_first, "cin", 0)
    squares_old = hold(after(w_first_square, middle_second), w_second_square)
    gathered_second = doubled(middle_second, *orders[-1])
    for order in reversed(orders[near_steps:-1]):
        coeff_second = doubled(coeff_second, *order)
        gathered_second = doubled(after(gathered_second, *squares_old), *order)
    gathered_second = batch_gather(gathered_second, ("cin",))
    coeff_second = batch_gather(coeff_second, ("cin",))

    def scales_of(turned, coeff, scales):
        spec = pl.BlockSpec((3,) + scales.shape[1:], lambda tap: (tap, 0, 0))
        return pl.pallas_call(
            functools.partial(scales_kernel, turned),
            grid=(TAPS // 3,),
            in_specs=[pl.BlockSpec((3 * channels, width), lambda tap: (tap, 0)), spec],
            out_specs=spec,
            out_shape=shape(scales.shape, F32),
            compiler_params=pltpu.CompilerParams(vmem_limit_bytes=12 * 1024 * 1024),
        )(coeff, scales)

    scales_second_new = scales_of(True, coeff_second, scales_second)

    first_grad, second_grad, squares, small_grads = call(
        restore_kernel,
        [shape((TAPS, channels, width), BF), shape((TAPS, width, channels), BF), shape((8, LANES), F32), shape((72, LANES), F32)],
        [
            place,
            basis_in_first,
            gathered_first,
            basis_out_second,
            gathered_second,
            sums_first,
            sums_second,
            smalls,
        ],
        [pltpu.VMEM((channels, TAPS * width), BF)],
        near=tuple(range(1, 8)),
        near_out=(0, 1, 2, 3),
        room=16,
        flops=4 * TAPS * channels * channels * width,
    )
    square_slots = gathered(squares, "cout")
    square_slots[0] = after(square_slots[0], coeff_second)

    smalls = [small_grads]
    small_outs = [shape((2, width), F32)] * 4 + [shape((CLASSES, width), F32)] * 2 + [shape((1, CLASSES), F32)] * 2
    small_outs += [shape((1, 1), F32)] * 2
    first_spec = pl.BlockSpec((1, channels, width), lambda tap: (tap, 0, 0))
    second_spec = pl.BlockSpec((1, width, channels), lambda tap: (tap, 0, 0))
    pair = [first_spec, second_spec]
    first_like, second_like = shape(w_first.shape, F32), shape(w_second.shape, F32)

    def whole(leaf):
        return pl.BlockSpec(leaf.shape, lambda tap: (0,) * len(leaf.shape))

    def update(*refs):
        at = [0]

        def take(number):
            at[0] += number
            return refs[at[0] - number : at[0]]

        update_kernel(
            take(groups), take(2), take(2), take(2), take(2), take(len(smalls)),
            take(2), take(2), take(2), take(len(small_outs) - 2), take(2),
        )

    results = pl.pallas_call(
        update,
        grid=(TAPS,),
        in_specs=[pl.BlockSpec(memory_space=pltpu.VMEM)] * (groups + 8 + len(smalls)),
        out_specs=pair * 3 + [whole(leaf) for leaf in small_outs],
        out_shape=[first_like, second_like] * 3 + small_outs,
        compiler_params=pltpu.CompilerParams(vmem_limit_bytes=16 * 1024 * 1024),
    )(
        *square_slots, *weights, *means, *squares_old,
        first_grad, second_grad, *smalls,
    )
    (first_new, second_new, first_mean_new, second_mean_new, first_square_new, second_square_new,
     norm_first_mean, norm_first_square, norm_second_mean, norm_second_square,
     head_mean_new, head_square_new, bias_mean_new, bias_square_new, grad_norm, loss_total) = results
    return (
        loss_total.reshape(()),
        grad_norm.reshape(()),
        first_new,
        first_mean_new,
        first_square_new,
        second_new,
        second_mean_new,
        second_square_new,
        norm_first_mean,
        norm_first_square,
        norm_second_mean,
        norm_second_square,
        head_mean_new.T,
        head_square_new.T,
        bias_mean_new[0],
        bias_square_new[0],
        scales_first_new.reshape(scales_first.shape),
        scales_second_new,
    )


def solution(mesh):
    return jax.shard_map(
        local,
        mesh=mesh,
        in_specs=(
            P(None, ("dp", "cin"), None),
            P(None, ("dp", "cin")),
            P(("dp", "cin")),
            P(None, None, "cout"),
            P(None, "cout", None),
            P(None, "cout"),
            P("cout", None),
            P(),
            P(),
            P(None, None, "cout"),
            P(None, "cout", None),
            P(None, None, "cout"),
            P(None, None, "cout"),
            P(None, "cout", None),
            P(None, "cout", None),
            P(None, "cout"),
            P(None, "cout"),
            P("cout", None),
            P("cout", None),
            P(),
            P(),
        ),
        out_specs=(
            P(),
            P(),
            P(None, None, "cout"),
            P(None, None, "cout"),
            P(None, None, "cout"),
            P(None, "cout", None),
            P(None, "cout", None),
            P(None, "cout", None),
            P(None, "cout"),
            P(None, "cout"),
            P(None, "cout"),
            P(None, "cout"),
            P("cout", None),
            P("cout", None),
            P(),
            P(),
            P(None, None, "cout"),
            P(None, "cout", None),
        ),
        check_vma=False,
    )
```

```python
import functools
import math

import jax
import jax.numpy as jnp
from jax import lax
from jax.experimental import pallas as pl
from jax.experimental.pallas import tpu as pltpu
from jax.sharding import PartitionSpec as P

CLASSES = 10
SIDE = 4
PIX = 16
TAPS = 9
STEP = 10
LANES = 128

EPS_NORM = 1e-05
SCALE_DECAY = 0.95
DAMPING = 0.001
CLIP_NORM = 1.0
LEARN_RATE = 0.01
BETA_ONE = 0.9
BETA_TWO = 0.999
ADAM_EPS = 1e-08
WEIGHT_DECAY = 0.01
SMOOTH = 0.1
OFFSETS = [(row_step, col_step) for row_step in (-1, 0, 1) for col_step in (-1, 0, 1)]
EVERY = ("dp", "cout", "cin")
BF = jnp.bfloat16
F32 = jnp.float32
PRECISE = lax.Precision.HIGHEST
NN = (((1,), (0,)), ((), ()))
NT = (((1,), (1,)), ((), ()))
TN = (((0,), (0,)), ((), ()))


def matmul(left, right, dims=NN, precision=None):
    return lax.dot_general(
        left, right, dims, precision=precision, preferred_element_type=F32
    )


def runs(row_step, col_step, count):
    low, high = max(0, -col_step), min(SIDE, SIDE - col_step)
    found = []
    for row in range(max(0, -row_step), min(SIDE, SIDE - row_step)):
        to_row = (row * SIDE + low) * count
        from_row = ((row + row_step) * SIDE + low + col_step) * count
        length = (high - low) * count
        if found and found[-1][0] + found[-1][2] == to_row and found[-1][1] + found[-1][2] == from_row:
            found[-1] = (found[-1][0], found[-1][1], found[-1][2] + length)
        else:
            found.append((to_row, from_row, length))
    return found


class Late:
    def __init__(self, ref, copy):
        self.ref, self.copy, self.shape = ref, copy, ref.shape
        copy.start()

    def settle(self):
        if self.copy is not None:
            self.copy.wait()
        self.copy = None

    def __getitem__(self, index):
        self.settle()
        return self.ref[index]


class Result:
    def __init__(self, ref, copy):
        self.ref, self.copy, self.shape, self.sent = ref, copy, ref.shape, False

    def __getitem__(self, index):
        return self.ref[index]

    def __setitem__(self, index, values):
        self.ref[index] = values

    def send(self):
        if not self.sent:
            self.copy.start()
        self.sent = True


def call(kernel, outs, args, scratch=(), scalars=1, near=(), raw=(), near_out=(), flops=0, room=60):
    n_in, n_out = len(args), len(outs)
    copied = [at for at in range(scalars, n_in) if at not in near and at not in raw]
    copied_out = [at for at in range(n_out) if at not in near_out]

    def body(*refs):
        ins, results = list(refs[:n_in]), list(refs[n_in : n_in + n_out])
        rest = refs[n_in + n_out :]
        held, held_out = rest[: len(copied)], rest[len(copied) : len(copied) + len(copied_out)]
        own, arrived = rest[len(copied) + len(copied_out) : -1], rest[-1]
        for nth, at in enumerate(copied):
            ins[at] = Late(held[nth], pltpu.make_async_copy(ins[at], held[nth], arrived.at[nth]))
        for nth, at in enumerate(copied_out):
            copy = pltpu.make_async_copy(held_out[nth], results[at], arrived.at[len(copied) + nth])
            results[at] = Result(held_out[nth], copy)
        kernel(*ins, *results, *own)
        for at in copied:
            ins[at].settle()
        for at in copied_out:
            results[at].send()
        for at in copied_out:
            results[at].copy.wait()

    specs = [pl.BlockSpec(memory_space=pltpu.SMEM)] * scalars
    specs += [
        pl.BlockSpec(memory_space=pltpu.VMEM if at in near else pltpu.HBM) for at in range(scalars, n_in)
    ]
    moved = sum(math.prod(a.shape) * a.dtype.itemsize for a in list(args) + list(outs))
    return pl.pallas_call(
        body,
        out_shape=list(outs),
        in_specs=specs,
        out_specs=[
            pl.BlockSpec(memory_space=pltpu.VMEM if at in near_out else pltpu.HBM) for at in range(n_out)
        ],
        scratch_shapes=[pltpu.VMEM(args[at].shape, args[at].dtype) for at in copied]
        + [pltpu.VMEM(outs[at].shape, outs[at].dtype) for at in copied_out]
        + list(scratch)
        + [pltpu.SemaphoreType.DMA((max(1, len(copied) + len(copied_out)),))],
        compiler_params=pltpu.CompilerParams(vmem_limit_bytes=room * 1024 * 1024),
        cost_estimate=pl.CostEstimate(flops=flops, bytes_accessed=moved, transcendentals=0),
    )(*args)


def shape(dims, dtype):
    return jax.ShapeDtypeStruct(dims, dtype)


def gelu_parts(values):
    rate = math.sqrt(2.0 / math.pi)
    bend = jnp.tanh(rate * (values + 0.044715 * values * values * values))
    share = 0.5 * (1.0 + bend)
    slope = share + 0.5 * values * (1.0 - bend * bend) * rate * (1.0 + 0.134145 * values * values)
    return values * share, slope


def fill_mask(masks_ref, mask_ref):
    count = masks_ref.shape[1]
    same = lax.broadcasted_iota(jnp.int32, (count, count), 0) == lax.broadcasted_iota(
        jnp.int32, (count, count), 1
    )
    for pixel in range(PIX):
        row = masks_ref[pixel : pixel + 1, :].astype(F32)
        column = jnp.sum(jnp.where(same, row, 0.0), axis=1, keepdims=True)
        mask_ref[pixel * count : (pixel + 1) * count, :] = jnp.broadcast_to(column, (count, LANES))


def fill_inputs(images_ref, mask_ref, inputs_ref):
    low = mask_ref[...].astype(BF)
    for lane in range(0, images_ref.shape[1], LANES):
        inputs_ref[:, lane : lane + LANES] = images_ref[:, lane : lane + LANES] * low


def first_kernel(
    groups, place_ref, images_ref, masks_ref, weight_ref,
    sum_ref, all_mask_ref, stats_ref, own_mask_ref, mask_ref, inputs_ref, low_ref, wide_ref, arrived,
):
    count = masks_ref.shape[1]
    part = count // groups
    me = place_ref[0]
    copies = [
        pltpu.make_async_copy(weight_ref.at[at : at + 3], wide_ref.at[at : at + 3], arrived.at[at // 3])
        for at in range(0, TAPS, 3)
    ]
    for copy in copies:
        copy.start()
    fill_mask(masks_ref, mask_ref)
    fill_inputs(images_ref, mask_ref, inputs_ref)
    all_mask_ref[...] = mask_ref[...].astype(BF)
    all_mask_ref.send()
    for pixel in range(PIX):
        own = pl.multiple_of(pixel * count + me * part, part)
        own_mask_ref[pixel * part : (pixel + 1) * part, :] = mask_ref[pl.ds(own, part), :]
    own_mask_ref.send()
    for tap in range(TAPS):
        if tap % 3 == 0:
            copies[tap // 3].wait()
        low_ref[:, tap * LANES : (tap + 1) * LANES] = wide_ref[tap].astype(BF)
    sum_ref[...] = jnp.zeros(sum_ref.shape, F32)
    for tap in range(0, TAPS, 2):
        taps = min(2, TAPS - tap)
        product = matmul(inputs_ref[...], low_ref[:, tap * LANES : (tap + taps) * LANES])
        for nth in range(taps):
            for to_row, from_row, length in runs(*OFFSETS[tap + nth], count):
                sum_ref[to_row : to_row + length, :] += product[
                    from_row : from_row + length, nth * LANES : (nth + 1) * LANES
                ]
    sum_ref.send()
    mask = mask_ref[...]
    total = sum_ref[...]
    masked = total * mask
    tile = jnp.concatenate(
        [
            jnp.sum(masked, axis=0, keepdims=True),
            jnp.sum(masked * total, axis=0, keepdims=True),
            jnp.sum(mask, axis=0, keepdims=True),
            jnp.zeros((5, LANES), F32),
        ],
        axis=0,
    )
    stats_ref[...] = jnp.broadcast_to(tile[None], stats_ref.shape)


def first_norm_kernel(
    place_ref, got_ref, first_ref, mask_ref, params_ref, head_ref, send_refs, kept_ref, hidden_ref, scaled_ref
):
    total = total_of(got_ref)
    kept = total[2:3, :]
    mean = total[0:1, :] / kept
    rstd = lax.rsqrt(total[1:2, :] / kept - mean * mean + EPS_NORM)
    kept_ref[...] = jnp.broadcast_to(kept, kept_ref.shape)
    gain, shift = params_ref[0:1, :], params_ref[1:2, :]
    count = first_ref.shape[0] // PIX
    part = count // len(send_refs)
    scaled = (first_ref[...] - mean) * rstd
    value, _ = gelu_parts(gain * scaled + shift)
    hidden_ref[...] = (value * mask_ref[...].astype(F32)).astype(BF)
    scaled_ref[...] = scaled.astype(BF)
    lines = [head_ref[...]]
    for line in (rstd, gain, shift):
        high = line.astype(BF).astype(F32)
        lines += [high, line - high]
    extra = jnp.concatenate(lines, axis=0).astype(BF)
    rows = PIX * part
    for step, send_ref in enumerate(send_refs):
        for pixel in range(PIX):
            base = pl.ds(pl.multiple_of(pixel * count + (place_ref[0] ^ step) * part, part), part)
            send_ref[pixel * part : (pixel + 1) * part, :] = hidden_ref[base, :]
            send_ref[rows + pixel * part : rows + (pixel + 1) * part, :] = scaled_ref[base, :]
        send_ref[2 * rows : 2 * rows + 16, :] = extra


def hidden_kernel(place_ref, slot_refs, mask_ref, hidden_ref):
    rows = hidden_ref.shape[0]
    for step, slot_ref in enumerate(slot_refs):
        lanes = pl.ds(pl.multiple_of((place_ref[0] ^ step) * LANES, LANES), LANES)
        hidden_ref[:, lanes] = slot_ref[0:rows, :]
    hidden_ref[:, len(slot_refs) * LANES :] = mask_ref[...].astype(BF)


def gather_kernel(place_ref, slot_refs, kept_ref, scaled_ref, norm_ref, head_ref):
    rows = scaled_ref.shape[0]
    norm_ref[0:1, :] = jnp.zeros((1, norm_ref.shape[1]), F32)
    norm_ref[5:8, :] = jnp.zeros((3, norm_ref.shape[1]), F32)
    for step, slot_ref in enumerate(slot_refs):
        lanes = pl.ds(pl.multiple_of((place_ref[0] ^ step) * LANES, LANES), LANES)
        scaled_ref[:, lanes] = slot_ref[rows : 2 * rows, :]
        extra = slot_ref[2 * rows : 2 * rows + 16, :].astype(F32)
        line = lax.broadcasted_iota(jnp.int32, (16, LANES), 0)
        head_ref[:, lanes] = jnp.where(line < CLASSES, extra, 0.0).astype(BF)
        for at in range(3):
            norm_ref[at + 1 : at + 2, lanes] = (
                extra[CLASSES + 2 * at : CLASSES + 2 * at + 1, :] + extra[CLASSES + 2 * at + 1 : CLASSES + 2 * at + 2, :]
            )
        norm_ref[4:5, lanes] = kept_ref[0:1, :]


def second_kernel(
    place_ref, own_ref, other_ref, params_ref, slot_refs,
    mine_ref, theirs_ref, stats_ref, inputs_ref, weight_ref, sum_ref, arrived,
):
    me = place_ref[0]
    rows = own_ref.shape[0]
    part = rows // PIX
    depth, half = slot_refs[0].shape[1:]
    copies = []
    for step, slot_ref in enumerate(slot_refs):
        span = pl.ds(pl.multiple_of((me ^ step) * depth, depth), depth)
        copies.append(pltpu.make_async_copy(slot_ref, weight_ref.at[:, span, :], arrived.at[step]))
        copies[-1].start()
    channels = inputs_ref.shape[1]
    inputs_ref[0:rows, :] = own_ref[:, 0:channels]
    inputs_ref[rows : 2 * rows, :] = other_ref[:, 0:channels]
    sum_ref[...] = jnp.zeros_like(sum_ref)
    for copy in copies:
        copy.wait()
    for tap in range(TAPS):
        product = matmul(inputs_ref[...], weight_ref[tap])
        for to_row, from_row, length in runs(*OFFSETS[tap], part):
            for base in (0, rows):
                sum_ref[base + to_row : base + to_row + length, :] += product[
                    base + from_row : base + from_row + length, :
                ]
    mine_ref[...] = sum_ref[0:rows, :]
    theirs_ref[...] = sum_ref[rows : 2 * rows, :]
    lines = [[], []]
    for lane in range(0, half, LANES):
        first = square = None
        for base, ref in ((0, own_ref), (rows, other_ref)):
            total = sum_ref[base : base + rows, lane : lane + LANES]
            masked = total * ref[:, channels : channels + LANES].astype(F32)
            first_part = jnp.sum(masked, axis=0, keepdims=True)
            square_part = jnp.sum(masked * total, axis=0, keepdims=True)
            first = first_part if first is None else first + first_part
            square = square_part if square is None else square + square_part
        lines[0].append(first)
        lines[1].append(square)
    spare = 8 - 2 * (half // LANES) - 2
    tile = jnp.concatenate(
        lines[0] + lines[1] + [params_ref[2:4, :], jnp.zeros((spare, LANES), F32)], axis=0
    )
    stats_ref[...] = jnp.broadcast_to(tile[None], stats_ref.shape)


def head_kernel(
    sizes, place_ref, mine_ref, got_ref_rows, got_ref, norm_first_ref, mask_ref, head_ref, bias_ref, labels_ref,
    wide_ref, norm_ref, dz_ref, sums_ref, head_out_ref, slope_ref, pooled_ref, weight_ref,
):
    count_dp, groups, count_cin = sizes
    side = place_ref[1]
    rows, half = mine_ref.shape
    part = rows // PIX
    blocks = half // LANES
    wide_ref[:, pl.ds(pl.multiple_of(side * half, half), half)] = mine_ref[...]
    wide_ref[:, pl.ds(pl.multiple_of((1 - side) * half, half), half)] = got_ref_rows[...]
    totals = [None, None]
    for source in range(count_dp * groups * count_cin):
        which = source % count_cin % 2
        tile = got_ref[source]
        totals[which] = tile if totals[which] is None else totals[which] + tile
    kept = norm_first_ref[4:5, 0:LANES]
    mask = mask_ref[...]
    for group in range(groups):
        lanes = slice(group * LANES, (group + 1) * LANES)
        total, line = totals[group // blocks], group % blocks
        mean = total[line : line + 1, :] / kept
        rstd = lax.rsqrt(total[blocks + line : blocks + line + 1, :] / kept - mean * mean + EPS_NORM)
        single = got_ref[group * count_cin]
        gain = single[2 * blocks : 2 * blocks + 1, :]
        shift = single[2 * blocks + 1 : 2 * blocks + 2, :]
        norm_ref[0:1, lanes] = mean
        norm_ref[1:2, lanes] = rstd
        norm_ref[2:3, lanes] = gain
        norm_ref[3:4, lanes] = shift
        norm_ref[4:8, lanes] = jnp.broadcast_to(kept, (4, LANES))
        value, slope = gelu_parts(gain * ((wide_ref[:, lanes] - mean) * rstd) + shift)
        slope_ref[:, lanes] = slope * mask * (1.0 / PIX)
        pooled_ref[:, lanes] = jnp.sum((value * mask).reshape(PIX, part, LANES), axis=0) * (1.0 / PIX)
    wide_ref.send()
    norm_ref.send()
    weight_ref[0:16, :] = head_ref[...]
    weight_ref[16:LANES, :] = jnp.zeros((LANES - 16, weight_ref.shape[1]), BF)
    pooled = pooled_ref[...].astype(BF)
    head = weight_ref[...]
    class_index = lax.broadcasted_iota(jnp.int32, (part, LANES), 1)
    logits = matmul(pooled, head, NT) + bias_ref[...]
    logits = jnp.where(class_index < CLASSES, logits, -1e30)
    logits = logits - jnp.max(logits, axis=1, keepdims=True)
    log_probs = logits - jnp.log(jnp.sum(jnp.exp(logits), axis=1, keepdims=True))
    wanted = jnp.where(class_index == labels_ref[...], 1.0 - SMOOTH, 0.0) + SMOOTH / CLASSES
    wanted = jnp.where(class_index < CLASSES, wanted, 0.0)
    loss = -jnp.sum(jnp.sum(wanted * log_probs, axis=1, keepdims=True), axis=0, keepdims=True)
    logit_grad = jnp.exp(log_probs) - wanted
    head_grad = matmul(logit_grad, pooled.astype(F32), TN, PRECISE)
    pooled_grad = matmul(logit_grad, head.astype(F32), NN, PRECISE)
    extra = jnp.sum(logit_grad, axis=0, keepdims=True)
    extra = jnp.where(class_index[0:1, :] == CLASSES, loss, extra)
    line = lax.broadcasted_iota(jnp.int32, (16, LANES), 0)
    gains, shifts = [], []
    for group in range(groups):
        lanes = slice(group * LANES, (group + 1) * LANES)
        head_out_ref[group] = jnp.where(line == CLASSES, extra, head_grad[0:16, lanes])
        spread = jnp.broadcast_to(pooled_grad[:, lanes][None], (PIX, part, LANES)).reshape(rows, LANES)
        dz = slope_ref[:, lanes] * spread
        dz_ref[:, lanes] = dz
        scaled = (wide_ref[:, lanes] - norm_ref[0:1, lanes]) * norm_ref[1:2, lanes]
        gains.append(jnp.sum(dz * scaled, axis=0, keepdims=True))
        shifts.append(jnp.sum(dz, axis=0, keepdims=True))
    sums_ref[...] = jnp.broadcast_to(jnp.concatenate(gains + shifts, axis=0)[None], sums_ref.shape)


def total_of(got_ref):
    total = got_ref[0]
    for source in range(1, got_ref.shape[0]):
        total = total + got_ref[source]
    return total


def norm_back(scaled, dz, norm, mask, gain_grad, shift_grad):
    gain = norm[2:3, :]
    return norm[1:2, :] * (
        gain * dz - mask * (gain / norm[4:5, :]) * (shift_grad + scaled * gain_grad)
    )


def second_back_kernel(
    place_ref, dz_ref, wide_ref, norm_ref, got_ref, mask_ref, first_ref, norm_first_ref, head_ref, basis_ref, near_refs, far_refs,
    grad_ref, sums_out_ref, sums_ref, send_refs, part_ref, weight_ref, sum_ref, arrived,
):
    me, side = place_ref[0], place_ref[1]
    depth, half = near_refs[0].shape[1:]
    copies = {}
    for tap in range(0, TAPS, 3):
        for which, (refs, at) in enumerate(((near_refs, side), (far_refs, 1 - side))):
            lanes = pl.ds(pl.multiple_of(at * half, half), half)
            for step, slot_ref in enumerate(refs):
                span = pl.ds(pl.multiple_of((me ^ step) * depth, depth), depth)
                number = which * len(refs) + step
                copies[tap, number] = pltpu.make_async_copy(
                    slot_ref.at[tap : tap + 3], weight_ref.at[tap : tap + 3, span, lanes], arrived.at[tap // 3, number]
                )
                copies[tap, number].start()
    total = total_of(got_ref)
    sums_out_ref[...] = total
    groups = total.shape[0] // 2
    mask = mask_ref[...]
    for group in range(groups):
        lanes = slice(group * LANES, (group + 1) * LANES)
        norm = norm_ref[:, lanes]
        grad_ref[:, lanes] = norm_back(
            (wide_ref[:, lanes] - norm[0:1, :]) * norm[1:2, :], dz_ref[:, lanes], norm, mask,
            total[group : group + 1, :], total[groups + group : groups + group + 1, :],
        ).astype(BF)
    grad_ref.send()
    sums_out_ref.send()
    rows, channels = grad_ref.shape
    part = rows // PIX
    sum_ref[...] = jnp.zeros_like(sum_ref)
    for tap in range(TAPS):
        if tap % 3 == 0:
            for number in range(2 * len(near_refs)):
                copies[tap, number].wait()
        product = matmul(grad_ref[...], weight_ref[tap], NT)
        row_step, col_step = OFFSETS[tap]
        for to_row, from_row, length in runs(-row_step, -col_step, part):
            sum_ref[to_row : to_row + length, :] += product[from_row : from_row + length, :]
    gains, shifts = [], []
    for lane in range(0, channels, LANES):
        lanes = slice(lane, lane + LANES)
        norm = norm_first_ref[:, lanes]
        scaled = first_ref[:, lanes].astype(F32)
        _, slope = gelu_parts(norm[2:3, :] * scaled + norm[3:4, :])
        dz = slope * mask * sum_ref[:, lanes]
        part_ref[:, lanes] = (norm[1:2, :] * norm[2:3, :] * dz).astype(BF)
        gains.append(jnp.sum(dz * scaled, axis=0, keepdims=True))
        shifts.append(jnp.sum(dz, axis=0, keepdims=True))
    sum_ref[...] = matmul(part_ref[...], basis_ref[...])
    send_columns(me, sum_ref, send_refs)
    count_dp, _, count_cin = sums_ref.shape[:3]
    for group in range(groups):
        tile = jnp.concatenate(gains + shifts + [head_ref[group], jnp.zeros((8, LANES), F32)], axis=0)
        tile = tile.astype(BF)
        for far in range(count_dp):
            for near in range(count_cin):
                sums_ref[far, group, near] = tile


def first_products_kernel(
    place_ref, got_ref, norm_ref, mask_ref, basis_ref, old_refs, big_refs, part_refs, scaled_refs,
    kept_ref, sent_ref, sums_ref, small_ref, left_ref, right_ref, slot_ref, column_ref, mask_slot_ref, out_ref,
):
    me = place_ref[0]
    rows, width = part_refs[0].shape
    part = rows // PIX
    count = mask_ref.shape[0] // PIX
    whole = got_ref[0].astype(F32)
    for source in range(1, got_ref.shape[0]):
        whole = whole + got_ref[source].astype(F32)
    sums_ref[...] = whole[0:8, :]
    small_ref[...] = jnp.zeros(small_ref.shape, F32)
    small_ref[8:24, :] = whole[8:24, :]
    for at, row in enumerate((24, 28, 32, 48, 64, 65)):
        lines, lanes = old_refs[at].shape
        small_ref[row : row + lines, 0:lanes] = old_refs[at][...]
    groups = len(part_refs)
    column_ref[...] = basis_ref[:, pl.ds(pl.multiple_of(me * width, width), width)]
    rates, shifts = [], []
    for group in range(groups):
        lanes = slice(group * LANES, (group + 1) * LANES)
        scale = norm_ref[1:2, lanes] * norm_ref[2:3, lanes] / norm_ref[4:5, lanes]
        rates.append(scale * whole[group : group + 1, :])
        shifts.append(scale * whole[groups + group : groups + group + 1, :])
    rate = jnp.concatenate(rates, axis=1)
    shift = jnp.broadcast_to(jnp.concatenate(shifts, axis=1), (8, groups * LANES))
    fixed = matmul(shift, column_ref[...].astype(F32), NN, PRECISE)[0:1, :]
    for step in range(groups):
        for pixel in range(PIX):
            base = pl.ds(pl.multiple_of(pixel * count + (me ^ step) * part, part), part)
            mask_slot_ref[pixel * part : (pixel + 1) * part, :] = mask_ref[base, :]
        moved = matmul((scaled_refs[step][...].astype(F32) * rate).astype(BF), column_ref[...])
        slot_ref[step] = (
            part_refs[step][...].astype(F32) - mask_slot_ref[...].astype(F32) * (fixed + moved)
        ).astype(BF)
    taps_kernel(-1, big_refs, [slot_ref.at[step] for step in range(groups)], out_ref, left_ref, right_ref)
    half = kept_ref.shape[0]
    sent_ref[...] = out_ref[pl.ds(pl.multiple_of((1 - place_ref[1]) * half, half), half), :]
    kept_ref[...] = out_ref[pl.ds(pl.multiple_of(place_ref[1] * half, half), half), :]


def left_second_kernel(place_ref, norm_ref, mask_ref, basis_ref, scaled_refs, left_refs, column_ref, wide_ref):
    me = place_ref[0]
    rows, width = left_refs[0].shape
    part = rows // PIX
    count = mask_ref.shape[0] // PIX
    column_ref[...] = basis_ref[:, pl.ds(pl.multiple_of(me * width, width), width)]
    for step, scaled_ref in enumerate(scaled_refs):
        mask = jnp.concatenate(
            [
                mask_ref[pl.ds(pl.multiple_of(pixel * count + (me ^ step) * part, part), part), :]
                for pixel in range(PIX)
            ],
            axis=0,
        ).astype(F32)
        for lane in range(0, wide_ref.shape[1], LANES):
            lanes = slice(lane, lane + LANES)
            value, _ = gelu_parts(
                norm_ref[2:3, lanes] * scaled_ref[:, lanes].astype(F32) + norm_ref[3:4, lanes]
            )
            wide_ref[:, lanes] = (value * mask).astype(BF)
        left_refs[step][...] = matmul(wide_ref[...], column_ref[...]).astype(BF)


def right_kernel(grad_ref, basis_ref, right_ref):
    right_ref[...] = jnp.transpose(matmul(grad_ref[...], basis_ref[...])).astype(BF)


def send_columns(me, product_ref, send_refs):
    for step, send_ref in enumerate(send_refs):
        lanes = pl.ds(pl.multiple_of((me ^ step) * LANES, LANES), LANES)
        send_ref[...] = product_ref[:, lanes].astype(BF)


def left_first_kernel(place_ref, images_ref, masks_ref, basis_ref, left_ref, mask_ref, inputs_ref, part_ref):
    slots = left_ref.shape[0]
    count = masks_ref.shape[1]
    part = count // slots
    me = place_ref[0]
    fill_mask(masks_ref, mask_ref)
    fill_inputs(images_ref, mask_ref, inputs_ref)
    for step in range(slots):
        for pixel in range(PIX):
            base = pl.multiple_of(pixel * count + (me ^ step) * part, part)
            part_ref[pixel * part : (pixel + 1) * part, :] = inputs_ref[pl.ds(base, part), :]
        left_ref[step] = jnp.transpose(matmul(part_ref[...], basis_ref[...])).astype(BF)


def pick_kernel(own_ref, full_ref, kept_ref, sent_ref):
    half = kept_ref.shape[0]
    kept_ref[...] = full_ref[pl.ds(pl.multiple_of(own_ref[0] * half, half), half), :]
    sent_ref[...] = full_ref[pl.ds(pl.multiple_of((1 - own_ref[0]) * half, half), half), :]


def split_kernel(own_ref, here_ref, came_ref, kept_ref, sent_ref):
    half = kept_ref.shape[0]
    for which, ref in ((own_ref[0], kept_ref), (1 - own_ref[0], sent_ref)):
        rows = pl.ds(pl.multiple_of(which * half, half), half)
        ref[...] = (here_ref[rows, :].astype(F32) + came_ref[rows, :].astype(F32)).astype(BF)


def merge_kernel(own_ref, here_ref, came_ref, out_ref):
    rows = here_ref.shape[0]
    for choice in range(2):

        @pl.when(own_ref[0] == choice)
        def _():
            out_ref[choice * rows : (choice + 1) * rows, :] = here_ref[...]
            out_ref[(1 - choice) * rows : (2 - choice) * rows, :] = came_ref[...]


def taps_kernel(sign, big_refs, small_refs, out_ref, left_ref, right_ref):
    rows, width = small_refs[0].shape
    channels = big_refs[0].shape[0]
    part = rows // PIX
    right_ref[...] = jnp.zeros_like(right_ref)
    for slot, (big_ref, small_ref) in enumerate(zip(big_refs, small_refs)):
        base = slot * rows
        left_ref[:, base : base + rows] = big_ref[...]
        for tap, (row_step, col_step) in enumerate(OFFSETS):
            for to_row, from_row, length in runs(sign * row_step, sign * col_step, part):
                right_ref[base + to_row : base + to_row + length, tap * width : (tap + 1) * width] = (
                    small_ref[from_row : from_row + length, :]
                )
    for tap in range(0, TAPS, 2):
        taps = min(2, TAPS - tap)
        product = matmul(left_ref[...], right_ref[:, tap * width : (tap + taps) * width])
        for nth in range(taps):
            out_ref[(tap + nth) * channels : (tap + nth + 1) * channels, :] = product[
                :, nth * width : (nth + 1) * width
            ].astype(BF)


def ratio_kernel(own_refs, scales_ref, coeff_ref, ratio_ref):
    coeff = None
    for ref in own_refs:
        coeff = ref[...].astype(F32) if coeff is None else coeff + ref[...].astype(F32)
    scales = SCALE_DECAY * scales_ref[...] + (1.0 - SCALE_DECAY) * coeff * coeff
    coeff_ref[...] = coeff.astype(BF)
    ratio_ref[...] = (coeff / (scales + DAMPING)).astype(BF)


def middle_kernel(basis_ref, slot_refs, out_ref):
    width = slot_refs[0].shape[1]
    ratio = jnp.concatenate([ref[...] for ref in slot_refs], axis=1)
    out_ref[...] = matmul(ratio, basis_ref[...], NT).astype(BF)


def scales_kernel(turned, coeff_ref, scales_ref, out_ref):
    taps = out_ref.shape[0]
    rows = coeff_ref.shape[0] // taps
    for tap in range(taps):
        coeff = coeff_ref[tap * rows : (tap + 1) * rows, :].astype(F32)
        if turned:
            coeff = jnp.transpose(coeff)
        out_ref[tap] = SCALE_DECAY * scales_ref[tap] + (1.0 - SCALE_DECAY) * coeff * coeff


def wide_ratio_kernel(place_ref, coeff_ref, scales_ref, scales_out_ref, ratio_ref):
    half = ratio_ref.shape[0]
    rows = pl.ds(pl.multiple_of(place_ref[1] * half, half), half)
    coeff = coeff_ref[...].astype(F32)
    scales_out_ref[...] = SCALE_DECAY * scales_ref[...] + (1.0 - SCALE_DECAY) * coeff * coeff
    scales_out_ref.send()
    ratio_ref[...] = (coeff_ref[rows, :].astype(F32) / (scales_out_ref[rows, :] + DAMPING)).astype(BF)


def add_squares(total, values):
    return total + jnp.sum((values * values).reshape(-1, 8, LANES), axis=0)


def restore_kernel(
    place_ref, basis_in_ref, middle_first_ref, basis_out_ref, middle_second_ref, sums_first_ref, sums_second_ref,
    old_ref, first_ref, second_ref, squares_ref, small_ref, stack_ref,
):
    me = place_ref[0]
    channels = basis_in_ref.shape[0]
    total = jnp.zeros((8, LANES), F32)
    for tap in range(TAPS):
        product = matmul(
            middle_second_ref[tap * channels : (tap + 1) * channels, :], basis_out_ref[...], (((0,), (1,)), ((), ()))
        )
        second_ref[tap] = product.astype(BF)
        for lane in range(0, channels, LANES):
            total = add_squares(total, product[:, lane : lane + LANES])
    for tap in range(TAPS):
        stack_ref[:, tap * LANES : (tap + 1) * LANES] = middle_first_ref[
            tap * channels : (tap + 1) * channels, :
        ]
    for tap in range(0, TAPS, 2):
        taps = min(2, TAPS - tap)
        product = matmul(basis_in_ref[...], stack_ref[:, tap * LANES : (tap + taps) * LANES])
        for nth in range(taps):
            block = product[:, nth * LANES : (nth + 1) * LANES]
            first_ref[tap + nth] = block.astype(BF)
            total = add_squares(total, block)
    groups = sums_first_ref.shape[0] // 2
    row = lax.broadcasted_iota(jnp.int32, (8, LANES), 0)
    mine = (row == me) | (row == me + groups)
    for ref in (sums_first_ref, sums_second_ref):
        total = total + jnp.where(mine, ref[...] * ref[...], 0.0)
    line = lax.broadcasted_iota(jnp.int32, (16, LANES), 0)
    lane = lax.broadcasted_iota(jnp.int32, (16, LANES), 1)
    counted = (line < CLASSES) | ((line == CLASSES) & (lane < CLASSES) & (me == 0))
    head = jnp.where(counted, old_ref[8:24, :], 0.0)
    small_ref[...] = old_ref[...]
    for at, ref in enumerate((sums_first_ref, sums_second_ref)):
        small_ref[2 * at : 2 * at + 1, :] = ref[pl.ds(me, 1), :]
        small_ref[2 * at + 1 : 2 * at + 2, :] = ref[pl.ds(me + groups, 1), :]
    squares_ref[...] = add_squares(total, head)


def update_kernel(
    square_refs, weight_refs, mean_refs, square_moment_refs, grad_refs, small_refs,
    weight_outs, mean_outs, square_outs, small_outs, scalar_outs, norm_ref,
):
    @pl.when(pl.program_id(0) == 0)
    def _():
        parts = [ref[...] for ref in square_refs]
        while len(parts) > 1:
            parts = [parts[at] + parts[at + 1] for at in range(0, len(parts), 2)]
        total = jnp.sum(jnp.sum(parts[0], axis=1, keepdims=True), axis=0, keepdims=True)
        found = jnp.sqrt(total)
        norm_ref[0:1, :] = jnp.broadcast_to(found, (1, LANES))
        norm_ref[1:2, :] = jnp.broadcast_to(CLIP_NORM / jnp.maximum(found, CLIP_NORM), (1, LANES))

    grad_norm, factor = norm_ref[0:1, 0:1], norm_ref[1:2, 0:1]

    def moments(gradient, mean_old, square_old):
        mean_new = BETA_ONE * mean_old + (1.0 - BETA_ONE) * gradient
        square_new = BETA_TWO * square_old + (1.0 - BETA_TWO) * gradient * gradient
        return mean_new, square_new

    taps = mean_outs[0].shape[0]
    for at in range(len(weight_refs)):
        for nth in range(taps):
            tap = pl.program_id(0) * taps + nth
            gradient = grad_refs[at][tap].astype(F32) * factor
            mean_new, square_new = moments(gradient, mean_refs[at][tap], square_moment_refs[at][tap])
            mean_outs[at][nth] = mean_new
            square_outs[at][nth] = square_new
            square_hat = square_new * (1.0 / (1.0 - BETA_TWO**STEP))
            size = square_hat * lax.rsqrt(square_hat) + ADAM_EPS
            step = mean_new * (LEARN_RATE / (1.0 - BETA_ONE**STEP)) * pl.reciprocal(size, approx=True)
            weight_outs[at][nth] = weight_refs[at][tap] * (1.0 - LEARN_RATE * WEIGHT_DECAY) - step

    @pl.when(pl.program_id(0) == 0)
    def _():
        norm_out, loss_out = scalar_outs
        norm_out[...] = grad_norm
        (small,) = small_refs
        loss_out[...] = small[8 + CLASSES : 9 + CLASSES, CLASSES : CLASSES + 1]
        results = moments(small[0:4, :] * factor, small[24:28, :], small[28:32, :])
        for at in range(2):
            small_outs[at][...] = results[at][0:2, :]
            small_outs[2 + at][...] = results[at][2:4, :]
        results = moments(
            small[8 : 8 + CLASSES, :] * factor, small[32 : 32 + CLASSES, :], small[48 : 48 + CLASSES, :]
        )
        for at in range(2):
            small_outs[4 + at][...] = results[at]
        lanes = slice(0, CLASSES)
        results = moments(small[8 + CLASSES : 9 + CLASSES, lanes] * factor, small[64:65, lanes], small[65:66, lanes])
        for at in range(2):
            small_outs[6 + at][...] = results[at]


def swap(values, axis, step):
    count = lax.axis_size(axis)
    return lax.ppermute(values, axis, [(here, here ^ step) for here in range(count)])


def gathered(values, axis):
    return [values] + [swap(values, axis, step) for step in range(1, lax.axis_size(axis))]


def exchanged(sends, axis):
    return [sends[0]] + [swap(sends[step], axis, step) for step in range(1, len(sends))]


def picked(values, index):
    return lax.dynamic_index_in_dim(values, index, 0, keepdims=False)


def after(values, *others):
    return lax.optimization_barrier((values,) + others)[0]


def tree_sum(slots):
    while len(slots) > 1:
        slots = [slots[at] + slots[at + 1] for at in range(0, len(slots), 2)]
    return slots[0]


def every_device(tiles):
    return lax.all_to_all(tiles, EVERY, 0, 0, tiled=True)


def bits_of(axis):
    return range(lax.axis_size(axis).bit_length() - 1)


def bit_of(axis, bit):
    return (lax.axis_index(axis) >> bit) & 1


def crossed(parts, axis, bit):
    return [parts[0], swap(parts[1], axis, 1 << bit)]


def halved(terms, axis, bit):
    rows, width = terms[0].shape
    own = bit_of(axis, bit)
    if rows // 2 % 16:
        total = joined(terms).reshape(2, rows // 2, width)
        return crossed([picked(total, own), picked(total, 1 - own)], axis, bit)
    half = shape((rows // 2, width), BF)
    parts = call(
        pick_kernel if len(terms) == 1 else split_kernel,
        [half, half],
        [own[None], *terms],
        near=tuple(range(1, 1 + len(terms))),
        near_out=(0, 1),
        room=16,
    )
    return crossed(parts, axis, bit)


def doubled(values, axis, bit):
    own = bit_of(axis, bit)
    rows, width = values.shape
    other = swap(values, axis, 1 << bit)
    (out,) = call(
        merge_kernel, [shape((2 * rows, width), BF)], [own[None], values, other], near=(1, 2), near_out=(0,), room=16
    )
    return out


def joined(terms):
    return terms[0] if len(terms) == 1 else (terms[0].astype(F32) + terms[1].astype(F32)).astype(BF)


def batch_gather(block, axes=("dp", "cin"), first=()):
    for order in reversed(first):
        block = doubled(block, *order)
    for axis in axes:
        for bit in reversed(bits_of(axis)):
            block = doubled(block, axis, bit)
    return block


def batch_rows(values):
    place = jnp.int32(0)
    for axis in ("cin", "dp"):
        for bit in bits_of(axis):
            place = place * 2 + ((lax.axis_index(axis) >> bit) & 1)
    rows = values.shape[0] // (lax.axis_size("dp") * lax.axis_size("cin"))
    return lax.dynamic_slice_in_dim(values, place * rows, rows, 0)


def local(
    images,
    masks,
    labels,
    w_first,
    w_second,
    norm_params,
    head_w,
    head_b,
    bases,
    scales_first,
    scales_second,
    w_first_mean,
    w_first_square,
    w_second_mean,
    w_second_square,
    norm_mean,
    norm_square,
    head_w_mean,
    head_w_square,
    head_b_mean,
    head_b_square,
):
    me = lax.axis_index("cout")
    side = lax.axis_index("cin") % 2
    place = jnp.stack([me, side]).astype(jnp.int32)
    sizes = tuple(lax.axis_size(name) for name in EVERY)
    groups = sizes[1]
    devices = sizes[0] * sizes[1] * sizes[2]
    channels = w_first.shape[1]
    width = w_first.shape[2]
    half = channels // 2
    count = images.shape[1]
    part = count // groups
    rows = PIX * part
    tile = shape((devices, 8, LANES), F32)
    wide = (rows, channels)
    basis_in_first, basis_out_first = bases[0, 0], bases[0, 1]
    basis_in_second, basis_out_second = bases[1, 0], bases[1, 1]
    bases_all = (basis_in_first, basis_out_first, basis_in_second, basis_out_second)

    piece = lax.dynamic_slice_in_dim(w_second, side * half, half, 2).astype(BF)
    own_labels = lax.dynamic_slice_in_dim(labels, me * part, part, 0)[:, None]
    bias_row = jnp.pad(head_b, (0, LANES - CLASSES))[None]

    flat_images = images.reshape(PIX * count, channels)
    first_out, all_mask, stats, mask = call(
        functools.partial(first_kernel, groups),
        [
            shape((PIX * count, width), F32),
            shape((PIX * count, LANES), BF),
            shape((sizes[0] * sizes[2], 8, LANES), F32),
            shape((rows, LANES), F32),
        ],
        [place, flat_images, masks, w_first],
        [
            pltpu.VMEM((PIX * count, LANES), F32),
            pltpu.VMEM((PIX * count, channels), BF),
            pltpu.VMEM((channels, TAPS * width), BF),
            pltpu.VMEM((TAPS, channels, width), F32),
            pltpu.SemaphoreType.DMA((3,)),
        ],
        near=(1, 2),
        raw=(3,),
        room=56,
        flops=2 * PIX * count * channels * width * TAPS,
    )
    got = lax.all_to_all(stats, ("dp", "cin"), 0, 0, tiled=True)
    (left_turned,) = call(
        left_first_kernel,
        [shape((groups, channels, rows), BF)],
        [place, after(flat_images, stats), masks, basis_in_first],
        [
            pltpu.VMEM((PIX * count, LANES), F32),
            pltpu.VMEM((PIX * count, channels), BF),
            pltpu.VMEM((rows, channels), BF),
        ],
        near=(1, 2, 3),
        room=20,
    )
    near_weights = [piece]
    for step in range(1, groups):
        ready = piece if step < groups - 1 else after(piece, stats)
        near_weights.append(swap(ready, "cout", step))
    first_mask = after(all_mask, left_turned, *near_weights[1:-1], *bases_all)
    *first_sends, kept = call(
        lambda *refs: first_norm_kernel(*refs[:6], refs[6 : 6 + groups], *refs[6 + groups :]),
        [shape((2 * rows + 16, width), BF)] * groups + [shape((8, LANES), F32)],
        [place, got, first_out, first_mask, norm_params, head_w.T],
        [pltpu.VMEM((PIX * count, LANES), BF), pltpu.VMEM((PIX * count, LANES), BF)],
        near_out=tuple(range(groups)),
    )
    def in_slots(values):
        return jnp.concatenate(
            [lax.dynamic_slice_in_dim(values, (me ^ step) * width, width, 1) for step in range(groups)], 1
        )

    def basis_rows(basis):
        return in_slots(lax.dynamic_slice_in_dim(basis, me * width, width, 0))

    scales_turned = batch_rows(
        jnp.swapaxes(after(scales_second, kept), 1, 2).reshape(TAPS * channels, width)
    )
    rows_first = basis_rows(after(basis_out_first, kept))
    rows_second = basis_rows(after(basis_in_second, kept))
    kept = after(kept, scales_turned, rows_first, rows_second)
    first_slots = exchanged(first_sends, "cout")
    (hidden,) = call(
        lambda *refs: hidden_kernel(refs[0], refs[1 : 1 + groups], *refs[1 + groups :]),
        [shape((rows, channels + LANES), BF)],
        [place, *first_slots, after(mask, kept)],
        near=tuple(range(1, 1 + groups)),
        near_out=(0,),
    )
    other_hidden = swap(hidden, "cin", 1)
    mine, theirs, stats = call(
        lambda *refs: second_kernel(*refs[:4], refs[4 : 4 + groups], *refs[4 + groups :]),
        [shape((rows, half), F32), shape((rows, half), F32), tile],
        [place, hidden, other_hidden, norm_params, *near_weights],
        [
            pltpu.VMEM((2 * rows, channels), BF),
            pltpu.VMEM((TAPS, channels, half), BF),
            pltpu.VMEM((2 * rows, half), F32),
            pltpu.SemaphoreType.DMA((groups,)),
        ],
        near=(1, 2),
        raw=tuple(range(4, 4 + groups)),
        flops=4 * rows * channels * half * TAPS,
    )
    scaled_first, norm_first, head_full = call(
        lambda *refs: gather_kernel(refs[0], refs[1 : 1 + groups], *refs[1 + groups :]),
        [shape(wide, BF), shape((8, channels), F32), shape((16, channels), BF)],
        [place, *first_slots, after(kept, mine)],
    )
    from_other = swap(theirs, "cin", 1)
    got_second = every_device(stats)
    far_weights = [swap(after(slot, mine), "cin", 1) for slot in near_weights]
    head_mask = after(mask, *far_weights)
    second_out, norm_second, dz_second, sums, head_blocks = call(
        functools.partial(head_kernel, sizes),
        [
            shape(wide, F32),
            shape((8, channels), F32),
            shape(wide, F32),
            tile,
            shape((groups, 16, width), F32),
        ],
        [place, mine, from_other, got_second, norm_first, head_mask, head_full, bias_row, own_labels],
        [
            pltpu.VMEM(wide, F32),
            pltpu.VMEM((part, channels), F32),
            pltpu.VMEM((LANES, channels), BF),
        ],
    )
    got = every_device(sums)
    scaled_slots = gathered(after(scaled_first, got_second), "cout")
    grad_second, sums_second, sums, *right_sends = call(
        lambda *refs: second_back_kernel(
            *refs[:10], refs[10 : 10 + groups], refs[10 + groups : 10 + 2 * groups],
            *refs[10 + 2 * groups : 13 + 2 * groups], refs[13 + 2 * groups : 13 + 3 * groups], *refs[13 + 3 * groups :]
        ),
        [shape(wide, BF), shape((8, LANES), F32), shape(sizes + (32, LANES), BF)] + [shape((rows, width), BF)] * groups,
        [
            place, dz_second, second_out, norm_second, got, after(mask, *scaled_slots), scaled_first,
            norm_first, head_blocks, basis_out_first, *near_weights, *far_weights,
        ],
        [
            pltpu.VMEM(wide, BF),
            pltpu.VMEM((TAPS, channels, channels), BF),
            pltpu.VMEM(wide, F32),
            pltpu.SemaphoreType.DMA((3, 2 * groups)),
        ],
        raw=tuple(range(10, 10 + 2 * groups)),
        flops=2 * rows * channels * channels * TAPS,
    )
    left_slots = call(
        lambda *refs: left_second_kernel(*refs[:4], refs[4 : 4 + groups], refs[4 + groups : 4 + 2 * groups], *refs[4 + 2 * groups :]),
        [shape((rows, width), BF)] * groups,
        [place, norm_first, after(all_mask, sums_second), basis_in_second, *scaled_slots],
        [pltpu.VMEM((channels, width), BF), pltpu.VMEM(wide, BF)],
    )
    (right_turned,) = call(
        right_kernel, [shape((channels, rows), BF)], [grad_second, basis_out_second], scalars=0
    )

    def products(sign, big, small, near=()):
        (out,) = call(
            lambda *refs: taps_kernel(sign, refs[:groups], refs[groups : 2 * groups], *refs[2 * groups :]),
            [shape((TAPS * channels, width), BF)],
            [*big, *small],
            [
                pltpu.VMEM((channels, groups * rows), BF),
                pltpu.VMEM((groups * rows, TAPS * width), BF),
            ],
            scalars=0,
            near=near,
            near_out=(0,),
            room=44,
            flops=2 * groups * rows * channels * width * TAPS,
        )
        return out

    right_parts = exchanged(right_sends, "cout")
    got = every_device(sums.reshape(devices, 32, LANES))
    right_slots = gathered(after(right_turned, got), "cout")
    orders = [(axis, bit) for axis in ("cin", "dp") for bit in bits_of(axis)]
    small_old = [norm_mean, norm_square, head_w_mean.T, head_w_square.T, head_b_mean[None], head_b_square[None]]
    def hold(*values):
        def copy_in(*refs):
            arrived = refs[-1]
            copies = [
                pltpu.make_async_copy(refs[at], refs[len(values) + at], arrived.at[at])
                for at in range(len(values))
            ]
            for copy in copies:
                copy.start()
            for copy in copies:
                copy.wait()

        return call(
            lambda *refs: copy_in(*refs),
            [shape(value.shape, value.dtype) for value in values],
            values,
            [pltpu.SemaphoreType.DMA((len(values),))],
            scalars=0,
            raw=tuple(range(len(values))),
            near_out=tuple(range(len(values))),
            room=16,
        )

    def ratio_of(terms, scales_own):
        chunk = shape(scales_own.shape, BF)
        return call(
            lambda *refs: ratio_kernel(refs[: len(terms)], *refs[len(terms) :]),
            [chunk, chunk],
            [*terms, scales_own],
            scalars=0,
            near=tuple(range(len(terms) + 1)),
            near_out=(0, 1),
            room=16,
        )

    def middle_of(slots, basis):
        (out,) = call(
            lambda basis_ref, *refs: middle_kernel(basis_ref, refs[:groups], refs[-1]),
            [shape(slots[0].shape, BF)],
            [basis, *slots],
            scalars=0,
            near=tuple(range(groups + 1)),
            near_out=(0,),
            room=16,
        )
        return out

    near_steps = len(bits_of("cin"))
    left_parts = [left_turned[step] for step in range(groups)]
    *products_first, sums_first, smalls = call(
        lambda *refs: first_products_kernel(
            *refs[:5], refs[5:11], *[refs[11 + at * groups : 11 + (at + 1) * groups] for at in range(3)],
            *refs[11 + 3 * groups :]
        ),
        [shape((TAPS * channels // 2, width), BF)] * 2 + [shape((8, LANES), F32), shape((72, LANES), F32)],
        [
            place, after(got, right_turned, *left_slots), norm_first, all_mask, basis_out_first, *small_old, *left_parts, *right_parts, *scaled_slots,
        ],
        [
            pltpu.VMEM((channels, groups * rows), BF),
            pltpu.VMEM((groups * rows, TAPS * width), BF),
            pltpu.VMEM((groups, rows, width), BF),
            pltpu.VMEM((channels, width), BF),
            pltpu.VMEM((rows, LANES), BF),
            pltpu.VMEM((TAPS * channels, width), BF),
        ],
        near_out=(0, 1),
        room=56,
        flops=2 * groups * rows * channels * width * TAPS,
    )
    terms_first = crossed(products_first, *orders[0])
    for order in orders[1:]:
        terms_first = halved(terms_first, *order)
    own_first = joined([after(terms_first[0], *right_slots), terms_first[1]])
    coeff_first = doubled(own_first, *orders[-1])
    terms_second = [products(1, [after(right_slots[0], own_first)] + right_slots[1:], left_slots)]
    for order in orders:
        terms_second = halved(terms_second, *order)
    for order in reversed(orders[near_steps:-1]):
        coeff_first = doubled(coeff_first, *order)
    coeff_first = batch_gather(coeff_first, ("cin",))
    flat_scales = scales_first.reshape(TAPS * channels, width)
    scales_first_new, ratio_first = call(
        wide_ratio_kernel,
        [shape(flat_scales.shape, F32), shape((TAPS * channels // 2, width), BF)],
        [place, coeff_first, flat_scales],
        near=(1, 2),
        near_out=(1,),
        room=16,
    )
    slots_first = gathered(ratio_first, "cout")
    own_second, ratio_second = ratio_of(terms_second, after(scales_turned, ratio_first))
    weights = hold(after(w_first, own_second), w_second)
    coeff_second = doubled(own_second, *orders[-1])
    middle_second = middle_of(gathered(ratio_second, "cout"), after(rows_second, coeff_second, ratio_first))
    means = hold(after(w_first_mean, weights[0]), w_second_mean)
    middle_first = middle_of(slots_first, after(rows_first, *means))
    gathered_first = doubled(middle_first, "cin", 0)
    squares_old = hold(after(w_first_square, middle_second), w_second_square)
    gathered_second = doubled(middle_second, *orders[-1])
    for order in reversed(orders[near_steps:-1]):
        coeff_second = doubled(coeff_second, *order)
        gathered_second = doubled(after(gathered_second, *squares_old), *order)
    gathered_second = batch_gather(gathered_second, ("cin",))
    coeff_second = batch_gather(coeff_second, ("cin",))

    def scales_of(turned, coeff, scales):
        spec = pl.BlockSpec((3,) + scales.shape[1:], lambda tap: (tap, 0, 0))
        return pl.pallas_call(
            functools.partial(scales_kernel, turned),
            grid=(TAPS // 3,),
            in_specs=[pl.BlockSpec((3 * channels, width), lambda tap: (tap, 0)), spec],
            out_specs=spec,
            out_shape=shape(scales.shape, F32),
            compiler_params=pltpu.CompilerParams(vmem_limit_bytes=12 * 1024 * 1024),
        )(coeff, scales)

    scales_second_new = scales_of(True, coeff_second, scales_second)

    first_grad, second_grad, squares, small_grads = call(
        restore_kernel,
        [shape((TAPS, channels, width), BF), shape((TAPS, width, channels), BF), shape((8, LANES), F32), shape((72, LANES), F32)],
        [
            place,
            basis_in_first,
            gathered_first,
            basis_out_second,
            gathered_second,
            sums_first,
            sums_second,
            smalls,
        ],
        [pltpu.VMEM((channels, TAPS * width), BF)],
        near=tuple(range(1, 8)),
        near_out=(0, 1, 2, 3),
        room=16,
        flops=4 * TAPS * channels * channels * width,
    )
    square_slots = gathered(squares, "cout")
    square_slots[0] = after(square_slots[0], coeff_second)

    smalls = [small_grads]
    small_outs = [shape((2, width), F32)] * 4 + [shape((CLASSES, width), F32)] * 2 + [shape((1, CLASSES), F32)] * 2
    small_outs += [shape((1, 1), F32)] * 2
    first_spec = pl.BlockSpec((3, channels, width), lambda tap: (tap, 0, 0))
    second_spec = pl.BlockSpec((3, width, channels), lambda tap: (tap, 0, 0))
    pair = [first_spec, second_spec]
    first_like, second_like = shape(w_first.shape, F32), shape(w_second.shape, F32)

    def whole(leaf):
        return pl.BlockSpec(leaf.shape, lambda tap: (0,) * len(leaf.shape))

    def update(*refs):
        at = [0]

        def take(number):
            at[0] += number
            return refs[at[0] - number : at[0]]

        update_kernel(
            take(groups), take(2), take(2), take(2), take(2), take(len(smalls)),
            take(2), take(2), take(2), take(len(small_outs) - 2), take(2), take(1)[0],
        )

    results = pl.pallas_call(
        update,
        grid=(TAPS // 3,),
        scratch_shapes=[pltpu.VMEM((8, LANES), F32)],
        in_specs=[pl.BlockSpec(memory_space=pltpu.VMEM)] * (groups + 8 + len(smalls)),
        out_specs=pair * 3 + [whole(leaf) for leaf in small_outs],
        out_shape=[first_like, second_like] * 3 + small_outs,
        compiler_params=pltpu.CompilerParams(vmem_limit_bytes=16 * 1024 * 1024),
    )(
        *square_slots, *weights, *means, *squares_old,
        first_grad, second_grad, *smalls,
    )
    (first_new, second_new, first_mean_new, second_mean_new, first_square_new, second_square_new,
     norm_first_mean, norm_first_square, norm_second_mean, norm_second_square,
     head_mean_new, head_square_new, bias_mean_new, bias_square_new, grad_norm, loss_total) = results
    return (
        loss_total.reshape(()),
        grad_norm.reshape(()),
        first_new,
        first_mean_new,
        first_square_new,
        second_new,
        second_mean_new,
        second_square_new,
        norm_first_mean,
        norm_first_square,
        norm_second_mean,
        norm_second_square,
        head_mean_new.T,
        head_square_new.T,
        bias_mean_new[0],
        bias_square_new[0],
        scales_first_new.reshape(scales_first.shape),
        scales_second_new,
    )


def solution(mesh):
    return jax.shard_map(
        local,
        mesh=mesh,
        in_specs=(
            P(None, ("dp", "cin"), None),
            P(None, ("dp", "cin")),
            P(("dp", "cin")),
            P(None, None, "cout"),
            P(None, "cout", None),
            P(None, "cout"),
            P("cout", None),
            P(),
            P(),
            P(None, None, "cout"),
            P(None, "cout", None),
            P(None, None, "cout"),
            P(None, None, "cout"),
            P(None, "cout", None),
            P(None, "cout", None),
            P(None, "cout"),
            P(None, "cout"),
            P("cout", None),
            P("cout", None),
            P(),
            P(),
        ),
        out_specs=(
            P(),
            P(),
            P(None, None, "cout"),
            P(None, None, "cout"),
            P(None, None, "cout"),
            P(None, "cout", None),
            P(None, "cout", None),
            P(None, "cout", None),
            P(None, "cout"),
            P(None, "cout"),
            P(None, "cout"),
            P(None, "cout"),
            P("cout", None),
            P("cout", None),
            P(),
            P(),
            P(None, None, "cout"),
            P(None, "cout", None),
        ),
        check_vma=False,
    )
```

```python
import functools
import math

import jax
import jax.numpy as jnp
from jax import lax
from jax.experimental import pallas as pl
from jax.experimental.pallas import tpu as pltpu
from jax.sharding import PartitionSpec as P

CLASSES = 10
SIDE = 4
PIX = 16
TAPS = 9
STEP = 10
LANES = 128

EPS_NORM = 1e-05
SCALE_DECAY = 0.95
DAMPING = 0.001
CLIP_NORM = 1.0
LEARN_RATE = 0.01
BETA_ONE = 0.9
BETA_TWO = 0.999
ADAM_EPS = 1e-08
WEIGHT_DECAY = 0.01
SMOOTH = 0.1
OFFSETS = [(row_step, col_step) for row_step in (-1, 0, 1) for col_step in (-1, 0, 1)]
EVERY = ("dp", "cout", "cin")
BF = jnp.bfloat16
F32 = jnp.float32
PRECISE = lax.Precision.HIGHEST
NN = (((1,), (0,)), ((), ()))
NT = (((1,), (1,)), ((), ()))
TN = (((0,), (0,)), ((), ()))


def matmul(left, right, dims=NN, precision=None):
    return lax.dot_general(
        left, right, dims, precision=precision, preferred_element_type=F32
    )


def runs(row_step, col_step, count):
    low, high = max(0, -col_step), min(SIDE, SIDE - col_step)
    found = []
    for row in range(max(0, -row_step), min(SIDE, SIDE - row_step)):
        to_row = (row * SIDE + low) * count
        from_row = ((row + row_step) * SIDE + low + col_step) * count
        length = (high - low) * count
        if found and found[-1][0] + found[-1][2] == to_row and found[-1][1] + found[-1][2] == from_row:
            found[-1] = (found[-1][0], found[-1][1], found[-1][2] + length)
        else:
            found.append((to_row, from_row, length))
    return found


class Late:
    def __init__(self, ref, copy):
        self.ref, self.copy, self.shape = ref, copy, ref.shape
        copy.start()

    def settle(self):
        if self.copy is not None:
            self.copy.wait()
        self.copy = None

    def __getitem__(self, index):
        self.settle()
        return self.ref[index]


class Result:
    def __init__(self, ref, copy):
        self.ref, self.copy, self.shape, self.sent = ref, copy, ref.shape, False

    def __getitem__(self, index):
        return self.ref[index]

    def __setitem__(self, index, values):
        self.ref[index] = values

    def send(self):
        if not self.sent:
            self.copy.start()
        self.sent = True


def call(kernel, outs, args, scratch=(), scalars=1, near=(), raw=(), near_out=(), flops=0, room=60):
    n_in, n_out = len(args), len(outs)
    copied = [at for at in range(scalars, n_in) if at not in near and at not in raw]
    copied_out = [at for at in range(n_out) if at not in near_out]

    def body(*refs):
        ins, results = list(refs[:n_in]), list(refs[n_in : n_in + n_out])
        rest = refs[n_in + n_out :]
        held, held_out = rest[: len(copied)], rest[len(copied) : len(copied) + len(copied_out)]
        own, arrived = rest[len(copied) + len(copied_out) : -1], rest[-1]
        for nth, at in enumerate(copied):
            ins[at] = Late(held[nth], pltpu.make_async_copy(ins[at], held[nth], arrived.at[nth]))
        for nth, at in enumerate(copied_out):
            copy = pltpu.make_async_copy(held_out[nth], results[at], arrived.at[len(copied) + nth])
            results[at] = Result(held_out[nth], copy)
        kernel(*ins, *results, *own)
        for at in copied:
            ins[at].settle()
        for at in copied_out:
            results[at].send()
        for at in copied_out:
            results[at].copy.wait()

    specs = [pl.BlockSpec(memory_space=pltpu.SMEM)] * scalars
    specs += [
        pl.BlockSpec(memory_space=pltpu.VMEM if at in near else pltpu.HBM) for at in range(scalars, n_in)
    ]
    moved = sum(math.prod(a.shape) * a.dtype.itemsize for a in list(args) + list(outs))
    return pl.pallas_call(
        body,
        out_shape=list(outs),
        in_specs=specs,
        out_specs=[
            pl.BlockSpec(memory_space=pltpu.VMEM if at in near_out else pltpu.HBM) for at in range(n_out)
        ],
        scratch_shapes=[pltpu.VMEM(args[at].shape, args[at].dtype) for at in copied]
        + [pltpu.VMEM(outs[at].shape, outs[at].dtype) for at in copied_out]
        + list(scratch)
        + [pltpu.SemaphoreType.DMA((max(1, len(copied) + len(copied_out)),))],
        compiler_params=pltpu.CompilerParams(vmem_limit_bytes=room * 1024 * 1024),
        cost_estimate=pl.CostEstimate(flops=flops, bytes_accessed=moved, transcendentals=0),
    )(*args)


def shape(dims, dtype):
    return jax.ShapeDtypeStruct(dims, dtype)


def gelu_parts(values):
    rate = math.sqrt(2.0 / math.pi)
    bend = jnp.tanh(rate * (values + 0.044715 * values * values * values))
    share = 0.5 * (1.0 + bend)
    slope = share + 0.5 * values * (1.0 - bend * bend) * rate * (1.0 + 0.134145 * values * values)
    return values * share, slope


def fill_mask(masks_ref, mask_ref):
    count = masks_ref.shape[1]
    same = lax.broadcasted_iota(jnp.int32, (count, count), 0) == lax.broadcasted_iota(
        jnp.int32, (count, count), 1
    )
    for pixel in range(PIX):
        row = masks_ref[pixel : pixel + 1, :].astype(F32)
        column = jnp.sum(jnp.where(same, row, 0.0), axis=1, keepdims=True)
        mask_ref[pixel * count : (pixel + 1) * count, :] = jnp.broadcast_to(column, (count, LANES))


def fill_inputs(images_ref, mask_ref, inputs_ref):
    low = mask_ref[...].astype(BF)
    for lane in range(0, images_ref.shape[1], LANES):
        inputs_ref[:, lane : lane + LANES] = images_ref[:, lane : lane + LANES] * low


def first_kernel(
    groups, place_ref, images_ref, masks_ref, weight_ref,
    sum_ref, all_mask_ref, stats_ref, own_mask_ref, mask_ref, inputs_ref, low_ref, wide_ref, arrived,
):
    count = masks_ref.shape[1]
    part = count // groups
    me = place_ref[0]
    copies = [
        pltpu.make_async_copy(weight_ref.at[at : at + 3], wide_ref.at[at : at + 3], arrived.at[at // 3])
        for at in range(0, TAPS, 3)
    ]
    for copy in copies:
        copy.start()
    fill_mask(masks_ref, mask_ref)
    fill_inputs(images_ref, mask_ref, inputs_ref)
    all_mask_ref[...] = mask_ref[...].astype(BF)
    all_mask_ref.send()
    for pixel in range(PIX):
        own = pl.multiple_of(pixel * count + me * part, part)
        own_mask_ref[pixel * part : (pixel + 1) * part, :] = mask_ref[pl.ds(own, part), :]
    own_mask_ref.send()
    for tap in range(TAPS):
        if tap % 3 == 0:
            copies[tap // 3].wait()
        low_ref[:, tap * LANES : (tap + 1) * LANES] = wide_ref[tap].astype(BF)
    sum_ref[...] = jnp.zeros(sum_ref.shape, F32)
    for tap in range(0, TAPS, 2):
        taps = min(2, TAPS - tap)
        product = matmul(inputs_ref[...], low_ref[:, tap * LANES : (tap + taps) * LANES])
        for nth in range(taps):
            for to_row, from_row, length in runs(*OFFSETS[tap + nth], count):
                sum_ref[to_row : to_row + length, :] += product[
                    from_row : from_row + length, nth * LANES : (nth + 1) * LANES
                ]
    sum_ref.send()
    mask = mask_ref[...]
    total = sum_ref[...]
    masked = total * mask
    tile = jnp.concatenate(
        [
            jnp.sum(masked, axis=0, keepdims=True),
            jnp.sum(masked * total, axis=0, keepdims=True),
            jnp.sum(mask, axis=0, keepdims=True),
            jnp.zeros((5, LANES), F32),
        ],
        axis=0,
    )
    stats_ref[...] = jnp.broadcast_to(tile[None], stats_ref.shape)


def first_norm_kernel(
    place_ref, got_ref, first_ref, mask_ref, params_ref, head_ref, send_refs, kept_ref, hidden_ref, scaled_ref
):
    total = total_of(got_ref)
    kept = total[2:3, :]
    mean = total[0:1, :] / kept
    rstd = lax.rsqrt(total[1:2, :] / kept - mean * mean + EPS_NORM)
    kept_ref[...] = jnp.broadcast_to(kept, kept_ref.shape)
    gain, shift = params_ref[0:1, :], params_ref[1:2, :]
    count = first_ref.shape[0] // PIX
    part = count // len(send_refs)
    scaled = (first_ref[...] - mean) * rstd
    value, _ = gelu_parts(gain * scaled + shift)
    hidden_ref[...] = (value * mask_ref[...].astype(F32)).astype(BF)
    scaled_ref[...] = scaled.astype(BF)
    lines = [head_ref[...]]
    for line in (rstd, gain, shift):
        high = line.astype(BF).astype(F32)
        lines += [high, line - high]
    extra = jnp.concatenate(lines, axis=0).astype(BF)
    rows = PIX * part
    for step, send_ref in enumerate(send_refs):
        for pixel in range(PIX):
            base = pl.ds(pl.multiple_of(pixel * count + (place_ref[0] ^ step) * part, part), part)
            send_ref[pixel * part : (pixel + 1) * part, :] = hidden_ref[base, :]
            send_ref[rows + pixel * part : rows + (pixel + 1) * part, :] = scaled_ref[base, :]
        send_ref[2 * rows : 2 * rows + 16, :] = extra


def hidden_kernel(place_ref, slot_refs, mask_ref, hidden_ref):
    rows = hidden_ref.shape[0]
    for step, slot_ref in enumerate(slot_refs):
        lanes = pl.ds(pl.multiple_of((place_ref[0] ^ step) * LANES, LANES), LANES)
        hidden_ref[:, lanes] = slot_ref[0:rows, :]
    hidden_ref[:, len(slot_refs) * LANES :] = mask_ref[...].astype(BF)


def gather_kernel(place_ref, slot_refs, kept_ref, scaled_ref, norm_ref, head_ref):
    rows = scaled_ref.shape[0]
    norm_ref[0:1, :] = jnp.zeros((1, norm_ref.shape[1]), F32)
    norm_ref[5:8, :] = jnp.zeros((3, norm_ref.shape[1]), F32)
    for step, slot_ref in enumerate(slot_refs):
        lanes = pl.ds(pl.multiple_of((place_ref[0] ^ step) * LANES, LANES), LANES)
        scaled_ref[:, lanes] = slot_ref[rows : 2 * rows, :]
        extra = slot_ref[2 * rows : 2 * rows + 16, :].astype(F32)
        line = lax.broadcasted_iota(jnp.int32, (16, LANES), 0)
        head_ref[:, lanes] = jnp.where(line < CLASSES, extra, 0.0).astype(BF)
        for at in range(3):
            norm_ref[at + 1 : at + 2, lanes] = (
                extra[CLASSES + 2 * at : CLASSES + 2 * at + 1, :] + extra[CLASSES + 2 * at + 1 : CLASSES + 2 * at + 2, :]
            )
        norm_ref[4:5, lanes] = kept_ref[0:1, :]


def second_kernel(
    place_ref, own_ref, other_ref, params_ref, slot_refs,
    mine_ref, theirs_ref, stats_ref, inputs_ref, weight_ref, sum_ref, arrived,
):
    me = place_ref[0]
    rows = own_ref.shape[0]
    part = rows // PIX
    depth, half = slot_refs[0].shape[1:]
    copies = []
    for step, slot_ref in enumerate(slot_refs):
        span = pl.ds(pl.multiple_of((me ^ step) * depth, depth), depth)
        copies.append(pltpu.make_async_copy(slot_ref, weight_ref.at[:, span, :], arrived.at[step]))
        copies[-1].start()
    channels = inputs_ref.shape[1]
    inputs_ref[0:rows, :] = own_ref[:, 0:channels]
    inputs_ref[rows : 2 * rows, :] = other_ref[:, 0:channels]
    sum_ref[...] = jnp.zeros_like(sum_ref)
    for copy in copies:
        copy.wait()
    for tap in range(TAPS):
        product = matmul(inputs_ref[...], weight_ref[tap])
        for to_row, from_row, length in runs(*OFFSETS[tap], part):
            for base in (0, rows):
                sum_ref[base + to_row : base + to_row + length, :] += product[
                    base + from_row : base + from_row + length, :
                ]
    mine_ref[...] = sum_ref[0:rows, :]
    theirs_ref[...] = sum_ref[rows : 2 * rows, :]
    lines = [[], []]
    for lane in range(0, half, LANES):
        first = square = None
        for base, ref in ((0, own_ref), (rows, other_ref)):
            total = sum_ref[base : base + rows, lane : lane + LANES]
            masked = total * ref[:, channels : channels + LANES].astype(F32)
            first_part = jnp.sum(masked, axis=0, keepdims=True)
            square_part = jnp.sum(masked * total, axis=0, keepdims=True)
            first = first_part if first is None else first + first_part
            square = square_part if square is None else square + square_part
        lines[0].append(first)
        lines[1].append(square)
    spare = 8 - 2 * (half // LANES) - 2
    tile = jnp.concatenate(
        lines[0] + lines[1] + [params_ref[2:4, :], jnp.zeros((spare, LANES), F32)], axis=0
    )
    stats_ref[...] = jnp.broadcast_to(tile[None], stats_ref.shape)


def head_kernel(
    sizes, place_ref, mine_ref, got_ref_rows, got_ref, norm_first_ref, mask_ref, head_ref, bias_ref, labels_ref,
    wide_ref, norm_ref, dz_ref, sums_ref, head_out_ref, slope_ref, pooled_ref, weight_ref,
):
    count_dp, groups, count_cin = sizes
    side = place_ref[1]
    rows, half = mine_ref.shape
    part = rows // PIX
    blocks = half // LANES
    wide_ref[:, pl.ds(pl.multiple_of(side * half, half), half)] = mine_ref[...]
    wide_ref[:, pl.ds(pl.multiple_of((1 - side) * half, half), half)] = got_ref_rows[...]
    totals = [None, None]
    for source in range(count_dp * groups * count_cin):
        which = source % count_cin % 2
        tile = got_ref[source]
        totals[which] = tile if totals[which] is None else totals[which] + tile
    kept = norm_first_ref[4:5, 0:LANES]
    mask = mask_ref[...]
    for group in range(groups):
        lanes = slice(group * LANES, (group + 1) * LANES)
        total, line = totals[group // blocks], group % blocks
        mean = total[line : line + 1, :] / kept
        rstd = lax.rsqrt(total[blocks + line : blocks + line + 1, :] / kept - mean * mean + EPS_NORM)
        single = got_ref[group * count_cin]
        gain = single[2 * blocks : 2 * blocks + 1, :]
        shift = single[2 * blocks + 1 : 2 * blocks + 2, :]
        norm_ref[0:1, lanes] = mean
        norm_ref[1:2, lanes] = rstd
        norm_ref[2:3, lanes] = gain
        norm_ref[3:4, lanes] = shift
        norm_ref[4:8, lanes] = jnp.broadcast_to(kept, (4, LANES))
        value, slope = gelu_parts(gain * ((wide_ref[:, lanes] - mean) * rstd) + shift)
        slope_ref[:, lanes] = slope * mask * (1.0 / PIX)
        pooled_ref[:, lanes] = jnp.sum((value * mask).reshape(PIX, part, LANES), axis=0) * (1.0 / PIX)
    wide_ref.send()
    norm_ref.send()
    weight_ref[0:16, :] = head_ref[...]
    weight_ref[16:LANES, :] = jnp.zeros((LANES - 16, weight_ref.shape[1]), BF)
    pooled = pooled_ref[...].astype(BF)
    head = weight_ref[...]
    class_index = lax.broadcasted_iota(jnp.int32, (part, LANES), 1)
    logits = matmul(pooled, head, NT) + bias_ref[...]
    logits = jnp.where(class_index < CLASSES, logits, -1e30)
    logits = logits - jnp.max(logits, axis=1, keepdims=True)
    log_probs = logits - jnp.log(jnp.sum(jnp.exp(logits), axis=1, keepdims=True))
    wanted = jnp.where(class_index == labels_ref[...], 1.0 - SMOOTH, 0.0) + SMOOTH / CLASSES
    wanted = jnp.where(class_index < CLASSES, wanted, 0.0)
    loss = -jnp.sum(jnp.sum(wanted * log_probs, axis=1, keepdims=True), axis=0, keepdims=True)
    logit_grad = jnp.exp(log_probs) - wanted
    head_grad = matmul(logit_grad, pooled.astype(F32), TN, PRECISE)
    pooled_grad = matmul(logit_grad, head.astype(F32), NN, PRECISE)
    extra = jnp.sum(logit_grad, axis=0, keepdims=True)
    extra = jnp.where(class_index[0:1, :] == CLASSES, loss, extra)
    line = lax.broadcasted_iota(jnp.int32, (16, LANES), 0)
    gains, shifts = [], []
    for group in range(groups):
        lanes = slice(group * LANES, (group + 1) * LANES)
        head_out_ref[group] = jnp.where(line == CLASSES, extra, head_grad[0:16, lanes])
        spread = jnp.broadcast_to(pooled_grad[:, lanes][None], (PIX, part, LANES)).reshape(rows, LANES)
        dz = slope_ref[:, lanes] * spread
        dz_ref[:, lanes] = dz
        scaled = (wide_ref[:, lanes] - norm_ref[0:1, lanes]) * norm_ref[1:2, lanes]
        gains.append(jnp.sum(dz * scaled, axis=0, keepdims=True))
        shifts.append(jnp.sum(dz, axis=0, keepdims=True))
    sums_ref[...] = jnp.broadcast_to(jnp.concatenate(gains + shifts, axis=0)[None], sums_ref.shape)


def total_of(got_ref):
    total = got_ref[0]
    for source in range(1, got_ref.shape[0]):
        total = total + got_ref[source]
    return total


def norm_back(scaled, dz, norm, mask, gain_grad, shift_grad):
    gain = norm[2:3, :]
    return norm[1:2, :] * (
        gain * dz - mask * (gain / norm[4:5, :]) * (shift_grad + scaled * gain_grad)
    )


def second_back_kernel(
    place_ref, dz_ref, wide_ref, norm_ref, got_ref, mask_ref, first_ref, norm_first_ref, head_ref, basis_ref, near_refs, far_refs,
    grad_ref, sums_out_ref, sums_ref, send_refs, part_ref, weight_ref, sum_ref, arrived,
):
    me, side = place_ref[0], place_ref[1]
    depth, half = near_refs[0].shape[1:]
    copies = {}
    for tap in range(0, TAPS, 3):
        for which, (refs, at) in enumerate(((near_refs, side), (far_refs, 1 - side))):
            lanes = pl.ds(pl.multiple_of(at * half, half), half)
            for step, slot_ref in enumerate(refs):
                span = pl.ds(pl.multiple_of((me ^ step) * depth, depth), depth)
                number = which * len(refs) + step
                copies[tap, number] = pltpu.make_async_copy(
                    slot_ref.at[tap : tap + 3], weight_ref.at[tap : tap + 3, span, lanes], arrived.at[tap // 3, number]
                )
                copies[tap, number].start()
    total = total_of(got_ref)
    sums_out_ref[...] = total
    groups = total.shape[0] // 2
    mask = mask_ref[...]
    for group in range(groups):
        lanes = slice(group * LANES, (group + 1) * LANES)
        norm = norm_ref[:, lanes]
        grad_ref[:, lanes] = norm_back(
            (wide_ref[:, lanes] - norm[0:1, :]) * norm[1:2, :], dz_ref[:, lanes], norm, mask,
            total[group : group + 1, :], total[groups + group : groups + group + 1, :],
        ).astype(BF)
    grad_ref.send()
    sums_out_ref.send()
    rows, channels = grad_ref.shape
    part = rows // PIX
    sum_ref[...] = jnp.zeros_like(sum_ref)
    for tap in range(TAPS):
        if tap % 3 == 0:
            for number in range(2 * len(near_refs)):
                copies[tap, number].wait()
        product = matmul(grad_ref[...], weight_ref[tap], NT)
        row_step, col_step = OFFSETS[tap]
        for to_row, from_row, length in runs(-row_step, -col_step, part):
            sum_ref[to_row : to_row + length, :] += product[from_row : from_row + length, :]
    gains, shifts = [], []
    for lane in range(0, channels, LANES):
        lanes = slice(lane, lane + LANES)
        norm = norm_first_ref[:, lanes]
        scaled = first_ref[:, lanes].astype(F32)
        _, slope = gelu_parts(norm[2:3, :] * scaled + norm[3:4, :])
        dz = slope * mask * sum_ref[:, lanes]
        part_ref[:, lanes] = (norm[1:2, :] * norm[2:3, :] * dz).astype(BF)
        gains.append(jnp.sum(dz * scaled, axis=0, keepdims=True))
        shifts.append(jnp.sum(dz, axis=0, keepdims=True))
    sum_ref[...] = matmul(part_ref[...], basis_ref[...])
    send_columns(me, sum_ref, send_refs)
    count_dp, _, count_cin = sums_ref.shape[:3]
    for group in range(groups):
        tile = jnp.concatenate(gains + shifts + [head_ref[group], jnp.zeros((8, LANES), F32)], axis=0)
        tile = tile.astype(BF)
        for far in range(count_dp):
            for near in range(count_cin):
                sums_ref[far, group, near] = tile


def first_products_kernel(
    place_ref, got_ref, norm_ref, mask_ref, basis_ref, old_refs, big_refs, part_refs, scaled_refs,
    kept_ref, sent_ref, sums_ref, small_ref, left_ref, right_ref, slot_ref, column_ref, mask_slot_ref, out_ref,
):
    me = place_ref[0]
    rows, width = part_refs[0].shape
    part = rows // PIX
    count = mask_ref.shape[0] // PIX
    whole = got_ref[0].astype(F32)
    for source in range(1, got_ref.shape[0]):
        whole = whole + got_ref[source].astype(F32)
    sums_ref[...] = whole[0:8, :]
    small_ref[...] = jnp.zeros(small_ref.shape, F32)
    small_ref[8:24, :] = whole[8:24, :]
    for at, row in enumerate((24, 28, 32, 48, 64, 65)):
        lines, lanes = old_refs[at].shape
        small_ref[row : row + lines, 0:lanes] = old_refs[at][...]
    groups = len(part_refs)
    column_ref[...] = basis_ref[:, pl.ds(pl.multiple_of(me * width, width), width)]
    rates, shifts = [], []
    for group in range(groups):
        lanes = slice(group * LANES, (group + 1) * LANES)
        scale = norm_ref[1:2, lanes] * norm_ref[2:3, lanes] / norm_ref[4:5, lanes]
        rates.append(scale * whole[group : group + 1, :])
        shifts.append(scale * whole[groups + group : groups + group + 1, :])
    rate = jnp.concatenate(rates, axis=1)
    shift = jnp.broadcast_to(jnp.concatenate(shifts, axis=1), (8, groups * LANES))
    fixed = matmul(shift, column_ref[...].astype(F32), NN, PRECISE)[0:1, :]
    for step in range(groups):
        for pixel in range(PIX):
            base = pl.ds(pl.multiple_of(pixel * count + (me ^ step) * part, part), part)
            mask_slot_ref[pixel * part : (pixel + 1) * part, :] = mask_ref[base, :]
        moved = matmul((scaled_refs[step][...].astype(F32) * rate).astype(BF), column_ref[...])
        slot_ref[step] = (
            part_refs[step][...].astype(F32) - mask_slot_ref[...].astype(F32) * (fixed + moved)
        ).astype(BF)
    taps_kernel(-1, big_refs, [slot_ref.at[step] for step in range(groups)], out_ref, left_ref, right_ref)
    half = kept_ref.shape[0]
    sent_ref[...] = out_ref[pl.ds(pl.multiple_of((1 - place_ref[1]) * half, half), half), :]
    kept_ref[...] = out_ref[pl.ds(pl.multiple_of(place_ref[1] * half, half), half), :]


def left_second_kernel(place_ref, norm_ref, mask_ref, basis_ref, scaled_refs, left_refs, column_ref, wide_ref):
    me = place_ref[0]
    rows, width = left_refs[0].shape
    part = rows // PIX
    count = mask_ref.shape[0] // PIX
    column_ref[...] = basis_ref[:, pl.ds(pl.multiple_of(me * width, width), width)]
    for step, scaled_ref in enumerate(scaled_refs):
        mask = jnp.concatenate(
            [
                mask_ref[pl.ds(pl.multiple_of(pixel * count + (me ^ step) * part, part), part), :]
                for pixel in range(PIX)
            ],
            axis=0,
        ).astype(F32)
        for lane in range(0, wide_ref.shape[1], LANES):
            lanes = slice(lane, lane + LANES)
            value, _ = gelu_parts(
                norm_ref[2:3, lanes] * scaled_ref[:, lanes].astype(F32) + norm_ref[3:4, lanes]
            )
            wide_ref[:, lanes] = (value * mask).astype(BF)
        left_refs[step][...] = matmul(wide_ref[...], column_ref[...]).astype(BF)


def right_kernel(grad_ref, basis_ref, right_ref):
    right_ref[...] = jnp.transpose(matmul(grad_ref[...], basis_ref[...])).astype(BF)


def send_columns(me, product_ref, send_refs):
    for step, send_ref in enumerate(send_refs):
        lanes = pl.ds(pl.multiple_of((me ^ step) * LANES, LANES), LANES)
        send_ref[...] = product_ref[:, lanes].astype(BF)


def left_first_kernel(place_ref, images_ref, masks_ref, basis_ref, left_ref, mask_ref, inputs_ref, part_ref):
    slots = left_ref.shape[0]
    count = masks_ref.shape[1]
    part = count // slots
    me = place_ref[0]
    fill_mask(masks_ref, mask_ref)
    fill_inputs(images_ref, mask_ref, inputs_ref)
    for step in range(slots):
        for pixel in range(PIX):
            base = pl.multiple_of(pixel * count + (me ^ step) * part, part)
            part_ref[pixel * part : (pixel + 1) * part, :] = inputs_ref[pl.ds(base, part), :]
        left_ref[step] = jnp.transpose(matmul(part_ref[...], basis_ref[...])).astype(BF)


def pick_kernel(own_ref, full_ref, kept_ref, sent_ref):
    half = kept_ref.shape[0]
    kept_ref[...] = full_ref[pl.ds(pl.multiple_of(own_ref[0] * half, half), half), :]
    sent_ref[...] = full_ref[pl.ds(pl.multiple_of((1 - own_ref[0]) * half, half), half), :]


def split_kernel(own_ref, here_ref, came_ref, kept_ref, sent_ref):
    half = kept_ref.shape[0]
    for which, ref in ((own_ref[0], kept_ref), (1 - own_ref[0], sent_ref)):
        rows = pl.ds(pl.multiple_of(which * half, half), half)
        ref[...] = (here_ref[rows, :].astype(F32) + came_ref[rows, :].astype(F32)).astype(BF)


def merge_kernel(own_ref, here_ref, came_ref, out_ref):
    rows = here_ref.shape[0]
    for choice in range(2):

        @pl.when(own_ref[0] == choice)
        def _():
            out_ref[choice * rows : (choice + 1) * rows, :] = here_ref[...]
            out_ref[(1 - choice) * rows : (2 - choice) * rows, :] = came_ref[...]


def taps_kernel(sign, big_refs, small_refs, out_ref, left_ref, right_ref):
    rows, width = small_refs[0].shape
    channels = big_refs[0].shape[0]
    part = rows // PIX
    right_ref[...] = jnp.zeros_like(right_ref)
    for slot, (big_ref, small_ref) in enumerate(zip(big_refs, small_refs)):
        base = slot * rows
        left_ref[:, base : base + rows] = big_ref[...]
        for tap, (row_step, col_step) in enumerate(OFFSETS):
            for to_row, from_row, length in runs(sign * row_step, sign * col_step, part):
                right_ref[base + to_row : base + to_row + length, tap * width : (tap + 1) * width] = (
                    small_ref[from_row : from_row + length, :]
                )
    for tap in range(0, TAPS, 2):
        taps = min(2, TAPS - tap)
        product = matmul(left_ref[...], right_ref[:, tap * width : (tap + taps) * width])
        for nth in range(taps):
            out_ref[(tap + nth) * channels : (tap + nth + 1) * channels, :] = product[
                :, nth * width : (nth + 1) * width
            ].astype(BF)


def ratio_kernel(own_refs, scales_ref, coeff_ref, ratio_ref):
    coeff = None
    for ref in own_refs:
        coeff = ref[...].astype(F32) if coeff is None else coeff + ref[...].astype(F32)
    scales = SCALE_DECAY * scales_ref[...] + (1.0 - SCALE_DECAY) * coeff * coeff
    coeff_ref[...] = coeff.astype(BF)
    ratio_ref[...] = (coeff / (scales + DAMPING)).astype(BF)


def middle_kernel(basis_ref, slot_refs, out_ref):
    width = slot_refs[0].shape[1]
    ratio = jnp.concatenate([ref[...] for ref in slot_refs], axis=1)
    out_ref[...] = matmul(ratio, basis_ref[...], NT).astype(BF)


def scales_kernel(turned, coeff_ref, scales_ref, out_ref):
    taps = out_ref.shape[0]
    rows = coeff_ref.shape[0] // taps
    for tap in range(taps):
        coeff = coeff_ref[tap * rows : (tap + 1) * rows, :].astype(F32)
        if turned:
            coeff = jnp.transpose(coeff)
        out_ref[tap] = SCALE_DECAY * scales_ref[tap] + (1.0 - SCALE_DECAY) * coeff * coeff


def wide_ratio_kernel(place_ref, coeff_ref, scales_ref, scales_out_ref, ratio_ref):
    half = ratio_ref.shape[0]
    rows = pl.ds(pl.multiple_of(place_ref[1] * half, half), half)
    coeff = coeff_ref[...].astype(F32)
    scales_out_ref[...] = SCALE_DECAY * scales_ref[...] + (1.0 - SCALE_DECAY) * coeff * coeff
    scales_out_ref.send()
    ratio_ref[...] = (coeff_ref[rows, :].astype(F32) / (scales_out_ref[rows, :] + DAMPING)).astype(BF)


def add_squares(total, values):
    return total + jnp.sum((values * values).reshape(-1, 8, LANES), axis=0)


def restore_kernel(
    place_ref, basis_in_ref, middle_first_ref, basis_out_ref, middle_second_ref, sums_first_ref, sums_second_ref,
    old_ref, first_ref, second_ref, squares_ref, small_ref, stack_ref,
):
    me = place_ref[0]
    channels = basis_in_ref.shape[0]
    total = jnp.zeros((8, LANES), F32)
    for tap in range(TAPS):
        product = matmul(
            middle_second_ref[tap * channels : (tap + 1) * channels, :], basis_out_ref[...], (((0,), (1,)), ((), ()))
        )
        second_ref[tap] = product.astype(BF)
        for lane in range(0, channels, LANES):
            total = add_squares(total, product[:, lane : lane + LANES])
    for tap in range(TAPS):
        stack_ref[:, tap * LANES : (tap + 1) * LANES] = middle_first_ref[
            tap * channels : (tap + 1) * channels, :
        ]
    for tap in range(0, TAPS, 2):
        taps = min(2, TAPS - tap)
        product = matmul(basis_in_ref[...], stack_ref[:, tap * LANES : (tap + taps) * LANES])
        for nth in range(taps):
            block = product[:, nth * LANES : (nth + 1) * LANES]
            first_ref[tap + nth] = block.astype(BF)
            total = add_squares(total, block)
    groups = sums_first_ref.shape[0] // 2
    row = lax.broadcasted_iota(jnp.int32, (8, LANES), 0)
    mine = (row == me) | (row == me + groups)
    for ref in (sums_first_ref, sums_second_ref):
        total = total + jnp.where(mine, ref[...] * ref[...], 0.0)
    line = lax.broadcasted_iota(jnp.int32, (16, LANES), 0)
    lane = lax.broadcasted_iota(jnp.int32, (16, LANES), 1)
    counted = (line < CLASSES) | ((line == CLASSES) & (lane < CLASSES) & (me == 0))
    head = jnp.where(counted, old_ref[8:24, :], 0.0)
    small_ref[...] = old_ref[...]
    for at, ref in enumerate((sums_first_ref, sums_second_ref)):
        small_ref[2 * at : 2 * at + 1, :] = ref[pl.ds(me, 1), :]
        small_ref[2 * at + 1 : 2 * at + 2, :] = ref[pl.ds(me + groups, 1), :]
    squares_ref[...] = add_squares(total, head)


def update_kernel(
    square_refs, weight_refs, mean_refs, square_moment_refs, grad_refs, small_refs,
    weight_outs, mean_outs, square_outs, small_outs, scalar_outs, norm_ref,
):
    @pl.when(pl.program_id(0) == 0)
    def _():
        parts = [ref[...] for ref in square_refs]
        while len(parts) > 1:
            parts = [parts[at] + parts[at + 1] for at in range(0, len(parts), 2)]
        total = jnp.sum(jnp.sum(parts[0], axis=1, keepdims=True), axis=0, keepdims=True)
        found = jnp.sqrt(total)
        norm_ref[0:1, :] = jnp.broadcast_to(found, (1, LANES))
        norm_ref[1:2, :] = jnp.broadcast_to(CLIP_NORM / jnp.maximum(found, CLIP_NORM), (1, LANES))

    grad_norm, factor = norm_ref[0:1, 0:1], norm_ref[1:2, 0:1]

    def moments(gradient, mean_old, square_old):
        mean_new = BETA_ONE * mean_old + (1.0 - BETA_ONE) * gradient
        square_new = BETA_TWO * square_old + (1.0 - BETA_TWO) * gradient * gradient
        return mean_new, square_new

    taps = mean_outs[0].shape[0]
    for at in range(len(weight_refs)):
        for nth in range(taps):
            tap = pl.program_id(0) * taps + nth
            gradient = grad_refs[at][tap].astype(F32) * factor
            mean_new, square_new = moments(gradient, mean_refs[at][tap], square_moment_refs[at][tap])
            mean_outs[at][nth] = mean_new
            square_outs[at][nth] = square_new
            square_hat = square_new * (1.0 / (1.0 - BETA_TWO**STEP))
            size = square_hat * lax.rsqrt(square_hat) + ADAM_EPS
            step = mean_new * (LEARN_RATE / (1.0 - BETA_ONE**STEP)) / size
            weight_outs[at][nth] = weight_refs[at][tap] * (1.0 - LEARN_RATE * WEIGHT_DECAY) - step

    @pl.when(pl.program_id(0) == 0)
    def _():
        norm_out, loss_out = scalar_outs
        norm_out[...] = grad_norm
        (small,) = small_refs
        loss_out[...] = small[8 + CLASSES : 9 + CLASSES, CLASSES : CLASSES + 1]
        results = moments(small[0:4, :] * factor, small[24:28, :], small[28:32, :])
        for at in range(2):
            small_outs[at][...] = results[at][0:2, :]
            small_outs[2 + at][...] = results[at][2:4, :]
        results = moments(
            small[8 : 8 + CLASSES, :] * factor, small[32 : 32 + CLASSES, :], small[48 : 48 + CLASSES, :]
        )
        for at in range(2):
            small_outs[4 + at][...] = results[at]
        lanes = slice(0, CLASSES)
        results = moments(small[8 + CLASSES : 9 + CLASSES, lanes] * factor, small[64:65, lanes], small[65:66, lanes])
        for at in range(2):
            small_outs[6 + at][...] = results[at]


def swap(values, axis, step):
    count = lax.axis_size(axis)
    return lax.ppermute(values, axis, [(here, here ^ step) for here in range(count)])


def gathered(values, axis):
    return [values] + [swap(values, axis, step) for step in range(1, lax.axis_size(axis))]


def exchanged(sends, axis):
    return [sends[0]] + [swap(sends[step], axis, step) for step in range(1, len(sends))]


def picked(values, index):
    return lax.dynamic_index_in_dim(values, index, 0, keepdims=False)


def after(values, *others):
    return lax.optimization_barrier((values,) + others)[0]


def tree_sum(slots):
    while len(slots) > 1:
        slots = [slots[at] + slots[at + 1] for at in range(0, len(slots), 2)]
    return slots[0]


def every_device(tiles):
    return lax.all_to_all(tiles, EVERY, 0, 0, tiled=True)


def bits_of(axis):
    return range(lax.axis_size(axis).bit_length() - 1)


def bit_of(axis, bit):
    return (lax.axis_index(axis) >> bit) & 1


def crossed(parts, axis, bit):
    return [parts[0], swap(parts[1], axis, 1 << bit)]


def halved(terms, axis, bit):
    rows, width = terms[0].shape
    own = bit_of(axis, bit)
    if rows // 2 % 16:
        total = joined(terms).reshape(2, rows // 2, width)
        return crossed([picked(total, own), picked(total, 1 - own)], axis, bit)
    half = shape((rows // 2, width), BF)
    parts = call(
        pick_kernel if len(terms) == 1 else split_kernel,
        [half, half],
        [own[None], *terms],
        near=tuple(range(1, 1 + len(terms))),
        near_out=(0, 1),
        room=16,
    )
    return crossed(parts, axis, bit)


def doubled(values, axis, bit):
    own = bit_of(axis, bit)
    rows, width = values.shape
    other = swap(values, axis, 1 << bit)
    (out,) = call(
        merge_kernel, [shape((2 * rows, width), BF)], [own[None], values, other], near=(1, 2), near_out=(0,), room=16
    )
    return out


def joined(terms):
    return terms[0] if len(terms) == 1 else (terms[0].astype(F32) + terms[1].astype(F32)).astype(BF)


def batch_gather(block, axes=("dp", "cin"), first=()):
    for order in reversed(first):
        block = doubled(block, *order)
    for axis in axes:
        for bit in reversed(bits_of(axis)):
            block = doubled(block, axis, bit)
    return block


def batch_rows(values):
    place = jnp.int32(0)
    for axis in ("cin", "dp"):
        for bit in bits_of(axis):
            place = place * 2 + ((lax.axis_index(axis) >> bit) & 1)
    rows = values.shape[0] // (lax.axis_size("dp") * lax.axis_size("cin"))
    return lax.dynamic_slice_in_dim(values, place * rows, rows, 0)


def local(
    images,
    masks,
    labels,
    w_first,
    w_second,
    norm_params,
    head_w,
    head_b,
    bases,
    scales_first,
    scales_second,
    w_first_mean,
    w_first_square,
    w_second_mean,
    w_second_square,
    norm_mean,
    norm_square,
    head_w_mean,
    head_w_square,
    head_b_mean,
    head_b_square,
):
    me = lax.axis_index("cout")
    side = lax.axis_index("cin") % 2
    place = jnp.stack([me, side]).astype(jnp.int32)
    sizes = tuple(lax.axis_size(name) for name in EVERY)
    groups = sizes[1]
    devices = sizes[0] * sizes[1] * sizes[2]
    channels = w_first.shape[1]
    width = w_first.shape[2]
    half = channels // 2
    count = images.shape[1]
    part = count // groups
    rows = PIX * part
    tile = shape((devices, 8, LANES), F32)
    wide = (rows, channels)
    basis_in_first, basis_out_first = bases[0, 0], bases[0, 1]
    basis_in_second, basis_out_second = bases[1, 0], bases[1, 1]
    bases_all = (basis_in_first, basis_out_first, basis_in_second, basis_out_second)

    piece = lax.dynamic_slice_in_dim(w_second, side * half, half, 2).astype(BF)
    own_labels = lax.dynamic_slice_in_dim(labels, me * part, part, 0)[:, None]
    bias_row = jnp.pad(head_b, (0, LANES - CLASSES))[None]

    flat_images = images.reshape(PIX * count, channels)
    first_out, all_mask, stats, mask = call(
        functools.partial(first_kernel, groups),
        [
            shape((PIX * count, width), F32),
            shape((PIX * count, LANES), BF),
            shape((sizes[0] * sizes[2], 8, LANES), F32),
            shape((rows, LANES), F32),
        ],
        [place, flat_images, masks, w_first],
        [
            pltpu.VMEM((PIX * count, LANES), F32),
            pltpu.VMEM((PIX * count, channels), BF),
            pltpu.VMEM((channels, TAPS * width), BF),
            pltpu.VMEM((TAPS, channels, width), F32),
            pltpu.SemaphoreType.DMA((3,)),
        ],
        near=(1, 2),
        raw=(3,),
        room=56,
        flops=2 * PIX * count * channels * width * TAPS,
    )
    got = lax.all_to_all(stats, ("dp", "cin"), 0, 0, tiled=True)
    (left_turned,) = call(
        left_first_kernel,
        [shape((groups, channels, rows), BF)],
        [place, after(flat_images, stats), masks, basis_in_first],
        [
            pltpu.VMEM((PIX * count, LANES), F32),
            pltpu.VMEM((PIX * count, channels), BF),
            pltpu.VMEM((rows, channels), BF),
        ],
        near=(1, 2, 3),
        room=20,
    )
    near_weights = [piece]
    for step in range(1, groups):
        ready = piece if step < groups - 1 else after(piece, stats)
        near_weights.append(swap(ready, "cout", step))
    first_mask = after(all_mask, left_turned, *near_weights[1:-1], *bases_all)
    *first_sends, kept = call(
        lambda *refs: first_norm_kernel(*refs[:6], refs[6 : 6 + groups], *refs[6 + groups :]),
        [shape((2 * rows + 16, width), BF)] * groups + [shape((8, LANES), F32)],
        [place, got, first_out, first_mask, norm_params, head_w.T],
        [pltpu.VMEM((PIX * count, LANES), BF), pltpu.VMEM((PIX * count, LANES), BF)],
        near_out=tuple(range(groups)),
    )
    def in_slots(values):
        return jnp.concatenate(
            [lax.dynamic_slice_in_dim(values, (me ^ step) * width, width, 1) for step in range(groups)], 1
        )

    def basis_rows(basis):
        return in_slots(lax.dynamic_slice_in_dim(basis, me * width, width, 0))

    scales_turned = batch_rows(
        jnp.swapaxes(after(scales_second, kept), 1, 2).reshape(TAPS * channels, width)
    )
    rows_first = basis_rows(after(basis_out_first, kept))
    rows_second = basis_rows(after(basis_in_second, kept))
    kept = after(kept, scales_turned, rows_first, rows_second)
    first_slots = exchanged(first_sends, "cout")
    (hidden,) = call(
        lambda *refs: hidden_kernel(refs[0], refs[1 : 1 + groups], *refs[1 + groups :]),
        [shape((rows, channels + LANES), BF)],
        [place, *first_slots, after(mask, kept)],
        near=tuple(range(1, 1 + groups)),
        near_out=(0,),
    )
    other_hidden = swap(hidden, "cin", 1)
    mine, theirs, stats = call(
        lambda *refs: second_kernel(*refs[:4], refs[4 : 4 + groups], *refs[4 + groups :]),
        [shape((rows, half), F32), shape((rows, half), F32), tile],
        [place, hidden, other_hidden, norm_params, *near_weights],
        [
            pltpu.VMEM((2 * rows, channels), BF),
            pltpu.VMEM((TAPS, channels, half), BF),
            pltpu.VMEM((2 * rows, half), F32),
            pltpu.SemaphoreType.DMA((groups,)),
        ],
        near=(1, 2),
        raw=tuple(range(4, 4 + groups)),
        flops=4 * rows * channels * half * TAPS,
    )
    scaled_first, norm_first, head_full = call(
        lambda *refs: gather_kernel(refs[0], refs[1 : 1 + groups], *refs[1 + groups :]),
        [shape(wide, BF), shape((8, channels), F32), shape((16, channels), BF)],
        [place, *first_slots, after(kept, mine)],
    )
    from_other = swap(theirs, "cin", 1)
    got_second = every_device(stats)
    far_weights = [swap(after(slot, mine), "cin", 1) for slot in near_weights]
    head_mask = after(mask, *far_weights)
    second_out, norm_second, dz_second, sums, head_blocks = call(
        functools.partial(head_kernel, sizes),
        [
            shape(wide, F32),
            shape((8, channels), F32),
            shape(wide, F32),
            tile,
            shape((groups, 16, width), F32),
        ],
        [place, mine, from_other, got_second, norm_first, head_mask, head_full, bias_row, own_labels],
        [
            pltpu.VMEM(wide, F32),
            pltpu.VMEM((part, channels), F32),
            pltpu.VMEM((LANES, channels), BF),
        ],
    )
    got = every_device(sums)
    scaled_slots = gathered(after(scaled_first, got_second), "cout")
    grad_second, sums_second, sums, *right_sends = call(
        lambda *refs: second_back_kernel(
            *refs[:10], refs[10 : 10 + groups], refs[10 + groups : 10 + 2 * groups],
            *refs[10 + 2 * groups : 13 + 2 * groups], refs[13 + 2 * groups : 13 + 3 * groups], *refs[13 + 3 * groups :]
        ),
        [shape(wide, BF), shape((8, LANES), F32), shape(sizes + (32, LANES), BF)] + [shape((rows, width), BF)] * groups,
        [
            place, dz_second, second_out, norm_second, got, after(mask, *scaled_slots), scaled_first,
            norm_first, head_blocks, basis_out_first, *near_weights, *far_weights,
        ],
        [
            pltpu.VMEM(wide, BF),
            pltpu.VMEM((TAPS, channels, channels), BF),
            pltpu.VMEM(wide, F32),
            pltpu.SemaphoreType.DMA((3, 2 * groups)),
        ],
        raw=tuple(range(10, 10 + 2 * groups)),
        flops=2 * rows * channels * channels * TAPS,
    )
    left_slots = call(
        lambda *refs: left_second_kernel(*refs[:4], refs[4 : 4 + groups], refs[4 + groups : 4 + 2 * groups], *refs[4 + 2 * groups :]),
        [shape((rows, width), BF)] * groups,
        [place, norm_first, after(all_mask, sums_second), basis_in_second, *scaled_slots],
        [pltpu.VMEM((channels, width), BF), pltpu.VMEM(wide, BF)],
    )
    (right_turned,) = call(
        right_kernel, [shape((channels, rows), BF)], [grad_second, basis_out_second], scalars=0
    )

    def products(sign, big, small, near=()):
        (out,) = call(
            lambda *refs: taps_kernel(sign, refs[:groups], refs[groups : 2 * groups], *refs[2 * groups :]),
            [shape((TAPS * channels, width), BF)],
            [*big, *small],
            [
                pltpu.VMEM((channels, groups * rows), BF),
                pltpu.VMEM((groups * rows, TAPS * width), BF),
            ],
            scalars=0,
            near=near,
            near_out=(0,),
            room=44,
            flops=2 * groups * rows * channels * width * TAPS,
        )
        return out

    right_parts = exchanged(right_sends, "cout")
    got = every_device(sums.reshape(devices, 32, LANES))
    right_slots = gathered(after(right_turned, got), "cout")
    orders = [(axis, bit) for axis in ("cin", "dp") for bit in bits_of(axis)]
    small_old = [norm_mean, norm_square, head_w_mean.T, head_w_square.T, head_b_mean[None], head_b_square[None]]
    def hold(*values):
        def copy_in(*refs):
            arrived = refs[-1]
            copies = [
                pltpu.make_async_copy(refs[at], refs[len(values) + at], arrived.at[at])
                for at in range(len(values))
            ]
            for copy in copies:
                copy.start()
            for copy in copies:
                copy.wait()

        return call(
            lambda *refs: copy_in(*refs),
            [shape(value.shape, value.dtype) for value in values],
            values,
            [pltpu.SemaphoreType.DMA((len(values),))],
            scalars=0,
            raw=tuple(range(len(values))),
            near_out=tuple(range(len(values))),
            room=16,
        )

    def ratio_of(terms, scales_own):
        chunk = shape(scales_own.shape, BF)
        return call(
            lambda *refs: ratio_kernel(refs[: len(terms)], *refs[len(terms) :]),
            [chunk, chunk],
            [*terms, scales_own],
            scalars=0,
            near=tuple(range(len(terms) + 1)),
            near_out=(0, 1),
            room=16,
        )

    def middle_of(slots, basis):
        (out,) = call(
            lambda basis_ref, *refs: middle_kernel(basis_ref, refs[:groups], refs[-1]),
            [shape(slots[0].shape, BF)],
            [basis, *slots],
            scalars=0,
            near=tuple(range(groups + 1)),
            near_out=(0,),
            room=16,
        )
        return out

    near_steps = len(bits_of("cin"))
    left_parts = [left_turned[step] for step in range(groups)]
    *products_first, sums_first, smalls = call(
        lambda *refs: first_products_kernel(
            *refs[:5], refs[5:11], *[refs[11 + at * groups : 11 + (at + 1) * groups] for at in range(3)],
            *refs[11 + 3 * groups :]
        ),
        [shape((TAPS * channels // 2, width), BF)] * 2 + [shape((8, LANES), F32), shape((72, LANES), F32)],
        [
            place, after(got, right_turned, *left_slots), norm_first, all_mask, basis_out_first, *small_old, *left_parts, *right_parts, *scaled_slots,
        ],
        [
            pltpu.VMEM((channels, groups * rows), BF),
            pltpu.VMEM((groups * rows, TAPS * width), BF),
            pltpu.VMEM((groups, rows, width), BF),
            pltpu.VMEM((channels, width), BF),
            pltpu.VMEM((rows, LANES), BF),
            pltpu.VMEM((TAPS * channels, width), BF),
        ],
        near_out=(0, 1),
        room=56,
        flops=2 * groups * rows * channels * width * TAPS,
    )
    terms_first = crossed(products_first, *orders[0])
    for order in orders[1:]:
        terms_first = halved(terms_first, *order)
    own_first = joined([after(terms_first[0], *right_slots), terms_first[1]])
    coeff_first = doubled(own_first, *orders[-1])
    terms_second = [products(1, [after(right_slots[0], own_first)] + right_slots[1:], left_slots)]
    for order in orders:
        terms_second = halved(terms_second, *order)
    for order in reversed(orders[near_steps:-1]):
        coeff_first = doubled(coeff_first, *order)
    coeff_first = batch_gather(coeff_first, ("cin",))
    flat_scales = scales_first.reshape(TAPS * channels, width)
    scales_first_new, ratio_first = call(
        wide_ratio_kernel,
        [shape(flat_scales.shape, F32), shape((TAPS * channels // 2, width), BF)],
        [place, coeff_first, flat_scales],
        near=(1, 2),
        near_out=(1,),
        room=16,
    )
    slots_first = gathered(ratio_first, "cout")
    own_second, ratio_second = ratio_of(terms_second, after(scales_turned, ratio_first))
    weights = hold(after(w_first, own_second), w_second)
    coeff_second = doubled(own_second, *orders[-1])
    middle_second = middle_of(gathered(ratio_second, "cout"), after(rows_second, coeff_second, ratio_first))
    means = hold(after(w_first_mean, weights[0]), w_second_mean)
    middle_first = middle_of(slots_first, after(rows_first, *means))
    gathered_first = doubled(middle_first, "cin", 0)
    squares_old = hold(after(w_first_square, middle_second), w_second_square)
    gathered_second = doubled(middle_second, *orders[-1])
    for order in reversed(orders[near_steps:-1]):
        coeff_second = doubled(coeff_second, *order)
        gathered_second = doubled(after(gathered_second, *squares_old), *order)
    gathered_second = batch_gather(gathered_second, ("cin",))
    coeff_second = batch_gather(coeff_second, ("cin",))

    def scales_of(turned, coeff, scales):
        spec = pl.BlockSpec((3,) + scales.shape[1:], lambda tap: (tap, 0, 0))
        return pl.pallas_call(
            functools.partial(scales_kernel, turned),
            grid=(TAPS // 3,),
            in_specs=[pl.BlockSpec((3 * channels, width), lambda tap: (tap, 0)), spec],
            out_specs=spec,
            out_shape=shape(scales.shape, F32),
            compiler_params=pltpu.CompilerParams(vmem_limit_bytes=12 * 1024 * 1024),
        )(coeff, scales)

    scales_second_new = scales_of(True, coeff_second, scales_second)

    first_grad, second_grad, squares, small_grads = call(
        restore_kernel,
        [shape((TAPS, channels, width), BF), shape((TAPS, width, channels), BF), shape((8, LANES), F32), shape((72, LANES), F32)],
        [
            place,
            basis_in_first,
            gathered_first,
            basis_out_second,
            gathered_second,
            sums_first,
            sums_second,
            smalls,
        ],
        [pltpu.VMEM((channels, TAPS * width), BF)],
        near=tuple(range(1, 8)),
        near_out=(0, 1, 2, 3),
        room=16,
        flops=4 * TAPS * channels * channels * width,
    )
    square_slots = gathered(squares, "cout")
    square_slots[0] = after(square_slots[0], coeff_second)

    smalls = [small_grads]
    small_outs = [shape((2, width), F32)] * 4 + [shape((CLASSES, width), F32)] * 2 + [shape((1, CLASSES), F32)] * 2
    small_outs += [shape((1, 1), F32)] * 2
    first_spec = pl.BlockSpec((3, channels, width), lambda tap: (tap, 0, 0))
    second_spec = pl.BlockSpec((3, width, channels), lambda tap: (tap, 0, 0))
    pair = [first_spec, second_spec]
    first_like, second_like = shape(w_first.shape, F32), shape(w_second.shape, F32)

    def whole(leaf):
        return pl.BlockSpec(leaf.shape, lambda tap: (0,) * len(leaf.shape))

    def update(*refs):
        at = [0]

        def take(number):
            at[0] += number
            return refs[at[0] - number : at[0]]

        update_kernel(
            take(groups), take(2), take(2), take(2), take(2), take(len(smalls)),
            take(2), take(2), take(2), take(len(small_outs) - 2), take(2), take(1)[0],
        )

    results = pl.pallas_call(
        update,
        grid=(TAPS // 3,),
        scratch_shapes=[pltpu.VMEM((8, LANES), F32)],
        in_specs=[pl.BlockSpec(memory_space=pltpu.VMEM)] * (groups + 8 + len(smalls)),
        out_specs=pair * 3 + [whole(leaf) for leaf in small_outs],
        out_shape=[first_like, second_like] * 3 + small_outs,
        compiler_params=pltpu.CompilerParams(vmem_limit_bytes=16 * 1024 * 1024),
    )(
        *square_slots, *weights, *means, *squares_old,
        first_grad, second_grad, *smalls,
    )
    (first_new, second_new, first_mean_new, second_mean_new, first_square_new, second_square_new,
     norm_first_mean, norm_first_square, norm_second_mean, norm_second_square,
     head_mean_new, head_square_new, bias_mean_new, bias_square_new, grad_norm, loss_total) = results
    return (
        loss_total.reshape(()),
        grad_norm.reshape(()),
        first_new,
        first_mean_new,
        first_square_new,
        second_new,
        second_mean_new,
        second_square_new,
        norm_first_mean,
        norm_first_square,
        norm_second_mean,
        norm_second_square,
        head_mean_new.T,
        head_square_new.T,
        bias_mean_new[0],
        bias_square_new[0],
        scales_first_new.reshape(scales_first.shape),
        scales_second_new,
    )


def solution(mesh):
    return jax.shard_map(
        local,
        mesh=mesh,
        in_specs=(
            P(None, ("dp", "cin"), None),
            P(None, ("dp", "cin")),
            P(("dp", "cin")),
            P(None, None, "cout"),
            P(None, "cout", None),
            P(None, "cout"),
            P("cout", None),
            P(),
            P(),
            P(None, None, "cout"),
            P(None, "cout", None),
            P(None, None, "cout"),
            P(None, None, "cout"),
            P(None, "cout", None),
            P(None, "cout", None),
            P(None, "cout"),
            P(None, "cout"),
            P("cout", None),
            P("cout", None),
            P(),
            P(),
        ),
        out_specs=(
            P(),
            P(),
            P(None, None, "cout"),
            P(None, None, "cout"),
            P(None, None, "cout"),
            P(None, "cout", None),
            P(None, "cout", None),
            P(None, "cout", None),
            P(None, "cout"),
            P(None, "cout"),
            P(None, "cout"),
            P(None, "cout"),
            P("cout", None),
            P("cout", None),
            P(),
            P(),
            P(None, None, "cout"),
            P(None, "cout", None),
        ),
        check_vma=False,
    )
```

```python
import functools
import math

import jax
import jax.numpy as jnp
from jax import lax
from jax.experimental import pallas as pl
from jax.experimental.pallas import tpu as pltpu
from jax.sharding import PartitionSpec as P

CLASSES = 10
SIDE = 4
PIX = 16
TAPS = 9
STEP = 10
LANES = 128

EPS_NORM = 1e-05
SCALE_DECAY = 0.95
DAMPING = 0.001
CLIP_NORM = 1.0
LEARN_RATE = 0.01
BETA_ONE = 0.9
BETA_TWO = 0.999
ADAM_EPS = 1e-08
WEIGHT_DECAY = 0.01
SMOOTH = 0.1
OFFSETS = [(row_step, col_step) for row_step in (-1, 0, 1) for col_step in (-1, 0, 1)]
EVERY = ("dp", "cout", "cin")
BF = jnp.bfloat16
F32 = jnp.float32
PRECISE = lax.Precision.HIGHEST
NN = (((1,), (0,)), ((), ()))
NT = (((1,), (1,)), ((), ()))
TN = (((0,), (0,)), ((), ()))


def matmul(left, right, dims=NN, precision=None):
    return lax.dot_general(
        left, right, dims, precision=precision, preferred_element_type=F32
    )


def runs(row_step, col_step, count):
    low, high = max(0, -col_step), min(SIDE, SIDE - col_step)
    found = []
    for row in range(max(0, -row_step), min(SIDE, SIDE - row_step)):
        to_row = (row * SIDE + low) * count
        from_row = ((row + row_step) * SIDE + low + col_step) * count
        length = (high - low) * count
        if found and found[-1][0] + found[-1][2] == to_row and found[-1][1] + found[-1][2] == from_row:
            found[-1] = (found[-1][0], found[-1][1], found[-1][2] + length)
        else:
            found.append((to_row, from_row, length))
    return found


class Late:
    def __init__(self, ref, copy):
        self.ref, self.copy, self.shape = ref, copy, ref.shape
        copy.start()

    def settle(self):
        if self.copy is not None:
            self.copy.wait()
        self.copy = None

    def __getitem__(self, index):
        self.settle()
        return self.ref[index]


class Result:
    def __init__(self, ref, copy):
        self.ref, self.copy, self.shape, self.sent = ref, copy, ref.shape, False

    def __getitem__(self, index):
        return self.ref[index]

    def __setitem__(self, index, values):
        self.ref[index] = values

    def send(self):
        if not self.sent:
            self.copy.start()
        self.sent = True


def call(kernel, outs, args, scratch=(), scalars=1, near=(), raw=(), near_out=(), flops=0, room=60):
    n_in, n_out = len(args), len(outs)
    copied = [at for at in range(scalars, n_in) if at not in near and at not in raw]
    copied_out = [at for at in range(n_out) if at not in near_out]

    def body(*refs):
        ins, results = list(refs[:n_in]), list(refs[n_in : n_in + n_out])
        rest = refs[n_in + n_out :]
        held, held_out = rest[: len(copied)], rest[len(copied) : len(copied) + len(copied_out)]
        own, arrived = rest[len(copied) + len(copied_out) : -1], rest[-1]
        for nth, at in enumerate(copied):
            ins[at] = Late(held[nth], pltpu.make_async_copy(ins[at], held[nth], arrived.at[nth]))
        for nth, at in enumerate(copied_out):
            copy = pltpu.make_async_copy(held_out[nth], results[at], arrived.at[len(copied) + nth])
            results[at] = Result(held_out[nth], copy)
        kernel(*ins, *results, *own)
        for at in copied:
            ins[at].settle()
        for at in copied_out:
            results[at].send()
        for at in copied_out:
            results[at].copy.wait()

    specs = [pl.BlockSpec(memory_space=pltpu.SMEM)] * scalars
    specs += [
        pl.BlockSpec(memory_space=pltpu.VMEM if at in near else pltpu.HBM) for at in range(scalars, n_in)
    ]
    moved = sum(math.prod(a.shape) * a.dtype.itemsize for a in list(args) + list(outs))
    return pl.pallas_call(
        body,
        out_shape=list(outs),
        in_specs=specs,
        out_specs=[
            pl.BlockSpec(memory_space=pltpu.VMEM if at in near_out else pltpu.HBM) for at in range(n_out)
        ],
        scratch_shapes=[pltpu.VMEM(args[at].shape, args[at].dtype) for at in copied]
        + [pltpu.VMEM(outs[at].shape, outs[at].dtype) for at in copied_out]
        + list(scratch)
        + [pltpu.SemaphoreType.DMA((max(1, len(copied) + len(copied_out)),))],
        compiler_params=pltpu.CompilerParams(vmem_limit_bytes=room * 1024 * 1024),
        cost_estimate=pl.CostEstimate(flops=flops, bytes_accessed=moved, transcendentals=0),
    )(*args)


def shape(dims, dtype):
    return jax.ShapeDtypeStruct(dims, dtype)


def gelu_parts(values):
    rate = math.sqrt(2.0 / math.pi)
    bend = jnp.tanh(rate * (values + 0.044715 * values * values * values))
    share = 0.5 * (1.0 + bend)
    slope = share + 0.5 * values * (1.0 - bend * bend) * rate * (1.0 + 0.134145 * values * values)
    return values * share, slope


def fill_mask(masks_ref, mask_ref):
    count = masks_ref.shape[1]
    same = lax.broadcasted_iota(jnp.int32, (count, count), 0) == lax.broadcasted_iota(
        jnp.int32, (count, count), 1
    )
    for pixel in range(PIX):
        row = masks_ref[pixel : pixel + 1, :].astype(F32)
        column = jnp.sum(jnp.where(same, row, 0.0), axis=1, keepdims=True)
        mask_ref[pixel * count : (pixel + 1) * count, :] = jnp.broadcast_to(column, (count, LANES))


def fill_inputs(images_ref, mask_ref, inputs_ref):
    low = mask_ref[...].astype(BF)
    for lane in range(0, images_ref.shape[1], LANES):
        inputs_ref[:, lane : lane + LANES] = images_ref[:, lane : lane + LANES] * low


def first_kernel(
    groups, place_ref, images_ref, masks_ref, weight_ref,
    sum_ref, all_mask_ref, stats_ref, own_mask_ref, mask_ref, inputs_ref, low_ref, wide_ref, arrived,
):
    count = masks_ref.shape[1]
    part = count // groups
    me = place_ref[0]
    copies = [
        pltpu.make_async_copy(weight_ref.at[at : at + 3], wide_ref.at[at : at + 3], arrived.at[at // 3])
        for at in range(0, TAPS, 3)
    ]
    for copy in copies:
        copy.start()
    fill_mask(masks_ref, mask_ref)
    fill_inputs(images_ref, mask_ref, inputs_ref)
    all_mask_ref[...] = mask_ref[...].astype(BF)
    all_mask_ref.send()
    for pixel in range(PIX):
        own = pl.multiple_of(pixel * count + me * part, part)
        own_mask_ref[pixel * part : (pixel + 1) * part, :] = mask_ref[pl.ds(own, part), :]
    own_mask_ref.send()
    for tap in range(TAPS):
        if tap % 3 == 0:
            copies[tap // 3].wait()
        low_ref[:, tap * LANES : (tap + 1) * LANES] = wide_ref[tap].astype(BF)
    sum_ref[...] = jnp.zeros(sum_ref.shape, F32)
    for tap in range(0, TAPS, 2):
        taps = min(2, TAPS - tap)
        product = matmul(inputs_ref[...], low_ref[:, tap * LANES : (tap + taps) * LANES])
        for nth in range(taps):
            for to_row, from_row, length in runs(*OFFSETS[tap + nth], count):
                sum_ref[to_row : to_row + length, :] += product[
                    from_row : from_row + length, nth * LANES : (nth + 1) * LANES
                ]
    sum_ref.send()
    mask = mask_ref[...]
    total = sum_ref[...]
    masked = total * mask
    tile = jnp.concatenate(
        [
            jnp.sum(masked, axis=0, keepdims=True),
            jnp.sum(masked * total, axis=0, keepdims=True),
            jnp.sum(mask, axis=0, keepdims=True),
            jnp.zeros((5, LANES), F32),
        ],
        axis=0,
    )
    stats_ref[...] = jnp.broadcast_to(tile[None], stats_ref.shape)


def first_norm_kernel(
    place_ref, got_ref, first_ref, mask_ref, params_ref, head_ref, send_refs, kept_ref, hidden_ref, scaled_ref
):
    total = total_of(got_ref)
    kept = total[2:3, :]
    mean = total[0:1, :] / kept
    rstd = lax.rsqrt(total[1:2, :] / kept - mean * mean + EPS_NORM)
    kept_ref[...] = jnp.broadcast_to(kept, kept_ref.shape)
    gain, shift = params_ref[0:1, :], params_ref[1:2, :]
    count = first_ref.shape[0] // PIX
    part = count // len(send_refs)
    scaled = (first_ref[...] - mean) * rstd
    value, _ = gelu_parts(gain * scaled + shift)
    hidden_ref[...] = (value * mask_ref[...].astype(F32)).astype(BF)
    scaled_ref[...] = scaled.astype(BF)
    lines = [head_ref[...]]
    for line in (rstd, gain, shift):
        high = line.astype(BF).astype(F32)
        lines += [high, line - high]
    extra = jnp.concatenate(lines, axis=0).astype(BF)
    rows = PIX * part
    for step, send_ref in enumerate(send_refs):
        for pixel in range(PIX):
            base = pl.ds(pl.multiple_of(pixel * count + (place_ref[0] ^ step) * part, part), part)
            send_ref[pixel * part : (pixel + 1) * part, :] = hidden_ref[base, :]
            send_ref[rows + pixel * part : rows + (pixel + 1) * part, :] = scaled_ref[base, :]
        send_ref[2 * rows : 2 * rows + 16, :] = extra


def hidden_kernel(place_ref, slot_refs, mask_ref, hidden_ref):
    rows = hidden_ref.shape[0]
    for step, slot_ref in enumerate(slot_refs):
        lanes = pl.ds(pl.multiple_of((place_ref[0] ^ step) * LANES, LANES), LANES)
        hidden_ref[:, lanes] = slot_ref[0:rows, :]
    hidden_ref[:, len(slot_refs) * LANES :] = mask_ref[...].astype(BF)


def gather_kernel(place_ref, slot_refs, kept_ref, scaled_ref, norm_ref, head_ref):
    rows = scaled_ref.shape[0]
    norm_ref[0:1, :] = jnp.zeros((1, norm_ref.shape[1]), F32)
    norm_ref[5:8, :] = jnp.zeros((3, norm_ref.shape[1]), F32)
    for step, slot_ref in enumerate(slot_refs):
        lanes = pl.ds(pl.multiple_of((place_ref[0] ^ step) * LANES, LANES), LANES)
        scaled_ref[:, lanes] = slot_ref[rows : 2 * rows, :]
        extra = slot_ref[2 * rows : 2 * rows + 16, :].astype(F32)
        line = lax.broadcasted_iota(jnp.int32, (16, LANES), 0)
        head_ref[:, lanes] = jnp.where(line < CLASSES, extra, 0.0).astype(BF)
        for at in range(3):
            norm_ref[at + 1 : at + 2, lanes] = (
                extra[CLASSES + 2 * at : CLASSES + 2 * at + 1, :] + extra[CLASSES + 2 * at + 1 : CLASSES + 2 * at + 2, :]
            )
        norm_ref[4:5, lanes] = kept_ref[0:1, :]


def second_kernel(
    place_ref, own_ref, other_ref, params_ref, slot_refs,
    mine_ref, theirs_ref, stats_ref, inputs_ref, weight_ref, sum_ref, arrived,
):
    me = place_ref[0]
    rows = own_ref.shape[0]
    part = rows // PIX
    depth, half = slot_refs[0].shape[1:]
    copies = []
    for step, slot_ref in enumerate(slot_refs):
        span = pl.ds(pl.multiple_of((me ^ step) * depth, depth), depth)
        copies.append(pltpu.make_async_copy(slot_ref, weight_ref.at[:, span, :], arrived.at[step]))
        copies[-1].start()
    channels = inputs_ref.shape[1]
    inputs_ref[0:rows, :] = own_ref[:, 0:channels]
    inputs_ref[rows : 2 * rows, :] = other_ref[:, 0:channels]
    sum_ref[...] = jnp.zeros_like(sum_ref)
    for copy in copies:
        copy.wait()
    for tap in range(TAPS):
        product = matmul(inputs_ref[...], weight_ref[tap])
        for to_row, from_row, length in runs(*OFFSETS[tap], part):
            for base in (0, rows):
                sum_ref[base + to_row : base + to_row + length, :] += product[
                    base + from_row : base + from_row + length, :
                ]
    mine_ref[...] = sum_ref[0:rows, :]
    theirs_ref[...] = sum_ref[rows : 2 * rows, :]
    lines = [[], []]
    for lane in range(0, half, LANES):
        first = square = None
        for base, ref in ((0, own_ref), (rows, other_ref)):
            total = sum_ref[base : base + rows, lane : lane + LANES]
            masked = total * ref[:, channels : channels + LANES].astype(F32)
            first_part = jnp.sum(masked, axis=0, keepdims=True)
            square_part = jnp.sum(masked * total, axis=0, keepdims=True)
            first = first_part if first is None else first + first_part
            square = square_part if square is None else square + square_part
        lines[0].append(first)
        lines[1].append(square)
    spare = 8 - 2 * (half // LANES) - 2
    tile = jnp.concatenate(
        lines[0] + lines[1] + [params_ref[2:4, :], jnp.zeros((spare, LANES), F32)], axis=0
    )
    stats_ref[...] = jnp.broadcast_to(tile[None], stats_ref.shape)


def head_kernel(
    sizes, place_ref, mine_ref, got_ref_rows, got_ref, norm_first_ref, mask_ref, head_ref, bias_ref, labels_ref,
    wide_ref, norm_ref, dz_ref, sums_ref, head_out_ref, slope_ref, pooled_ref, weight_ref,
):
    count_dp, groups, count_cin = sizes
    side = place_ref[1]
    rows, half = mine_ref.shape
    part = rows // PIX
    blocks = half // LANES
    wide_ref[:, pl.ds(pl.multiple_of(side * half, half), half)] = mine_ref[...]
    wide_ref[:, pl.ds(pl.multiple_of((1 - side) * half, half), half)] = got_ref_rows[...]
    totals = [None, None]
    for source in range(count_dp * groups * count_cin):
        which = source % count_cin % 2
        tile = got_ref[source]
        totals[which] = tile if totals[which] is None else totals[which] + tile
    kept = norm_first_ref[4:5, 0:LANES]
    mask = mask_ref[...]
    for group in range(groups):
        lanes = slice(group * LANES, (group + 1) * LANES)
        total, line = totals[group // blocks], group % blocks
        mean = total[line : line + 1, :] / kept
        rstd = lax.rsqrt(total[blocks + line : blocks + line + 1, :] / kept - mean * mean + EPS_NORM)
        single = got_ref[group * count_cin]
        gain = single[2 * blocks : 2 * blocks + 1, :]
        shift = single[2 * blocks + 1 : 2 * blocks + 2, :]
        norm_ref[0:1, lanes] = mean
        norm_ref[1:2, lanes] = rstd
        norm_ref[2:3, lanes] = gain
        norm_ref[3:4, lanes] = shift
        norm_ref[4:8, lanes] = jnp.broadcast_to(kept, (4, LANES))
        value, slope = gelu_parts(gain * ((wide_ref[:, lanes] - mean) * rstd) + shift)
        slope_ref[:, lanes] = slope * mask * (1.0 / PIX)
        pooled_ref[:, lanes] = jnp.sum((value * mask).reshape(PIX, part, LANES), axis=0) * (1.0 / PIX)
    wide_ref.send()
    norm_ref.send()
    weight_ref[0:16, :] = head_ref[...]
    weight_ref[16:LANES, :] = jnp.zeros((LANES - 16, weight_ref.shape[1]), BF)
    pooled = pooled_ref[...].astype(BF)
    head = weight_ref[...]
    class_index = lax.broadcasted_iota(jnp.int32, (part, LANES), 1)
    logits = matmul(pooled, head, NT) + bias_ref[...]
    logits = jnp.where(class_index < CLASSES, logits, -1e30)
    logits = logits - jnp.max(logits, axis=1, keepdims=True)
    log_probs = logits - jnp.log(jnp.sum(jnp.exp(logits), axis=1, keepdims=True))
    same = lax.broadcasted_iota(jnp.int32, (part, part), 0) == lax.broadcasted_iota(
        jnp.int32, (part, part), 1
    )
    label = jnp.sum(jnp.where(same, labels_ref[...].astype(F32), 0.0), axis=1, keepdims=True)
    wanted = jnp.where(class_index.astype(F32) == label, 1.0 - SMOOTH, 0.0) + SMOOTH / CLASSES
    wanted = jnp.where(class_index < CLASSES, wanted, 0.0)
    loss = -jnp.sum(jnp.sum(wanted * log_probs, axis=1, keepdims=True), axis=0, keepdims=True)
    logit_grad = jnp.exp(log_probs) - wanted
    head_grad = matmul(logit_grad, pooled.astype(F32), TN, PRECISE)
    pooled_grad = matmul(logit_grad, head.astype(F32), NN, PRECISE)
    extra = jnp.sum(logit_grad, axis=0, keepdims=True)
    extra = jnp.where(class_index[0:1, :] == CLASSES, loss, extra)
    line = lax.broadcasted_iota(jnp.int32, (16, LANES), 0)
    gains, shifts = [], []
    for group in range(groups):
        lanes = slice(group * LANES, (group + 1) * LANES)
        head_out_ref[group] = jnp.where(line == CLASSES, extra, head_grad[0:16, lanes])
        spread = jnp.broadcast_to(pooled_grad[:, lanes][None], (PIX, part, LANES)).reshape(rows, LANES)
        dz = slope_ref[:, lanes] * spread
        dz_ref[:, lanes] = dz
        scaled = (wide_ref[:, lanes] - norm_ref[0:1, lanes]) * norm_ref[1:2, lanes]
        gains.append(jnp.sum(dz * scaled, axis=0, keepdims=True))
        shifts.append(jnp.sum(dz, axis=0, keepdims=True))
    sums_ref[...] = jnp.broadcast_to(jnp.concatenate(gains + shifts, axis=0)[None], sums_ref.shape)


def total_of(got_ref):
    total = got_ref[0]
    for source in range(1, got_ref.shape[0]):
        total = total + got_ref[source]
    return total


def norm_back(scaled, dz, norm, mask, gain_grad, shift_grad):
    gain = norm[2:3, :]
    return norm[1:2, :] * (
        gain * dz - mask * (gain / norm[4:5, :]) * (shift_grad + scaled * gain_grad)
    )


def second_back_kernel(
    place_ref, dz_ref, wide_ref, norm_ref, got_ref, mask_ref, first_ref, norm_first_ref, head_ref, basis_ref, near_refs, far_refs,
    grad_ref, sums_out_ref, sums_ref, send_refs, part_ref, weight_ref, sum_ref, arrived,
):
    me, side = place_ref[0], place_ref[1]
    depth, half = near_refs[0].shape[1:]
    copies = {}
    for tap in range(0, TAPS, 3):
        for which, (refs, at) in enumerate(((near_refs, side), (far_refs, 1 - side))):
            lanes = pl.ds(pl.multiple_of(at * half, half), half)
            for step, slot_ref in enumerate(refs):
                span = pl.ds(pl.multiple_of((me ^ step) * depth, depth), depth)
                number = which * len(refs) + step
                copies[tap, number] = pltpu.make_async_copy(
                    slot_ref.at[tap : tap + 3], weight_ref.at[tap : tap + 3, span, lanes], arrived.at[tap // 3, number]
                )
                copies[tap, number].start()
    total = total_of(got_ref)
    sums_out_ref[...] = total
    groups = total.shape[0] // 2
    mask = mask_ref[...]
    for group in range(groups):
        lanes = slice(group * LANES, (group + 1) * LANES)
        norm = norm_ref[:, lanes]
        grad_ref[:, lanes] = norm_back(
            (wide_ref[:, lanes] - norm[0:1, :]) * norm[1:2, :], dz_ref[:, lanes], norm, mask,
            total[group : group + 1, :], total[groups + group : groups + group + 1, :],
        ).astype(BF)
    grad_ref.send()
    sums_out_ref.send()
    rows, channels = grad_ref.shape
    part = rows // PIX
    sum_ref[...] = jnp.zeros_like(sum_ref)
    for tap in range(TAPS):
        if tap % 3 == 0:
            for number in range(2 * len(near_refs)):
                copies[tap, number].wait()
        product = matmul(grad_ref[...], weight_ref[tap], NT)
        row_step, col_step = OFFSETS[tap]
        for to_row, from_row, length in runs(-row_step, -col_step, part):
            sum_ref[to_row : to_row + length, :] += product[from_row : from_row + length, :]
    gains, shifts = [], []
    for lane in range(0, channels, LANES):
        lanes = slice(lane, lane + LANES)
        norm = norm_first_ref[:, lanes]
        scaled = first_ref[:, lanes].astype(F32)
        _, slope = gelu_parts(norm[2:3, :] * scaled + norm[3:4, :])
        dz = slope * mask * sum_ref[:, lanes]
        part_ref[:, lanes] = (norm[1:2, :] * norm[2:3, :] * dz).astype(BF)
        gains.append(jnp.sum(dz * scaled, axis=0, keepdims=True))
        shifts.append(jnp.sum(dz, axis=0, keepdims=True))
    sum_ref[...] = matmul(part_ref[...], basis_ref[...])
    send_columns(me, sum_ref, send_refs)
    count_dp, _, count_cin = sums_ref.shape[:3]
    for group in range(groups):
        tile = jnp.concatenate(gains + shifts + [head_ref[group], jnp.zeros((8, LANES), F32)], axis=0)
        tile = tile.astype(BF)
        for far in range(count_dp):
            for near in range(count_cin):
                sums_ref[far, group, near] = tile


def first_products_kernel(
    place_ref, got_ref, norm_ref, mask_ref, basis_ref, old_refs, big_refs, part_refs, scaled_refs,
    kept_ref, sent_ref, sums_ref, small_ref, left_ref, right_ref, slot_ref, column_ref, mask_slot_ref, out_ref,
):
    me = place_ref[0]
    rows, width = part_refs[0].shape
    part = rows // PIX
    count = mask_ref.shape[0] // PIX
    whole = got_ref[0].astype(F32)
    for source in range(1, got_ref.shape[0]):
        whole = whole + got_ref[source].astype(F32)
    sums_ref[...] = whole[0:8, :]
    small_ref[...] = jnp.zeros(small_ref.shape, F32)
    small_ref[8:24, :] = whole[8:24, :]
    for at, row in enumerate((24, 28, 32, 48, 64, 65)):
        lines, lanes = old_refs[at].shape
        small_ref[row : row + lines, 0:lanes] = old_refs[at][...]
    groups = len(part_refs)
    column_ref[...] = basis_ref[:, pl.ds(pl.multiple_of(me * width, width), width)]
    rates, shifts = [], []
    for group in range(groups):
        lanes = slice(group * LANES, (group + 1) * LANES)
        scale = norm_ref[1:2, lanes] * norm_ref[2:3, lanes] / norm_ref[4:5, lanes]
        rates.append(scale * whole[group : group + 1, :])
        shifts.append(scale * whole[groups + group : groups + group + 1, :])
    rate = jnp.concatenate(rates, axis=1)
    shift = jnp.broadcast_to(jnp.concatenate(shifts, axis=1), (8, groups * LANES))
    fixed = matmul(shift, column_ref[...].astype(F32), NN, PRECISE)[0:1, :]
    for step in range(groups):
        for pixel in range(PIX):
            base = pl.ds(pl.multiple_of(pixel * count + (me ^ step) * part, part), part)
            mask_slot_ref[pixel * part : (pixel + 1) * part, :] = mask_ref[base, :]
        moved = matmul((scaled_refs[step][...].astype(F32) * rate).astype(BF), column_ref[...])
        slot_ref[step] = (
            part_refs[step][...].astype(F32) - mask_slot_ref[...].astype(F32) * (fixed + moved)
        ).astype(BF)
    taps_kernel(-1, big_refs, [slot_ref.at[step] for step in range(groups)], out_ref, left_ref, right_ref)
    half = kept_ref.shape[0]
    sent_ref[...] = out_ref[pl.ds(pl.multiple_of((1 - place_ref[1]) * half, half), half), :]
    kept_ref[...] = out_ref[pl.ds(pl.multiple_of(place_ref[1] * half, half), half), :]


def left_second_kernel(place_ref, norm_ref, mask_ref, basis_ref, scaled_refs, left_refs, column_ref, wide_ref):
    me = place_ref[0]
    rows, width = left_refs[0].shape
    part = rows // PIX
    count = mask_ref.shape[0] // PIX
    column_ref[...] = basis_ref[:, pl.ds(pl.multiple_of(me * width, width), width)]
    for step, scaled_ref in enumerate(scaled_refs):
        mask = jnp.concatenate(
            [
                mask_ref[pl.ds(pl.multiple_of(pixel * count + (me ^ step) * part, part), part), :]
                for pixel in range(PIX)
            ],
            axis=0,
        ).astype(F32)
        for lane in range(0, wide_ref.shape[1], LANES):
            lanes = slice(lane, lane + LANES)
            value, _ = gelu_parts(
                norm_ref[2:3, lanes] * scaled_ref[:, lanes].astype(F32) + norm_ref[3:4, lanes]
            )
            wide_ref[:, lanes] = (value * mask).astype(BF)
        left_refs[step][...] = matmul(wide_ref[...], column_ref[...]).astype(BF)


def right_kernel(grad_ref, basis_ref, right_ref):
    right_ref[...] = jnp.transpose(matmul(grad_ref[...], basis_ref[...])).astype(BF)


def send_columns(me, product_ref, send_refs):
    for step, send_ref in enumerate(send_refs):
        lanes = pl.ds(pl.multiple_of((me ^ step) * LANES, LANES), LANES)
        send_ref[...] = product_ref[:, lanes].astype(BF)


def left_first_kernel(place_ref, images_ref, masks_ref, basis_ref, left_ref, mask_ref, inputs_ref, part_ref):
    slots = left_ref.shape[0]
    count = masks_ref.shape[1]
    part = count // slots
    me = place_ref[0]
    fill_mask(masks_ref, mask_ref)
    fill_inputs(images_ref, mask_ref, inputs_ref)
    for step in range(slots):
        for pixel in range(PIX):
            base = pl.multiple_of(pixel * count + (me ^ step) * part, part)
            part_ref[pixel * part : (pixel + 1) * part, :] = inputs_ref[pl.ds(base, part), :]
        left_ref[step] = jnp.transpose(matmul(part_ref[...], basis_ref[...])).astype(BF)


def pick_kernel(own_ref, full_ref, kept_ref, sent_ref):
    half = kept_ref.shape[0]
    kept_ref[...] = full_ref[pl.ds(pl.multiple_of(own_ref[0] * half, half), half), :]
    sent_ref[...] = full_ref[pl.ds(pl.multiple_of((1 - own_ref[0]) * half, half), half), :]


def split_kernel(own_ref, here_ref, came_ref, kept_ref, sent_ref):
    half = kept_ref.shape[0]
    for which, ref in ((own_ref[0], kept_ref), (1 - own_ref[0], sent_ref)):
        rows = pl.ds(pl.multiple_of(which * half, half), half)
        ref[...] = (here_ref[rows, :].astype(F32) + came_ref[rows, :].astype(F32)).astype(BF)


def merge_kernel(own_ref, here_ref, came_ref, out_ref):
    rows = here_ref.shape[0]
    for choice in range(2):

        @pl.when(own_ref[0] == choice)
        def _():
            out_ref[choice * rows : (choice + 1) * rows, :] = here_ref[...]
            out_ref[(1 - choice) * rows : (2 - choice) * rows, :] = came_ref[...]


def taps_kernel(sign, big_refs, small_refs, out_ref, left_ref, right_ref):
    rows, width = small_refs[0].shape
    channels = big_refs[0].shape[0]
    part = rows // PIX
    right_ref[...] = jnp.zeros_like(right_ref)
    for slot, (big_ref, small_ref) in enumerate(zip(big_refs, small_refs)):
        base = slot * rows
        left_ref[:, base : base + rows] = big_ref[...]
        for tap, (row_step, col_step) in enumerate(OFFSETS):
            for to_row, from_row, length in runs(sign * row_step, sign * col_step, part):
                right_ref[base + to_row : base + to_row + length, tap * width : (tap + 1) * width] = (
                    small_ref[from_row : from_row + length, :]
                )
    for tap in range(0, TAPS, 2):
        taps = min(2, TAPS - tap)
        product = matmul(left_ref[...], right_ref[:, tap * width : (tap + taps) * width])
        for nth in range(taps):
            out_ref[(tap + nth) * channels : (tap + nth + 1) * channels, :] = product[
                :, nth * width : (nth + 1) * width
            ].astype(BF)


def ratio_kernel(own_refs, scales_ref, coeff_ref, ratio_ref):
    coeff = None
    for ref in own_refs:
        coeff = ref[...].astype(F32) if coeff is None else coeff + ref[...].astype(F32)
    scales = SCALE_DECAY * scales_ref[...] + (1.0 - SCALE_DECAY) * coeff * coeff
    coeff_ref[...] = coeff.astype(BF)
    ratio_ref[...] = (coeff / (scales + DAMPING)).astype(BF)


def middle_kernel(basis_ref, slot_refs, out_ref):
    width = slot_refs[0].shape[1]
    ratio = jnp.concatenate([ref[...] for ref in slot_refs], axis=1)
    out_ref[...] = matmul(ratio, basis_ref[...], NT).astype(BF)


def scales_kernel(turned, coeff_ref, scales_ref, out_ref):
    taps = out_ref.shape[0]
    rows = coeff_ref.shape[0] // taps
    for tap in range(taps):
        coeff = coeff_ref[tap * rows : (tap + 1) * rows, :].astype(F32)
        if turned:
            coeff = jnp.transpose(coeff)
        out_ref[tap] = SCALE_DECAY * scales_ref[tap] + (1.0 - SCALE_DECAY) * coeff * coeff


def wide_ratio_kernel(place_ref, coeff_ref, scales_ref, scales_out_ref, ratio_ref):
    half = ratio_ref.shape[0]
    rows = pl.ds(pl.multiple_of(place_ref[1] * half, half), half)
    coeff = coeff_ref[...].astype(F32)
    scales_out_ref[...] = SCALE_DECAY * scales_ref[...] + (1.0 - SCALE_DECAY) * coeff * coeff
    scales_out_ref.send()
    ratio_ref[...] = (coeff_ref[rows, :].astype(F32) / (scales_out_ref[rows, :] + DAMPING)).astype(BF)


def add_squares(total, values):
    return total + jnp.sum((values * values).reshape(-1, 8, LANES), axis=0)


def restore_kernel(
    place_ref, basis_in_ref, middle_first_ref, basis_out_ref, middle_second_ref, sums_first_ref, sums_second_ref,
    old_ref, first_ref, second_ref, squares_ref, small_ref, stack_ref,
):
    me = place_ref[0]
    channels = basis_in_ref.shape[0]
    total = jnp.zeros((8, LANES), F32)
    for tap in range(TAPS):
        product = matmul(
            middle_second_ref[tap * channels : (tap + 1) * channels, :], basis_out_ref[...], (((0,), (1,)), ((), ()))
        )
        second_ref[tap] = product.astype(BF)
        for lane in range(0, channels, LANES):
            total = add_squares(total, product[:, lane : lane + LANES])
    for tap in range(TAPS):
        stack_ref[:, tap * LANES : (tap + 1) * LANES] = middle_first_ref[
            tap * channels : (tap + 1) * channels, :
        ]
    for tap in range(0, TAPS, 2):
        taps = min(2, TAPS - tap)
        product = matmul(basis_in_ref[...], stack_ref[:, tap * LANES : (tap + taps) * LANES])
        for nth in range(taps):
            block = product[:, nth * LANES : (nth + 1) * LANES]
            first_ref[tap + nth] = block.astype(BF)
            total = add_squares(total, block)
    groups = sums_first_ref.shape[0] // 2
    row = lax.broadcasted_iota(jnp.int32, (8, LANES), 0)
    mine = (row == me) | (row == me + groups)
    for ref in (sums_first_ref, sums_second_ref):
        total = total + jnp.where(mine, ref[...] * ref[...], 0.0)
    line = lax.broadcasted_iota(jnp.int32, (16, LANES), 0)
    lane = lax.broadcasted_iota(jnp.int32, (16, LANES), 1)
    counted = (line < CLASSES) | ((line == CLASSES) & (lane < CLASSES) & (me == 0))
    head = jnp.where(counted, old_ref[8:24, :], 0.0)
    small_ref[...] = old_ref[...]
    for at, ref in enumerate((sums_first_ref, sums_second_ref)):
        small_ref[2 * at : 2 * at + 1, :] = ref[pl.ds(me, 1), :]
        small_ref[2 * at + 1 : 2 * at + 2, :] = ref[pl.ds(me + groups, 1), :]
    squares_ref[...] = add_squares(total, head)


def update_kernel(
    square_refs, weight_refs, mean_refs, square_moment_refs, grad_refs, small_refs,
    weight_outs, mean_outs, square_outs, small_outs, scalar_outs, norm_ref,
):
    @pl.when(pl.program_id(0) == 0)
    def _():
        parts = [ref[...] for ref in square_refs]
        while len(parts) > 1:
            parts = [parts[at] + parts[at + 1] for at in range(0, len(parts), 2)]
        total = jnp.sum(jnp.sum(parts[0], axis=1, keepdims=True), axis=0, keepdims=True)
        found = jnp.sqrt(total)
        norm_ref[0:1, :] = jnp.broadcast_to(found, (1, LANES))
        norm_ref[1:2, :] = jnp.broadcast_to(CLIP_NORM / jnp.maximum(found, CLIP_NORM), (1, LANES))

    grad_norm, factor = norm_ref[0:1, 0:1], norm_ref[1:2, 0:1]

    def moments(gradient, mean_old, square_old):
        mean_new = BETA_ONE * mean_old + (1.0 - BETA_ONE) * gradient
        square_new = BETA_TWO * square_old + (1.0 - BETA_TWO) * gradient * gradient
        return mean_new, square_new

    taps = mean_outs[0].shape[0]
    for at in range(len(weight_refs)):
        for nth in range(taps):
            tap = pl.program_id(0) * taps + nth
            gradient = grad_refs[at][tap].astype(F32) * factor
            mean_new, square_new = moments(gradient, mean_refs[at][tap], square_moment_refs[at][tap])
            mean_outs[at][nth] = mean_new
            square_outs[at][nth] = square_new
            square_hat = square_new * (1.0 / (1.0 - BETA_TWO**STEP))
            size = square_hat * lax.rsqrt(square_hat) + ADAM_EPS
            step = mean_new * (LEARN_RATE / (1.0 - BETA_ONE**STEP)) / size
            weight_outs[at][nth] = weight_refs[at][tap] * (1.0 - LEARN_RATE * WEIGHT_DECAY) - step

    @pl.when(pl.program_id(0) == 0)
    def _():
        norm_out, loss_out = scalar_outs
        norm_out[...] = grad_norm
        (small,) = small_refs
        loss_out[...] = small[8 + CLASSES : 9 + CLASSES, CLASSES : CLASSES + 1]
        results = moments(small[0:4, :] * factor, small[24:28, :], small[28:32, :])
        for at in range(2):
            small_outs[at][...] = results[at][0:2, :]
            small_outs[2 + at][...] = results[at][2:4, :]
        results = moments(
            small[8 : 8 + CLASSES, :] * factor, small[32 : 32 + CLASSES, :], small[48 : 48 + CLASSES, :]
        )
        for at in range(2):
            small_outs[4 + at][...] = results[at]
        lanes = slice(0, CLASSES)
        results = moments(small[8 + CLASSES : 9 + CLASSES, lanes] * factor, small[64:65, lanes], small[65:66, lanes])
        for at in range(2):
            small_outs[6 + at][...] = results[at]


def swap(values, axis, step):
    count = lax.axis_size(axis)
    return lax.ppermute(values, axis, [(here, here ^ step) for here in range(count)])


def gathered(values, axis):
    return [values] + [swap(values, axis, step) for step in range(1, lax.axis_size(axis))]


def exchanged(sends, axis):
    return [sends[0]] + [swap(sends[step], axis, step) for step in range(1, len(sends))]


def picked(values, index):
    return lax.dynamic_index_in_dim(values, index, 0, keepdims=False)


def after(values, *others):
    return lax.optimization_barrier((values,) + others)[0]


def tree_sum(slots):
    while len(slots) > 1:
        slots = [slots[at] + slots[at + 1] for at in range(0, len(slots), 2)]
    return slots[0]


def every_device(tiles):
    return lax.all_to_all(tiles, EVERY, 0, 0, tiled=True)


def bits_of(axis):
    return range(lax.axis_size(axis).bit_length() - 1)


def bit_of(axis, bit):
    return (lax.axis_index(axis) >> bit) & 1


def crossed(parts, axis, bit):
    return [parts[0], swap(parts[1], axis, 1 << bit)]


def halved(terms, axis, bit):
    rows, width = terms[0].shape
    own = bit_of(axis, bit)
    if rows // 2 % 16:
        total = joined(terms).reshape(2, rows // 2, width)
        return crossed([picked(total, own), picked(total, 1 - own)], axis, bit)
    half = shape((rows // 2, width), BF)
    parts = call(
        pick_kernel if len(terms) == 1 else split_kernel,
        [half, half],
        [own[None], *terms],
        near=tuple(range(1, 1 + len(terms))),
        near_out=(0, 1),
        room=16,
    )
    return crossed(parts, axis, bit)


def doubled(values, axis, bit):
    own = bit_of(axis, bit)
    rows, width = values.shape
    other = swap(values, axis, 1 << bit)
    (out,) = call(
        merge_kernel, [shape((2 * rows, width), BF)], [own[None], values, other], near=(1, 2), near_out=(0,), room=16
    )
    return out


def joined(terms):
    return terms[0] if len(terms) == 1 else (terms[0].astype(F32) + terms[1].astype(F32)).astype(BF)


def batch_gather(block, axes=("dp", "cin"), first=()):
    for order in reversed(first):
        block = doubled(block, *order)
    for axis in axes:
        for bit in reversed(bits_of(axis)):
            block = doubled(block, axis, bit)
    return block


def batch_rows(values):
    place = jnp.int32(0)
    for axis in ("cin", "dp"):
        for bit in bits_of(axis):
            place = place * 2 + ((lax.axis_index(axis) >> bit) & 1)
    rows = values.shape[0] // (lax.axis_size("dp") * lax.axis_size("cin"))
    return lax.dynamic_slice_in_dim(values, place * rows, rows, 0)


def local(
    images,
    masks,
    labels,
    w_first,
    w_second,
    norm_params,
    head_w,
    head_b,
    bases,
    scales_first,
    scales_second,
    w_first_mean,
    w_first_square,
    w_second_mean,
    w_second_square,
    norm_mean,
    norm_square,
    head_w_mean,
    head_w_square,
    head_b_mean,
    head_b_square,
):
    me = lax.axis_index("cout")
    side = lax.axis_index("cin") % 2
    place = jnp.stack([me, side]).astype(jnp.int32)
    sizes = tuple(lax.axis_size(name) for name in EVERY)
    groups = sizes[1]
    devices = sizes[0] * sizes[1] * sizes[2]
    channels = w_first.shape[1]
    width = w_first.shape[2]
    half = channels // 2
    count = images.shape[1]
    part = count // groups
    rows = PIX * part
    tile = shape((devices, 8, LANES), F32)
    wide = (rows, channels)
    basis_in_first, basis_out_first = bases[0, 0], bases[0, 1]
    basis_in_second, basis_out_second = bases[1, 0], bases[1, 1]
    bases_all = (basis_in_first, basis_out_first, basis_in_second, basis_out_second)

    piece = lax.dynamic_slice_in_dim(w_second, side * half, half, 2).astype(BF)
    own_labels = lax.dynamic_slice_in_dim(labels, me * part, part, 0)[None]
    bias_row = jnp.pad(head_b, (0, LANES - CLASSES))[None]

    flat_images = images.reshape(PIX * count, channels)
    first_out, all_mask, stats, mask = call(
        functools.partial(first_kernel, groups),
        [
            shape((PIX * count, width), F32),
            shape((PIX * count, LANES), BF),
            shape((sizes[0] * sizes[2], 8, LANES), F32),
            shape((rows, LANES), F32),
        ],
        [place, flat_images, masks, w_first],
        [
            pltpu.VMEM((PIX * count, LANES), F32),
            pltpu.VMEM((PIX * count, channels), BF),
            pltpu.VMEM((channels, TAPS * width), BF),
            pltpu.VMEM((TAPS, channels, width), F32),
            pltpu.SemaphoreType.DMA((3,)),
        ],
        near=(1, 2),
        raw=(3,),
        room=56,
        flops=2 * PIX * count * channels * width * TAPS,
    )
    got = lax.all_to_all(stats, ("dp", "cin"), 0, 0, tiled=True)
    (left_turned,) = call(
        left_first_kernel,
        [shape((groups, channels, rows), BF)],
        [place, after(flat_images, stats), masks, basis_in_first],
        [
            pltpu.VMEM((PIX * count, LANES), F32),
            pltpu.VMEM((PIX * count, channels), BF),
            pltpu.VMEM((rows, channels), BF),
        ],
        near=(1, 2, 3),
        room=20,
    )
    near_weights = [piece]
    for step in range(1, groups):
        ready = piece if step < groups - 1 else after(piece, stats)
        near_weights.append(swap(ready, "cout", step))
    first_mask = after(all_mask, left_turned, *near_weights[1:-1], *bases_all)
    *first_sends, kept = call(
        lambda *refs: first_norm_kernel(*refs[:6], refs[6 : 6 + groups], *refs[6 + groups :]),
        [shape((2 * rows + 16, width), BF)] * groups + [shape((8, LANES), F32)],
        [place, got, first_out, first_mask, norm_params, head_w.T],
        [pltpu.VMEM((PIX * count, LANES), BF), pltpu.VMEM((PIX * count, LANES), BF)],
        near_out=tuple(range(groups)),
    )
    def in_slots(values):
        return jnp.concatenate(
            [lax.dynamic_slice_in_dim(values, (me ^ step) * width, width, 1) for step in range(groups)], 1
        )

    def basis_rows(basis):
        return in_slots(lax.dynamic_slice_in_dim(basis, me * width, width, 0))

    scales_turned = batch_rows(
        jnp.swapaxes(after(scales_second, kept), 1, 2).reshape(TAPS * channels, width)
    )
    rows_first = basis_rows(after(basis_out_first, kept))
    rows_second = basis_rows(after(basis_in_second, kept))
    kept = after(kept, scales_turned, rows_first, rows_second)
    first_slots = exchanged(first_sends, "cout")
    (hidden,) = call(
        lambda *refs: hidden_kernel(refs[0], refs[1 : 1 + groups], *refs[1 + groups :]),
        [shape((rows, channels + LANES), BF)],
        [place, *first_slots, after(mask, kept)],
        near=tuple(range(1, 1 + groups)),
        near_out=(0,),
    )
    other_hidden = swap(hidden, "cin", 1)
    mine, theirs, stats = call(
        lambda *refs: second_kernel(*refs[:4], refs[4 : 4 + groups], *refs[4 + groups :]),
        [shape((rows, half), F32), shape((rows, half), F32), tile],
        [place, hidden, other_hidden, norm_params, *near_weights],
        [
            pltpu.VMEM((2 * rows, channels), BF),
            pltpu.VMEM((TAPS, channels, half), BF),
            pltpu.VMEM((2 * rows, half), F32),
            pltpu.SemaphoreType.DMA((groups,)),
        ],
        near=(1, 2),
        raw=tuple(range(4, 4 + groups)),
        flops=4 * rows * channels * half * TAPS,
    )
    scaled_first, norm_first, head_full = call(
        lambda *refs: gather_kernel(refs[0], refs[1 : 1 + groups], *refs[1 + groups :]),
        [shape(wide, BF), shape((8, channels), F32), shape((16, channels), BF)],
        [place, *first_slots, after(kept, mine)],
    )
    from_other = swap(theirs, "cin", 1)
    got_second = every_device(stats)
    far_weights = [swap(after(slot, mine), "cin", 1) for slot in near_weights]
    head_mask = after(mask, *far_weights)
    second_out, norm_second, dz_second, sums, head_blocks = call(
        functools.partial(head_kernel, sizes),
        [
            shape(wide, F32),
            shape((8, channels), F32),
            shape(wide, F32),
            tile,
            shape((groups, 16, width), F32),
        ],
        [place, mine, from_other, got_second, norm_first, head_mask, head_full, bias_row, own_labels],
        [
            pltpu.VMEM(wide, F32),
            pltpu.VMEM((part, channels), F32),
            pltpu.VMEM((LANES, channels), BF),
        ],
    )
    got = every_device(sums)
    scaled_slots = gathered(after(scaled_first, got_second), "cout")
    grad_second, sums_second, sums, *right_sends = call(
        lambda *refs: second_back_kernel(
            *refs[:10], refs[10 : 10 + groups], refs[10 + groups : 10 + 2 * groups],
            *refs[10 + 2 * groups : 13 + 2 * groups], refs[13 + 2 * groups : 13 + 3 * groups], *refs[13 + 3 * groups :]
        ),
        [shape(wide, BF), shape((8, LANES), F32), shape(sizes + (32, LANES), BF)] + [shape((rows, width), BF)] * groups,
        [
            place, dz_second, second_out, norm_second, got, after(mask, *scaled_slots), scaled_first,
            norm_first, head_blocks, basis_out_first, *near_weights, *far_weights,
        ],
        [
            pltpu.VMEM(wide, BF),
            pltpu.VMEM((TAPS, channels, channels), BF),
            pltpu.VMEM(wide, F32),
            pltpu.SemaphoreType.DMA((3, 2 * groups)),
        ],
        raw=tuple(range(10, 10 + 2 * groups)),
        flops=2 * rows * channels * channels * TAPS,
    )
    left_slots = call(
        lambda *refs: left_second_kernel(*refs[:4], refs[4 : 4 + groups], refs[4 + groups : 4 + 2 * groups], *refs[4 + 2 * groups :]),
        [shape((rows, width), BF)] * groups,
        [place, norm_first, after(all_mask, sums_second), basis_in_second, *scaled_slots],
        [pltpu.VMEM((channels, width), BF), pltpu.VMEM(wide, BF)],
    )
    (right_turned,) = call(
        right_kernel, [shape((channels, rows), BF)], [grad_second, basis_out_second], scalars=0
    )

    def products(sign, big, small, near=()):
        (out,) = call(
            lambda *refs: taps_kernel(sign, refs[:groups], refs[groups : 2 * groups], *refs[2 * groups :]),
            [shape((TAPS * channels, width), BF)],
            [*big, *small],
            [
                pltpu.VMEM((channels, groups * rows), BF),
                pltpu.VMEM((groups * rows, TAPS * width), BF),
            ],
            scalars=0,
            near=near,
            near_out=(0,),
            room=44,
            flops=2 * groups * rows * channels * width * TAPS,
        )
        return out

    right_parts = exchanged(right_sends, "cout")
    got = every_device(sums.reshape(devices, 32, LANES))
    right_slots = gathered(after(right_turned, got), "cout")
    orders = [(axis, bit) for axis in ("cin", "dp") for bit in bits_of(axis)]
    small_old = [norm_mean, norm_square, head_w_mean.T, head_w_square.T, head_b_mean[None], head_b_square[None]]
    def hold(*values):
        def copy_in(*refs):
            arrived = refs[-1]
            copies = [
                pltpu.make_async_copy(refs[at], refs[len(values) + at], arrived.at[at])
                for at in range(len(values))
            ]
            for copy in copies:
                copy.start()
            for copy in copies:
                copy.wait()

        return call(
            lambda *refs: copy_in(*refs),
            [shape(value.shape, value.dtype) for value in values],
            values,
            [pltpu.SemaphoreType.DMA((len(values),))],
            scalars=0,
            raw=tuple(range(len(values))),
            near_out=tuple(range(len(values))),
            room=16,
        )

    def ratio_of(terms, scales_own):
        chunk = shape(scales_own.shape, BF)
        return call(
            lambda *refs: ratio_kernel(refs[: len(terms)], *refs[len(terms) :]),
            [chunk, chunk],
            [*terms, scales_own],
            scalars=0,
            near=tuple(range(len(terms) + 1)),
            near_out=(0, 1),
            room=16,
        )

    def middle_of(slots, basis):
        (out,) = call(
            lambda basis_ref, *refs: middle_kernel(basis_ref, refs[:groups], refs[-1]),
            [shape(slots[0].shape, BF)],
            [basis, *slots],
            scalars=0,
            near=tuple(range(groups + 1)),
            near_out=(0,),
            room=16,
        )
        return out

    near_steps = len(bits_of("cin"))
    left_parts = [left_turned[step] for step in range(groups)]
    *products_first, sums_first, smalls = call(
        lambda *refs: first_products_kernel(
            *refs[:5], refs[5:11], *[refs[11 + at * groups : 11 + (at + 1) * groups] for at in (2, 0, 1)],
            *refs[11 + 3 * groups :]
        ),
        [shape((TAPS * channels // 2, width), BF)] * 2 + [shape((8, LANES), F32), shape((72, LANES), F32)],
        [
            place, after(got, right_turned, *left_slots), norm_first, all_mask, basis_out_first, *small_old, *right_parts, *scaled_slots, *left_parts,
        ],
        [
            pltpu.VMEM((channels, groups * rows), BF),
            pltpu.VMEM((groups * rows, TAPS * width), BF),
            pltpu.VMEM((groups, rows, width), BF),
            pltpu.VMEM((channels, width), BF),
            pltpu.VMEM((rows, LANES), BF),
            pltpu.VMEM((TAPS * channels, width), BF),
        ],
        near_out=(0, 1),
        room=56,
        flops=2 * groups * rows * channels * width * TAPS,
    )
    terms_first = crossed(products_first, *orders[0])
    for order in orders[1:]:
        terms_first = halved(terms_first, *order)
    own_first = joined([after(terms_first[0], *right_slots), terms_first[1]])
    coeff_first = doubled(own_first, *orders[-1])
    terms_second = [products(1, [after(right_slots[0], own_first)] + right_slots[1:], left_slots)]
    for order in orders:
        terms_second = halved(terms_second, *order)
    for order in reversed(orders[near_steps:-1]):
        coeff_first = doubled(coeff_first, *order)
    coeff_first = batch_gather(coeff_first, ("cin",))
    flat_scales = scales_first.reshape(TAPS * channels, width)
    scales_first_new, ratio_first = call(
        wide_ratio_kernel,
        [shape(flat_scales.shape, F32), shape((TAPS * channels // 2, width), BF)],
        [place, coeff_first, flat_scales],
        near=(1, 2),
        near_out=(1,),
        room=16,
    )
    slots_first = gathered(ratio_first, "cout")
    own_second, ratio_second = ratio_of(terms_second, after(scales_turned, ratio_first))
    weights = hold(after(w_first, own_second), w_second)
    coeff_second = doubled(own_second, *orders[-1])
    middle_second = middle_of(gathered(ratio_second, "cout"), after(rows_second, coeff_second, ratio_first))
    means = hold(after(w_first_mean, weights[0]), w_second_mean)
    middle_first = middle_of(slots_first, after(rows_first, *means))
    gathered_first = doubled(middle_first, "cin", 0)
    squares_old = hold(after(w_first_square, middle_second), w_second_square)
    gathered_second = doubled(middle_second, *orders[-1])
    for order in reversed(orders[near_steps:-1]):
        coeff_second = doubled(coeff_second, *order)
        gathered_second = doubled(after(gathered_second, *squares_old), *order)
    gathered_second = batch_gather(gathered_second, ("cin",))
    coeff_second = batch_gather(coeff_second, ("cin",))

    def scales_of(turned, coeff, scales):
        spec = pl.BlockSpec((3,) + scales.shape[1:], lambda tap: (tap, 0, 0))
        return pl.pallas_call(
            functools.partial(scales_kernel, turned),
            grid=(TAPS // 3,),
            in_specs=[pl.BlockSpec((3 * channels, width), lambda tap: (tap, 0)), spec],
            out_specs=spec,
            out_shape=shape(scales.shape, F32),
            compiler_params=pltpu.CompilerParams(vmem_limit_bytes=12 * 1024 * 1024),
        )(coeff, scales)

    scales_second_new = scales_of(True, coeff_second, scales_second)

    first_grad, second_grad, squares, small_grads = call(
        restore_kernel,
        [shape((TAPS, channels, width), BF), shape((TAPS, width, channels), BF), shape((8, LANES), F32), shape((72, LANES), F32)],
        [
            place,
            basis_in_first,
            gathered_first,
            basis_out_second,
            gathered_second,
            sums_first,
            sums_second,
            smalls,
        ],
        [pltpu.VMEM((channels, TAPS * width), BF)],
        near=tuple(range(1, 8)),
        near_out=(0, 1, 2, 3),
        room=16,
        flops=4 * TAPS * channels * channels * width,
    )
    square_slots = gathered(squares, "cout")
    square_slots[0] = after(square_slots[0], coeff_second)

    smalls = [small_grads]
    small_outs = [shape((2, width), F32)] * 4 + [shape((CLASSES, width), F32)] * 2 + [shape((1, CLASSES), F32)] * 2
    small_outs += [shape((1, 1), F32)] * 2
    first_spec = pl.BlockSpec((3, channels, width), lambda tap: (tap, 0, 0))
    second_spec = pl.BlockSpec((3, width, channels), lambda tap: (tap, 0, 0))
    pair = [first_spec, second_spec]
    first_like, second_like = shape(w_first.shape, F32), shape(w_second.shape, F32)

    def whole(leaf):
        return pl.BlockSpec(leaf.shape, lambda tap: (0,) * len(leaf.shape))

    def update(*refs):
        at = [0]

        def take(number):
            at[0] += number
            return refs[at[0] - number : at[0]]

        update_kernel(
            take(groups), take(2), take(2), take(2), take(2), take(len(smalls)),
            take(2), take(2), take(2), take(len(small_outs) - 2), take(2), take(1)[0],
        )

    results = pl.pallas_call(
        update,
        grid=(TAPS // 3,),
        scratch_shapes=[pltpu.VMEM((8, LANES), F32)],
        in_specs=[pl.BlockSpec(memory_space=pltpu.VMEM)] * (groups + 8 + len(smalls)),
        out_specs=pair * 3 + [whole(leaf) for leaf in small_outs],
        out_shape=[first_like, second_like] * 3 + small_outs,
        compiler_params=pltpu.CompilerParams(vmem_limit_bytes=16 * 1024 * 1024),
    )(
        *square_slots, *weights, *means, *squares_old,
        first_grad, second_grad, *smalls,
    )
    (first_new, second_new, first_mean_new, second_mean_new, first_square_new, second_square_new,
     norm_first_mean, norm_first_square, norm_second_mean, norm_second_square,
     head_mean_new, head_square_new, bias_mean_new, bias_square_new, grad_norm, loss_total) = results
    return (
        loss_total.reshape(()),
        grad_norm.reshape(()),
        first_new,
        first_mean_new,
        first_square_new,
        second_new,
        second_mean_new,
        second_square_new,
        norm_first_mean,
        norm_first_square,
        norm_second_mean,
        norm_second_square,
        head_mean_new.T,
        head_square_new.T,
        bias_mean_new[0],
        bias_square_new[0],
        scales_first_new.reshape(scales_first.shape),
        scales_second_new,
    )


def solution(mesh):
    return jax.shard_map(
        local,
        mesh=mesh,
        in_specs=(
            P(None, ("dp", "cin"), None),
            P(None, ("dp", "cin")),
            P(("dp", "cin")),
            P(None, None, "cout"),
            P(None, "cout", None),
            P(None, "cout"),
            P("cout", None),
            P(),
            P(),
            P(None, None, "cout"),
            P(None, "cout", None),
            P(None, None, "cout"),
            P(None, None, "cout"),
            P(None, "cout", None),
            P(None, "cout", None),
            P(None, "cout"),
            P(None, "cout"),
            P("cout", None),
            P("cout", None),
            P(),
            P(),
        ),
        out_specs=(
            P(),
            P(),
            P(None, None, "cout"),
            P(None, None, "cout"),
            P(None, None, "cout"),
            P(None, "cout", None),
            P(None, "cout", None),
            P(None, "cout", None),
            P(None, "cout"),
            P(None, "cout"),
            P(None, "cout"),
            P(None, "cout"),
            P("cout", None),
            P("cout", None),
            P(),
            P(),
            P(None, None, "cout"),
            P(None, "cout", None),
        ),
        check_vma=False,
    )
```
